128 devices in a mesh: gx: 16 (over y, z_lo, core), gy: 8 (over x, z_hi).
Axes of the slice: x: 4, y: 4, z: 4 (z_hi: 2, z_lo: 2; z = z_hi * 2 + z_lo), core: 2. Of those that a mesh axis runs over, the one named last changes fastest.
Arguments:
- populations: float32 [19, 128, 32768], P(None, 'gx', 'gy'), may hold values from 0.016 to 0.467, as said below
- h_axial: float32 [128, 32768], P('gx', 'gy'), may hold values from 1 to 3
- h_transverse: float32 [2, 128, 32768], P(None, 'gx', 'gy'), may hold values from -4 to 4
Outputs:
- populations_next: float32 [19, 128, 32768], P(None, 'gx', 'gy')
- demag_field: float32 [3, 128, 32768], P(None, 'gx', 'gy')
The draws below stay inside these ranges and needn't reach their ends.
Inputs may be any that keep to these rules, and one draw needn't show every extreme that they name: `populations`: each population lies between 0.6 and 1.4 times its lattice weight.
All inputs are finite; a program needn't handle non-finite values.
Results may differ from the reference program's by a relative error of at most 0.000078.
Values sent between devices are 32-bit elements; how exact they have to be, the bound alone decides.
No kernel may reach another device: no remote copies, remote signals or barrier semaphores. Data moves between devices by JAX's collectives and lax.ppermute only.
A program may use at most 128 MiB of HBM per device.

```python
import jax
import jax.numpy as jnp
from jax import lax

NZ = 64
Q = 19
NX = 128
NY = 512


LATTICE_WEIGHTS = (1.0 / 3.0,) + (1.0 / 18.0,) * 6 + (1.0 / 36.0,) * 12


def draw_populations(key, part):
    key = jax.random.fold_in(key, 11)
    weights = jnp.array(LATTICE_WEIGHTS, dtype=jnp.float32).reshape(19, 1, 1)
    factor = jax.random.uniform(key, (Q, NX, NY * NZ), jnp.float32, 0.7, 1.3)
    return weights * factor


def draw_h_transverse(key, part):
    key = jax.random.fold_in(key, 23)
    return 0.8 * jnp.clip(jax.random.normal(key, (2, NX, NY * NZ), jnp.float32), -5.0, 5.0)


def shard_levels(key, dims, split, smallest, high):
    factor_of, own = 1.0, jax.random.fold_in(key, 6)
    for position, blocks in split:
        draws = jnp.exp(jax.random.uniform(jax.random.fold_in(own, position), (blocks,), jnp.float32, smallest / len(split), high / len(split)))
        factor_of = factor_of * jnp.repeat(draws, dims[position] // blocks).reshape([-1 if axis == position else 1 for axis in range(len(dims))])
    return factor_of


def setup_inputs(seed: int = 0) -> dict:
    seeds = jax.random.split(jax.random.key(seed), 4)
    return {
        "populations": draw_populations(jax.random.fold_in(seeds[3], 71), 0),
        "h_axial": jnp.clip(1.0 + 2.0 * jax.random.uniform(seeds[1], (NX, NY * NZ), jnp.float32) ** shard_levels(seeds[1], (NX, NY * NZ), ((0, 16), (1, 8)), -0.2, 0.2), 1.0, 3.0),
        "h_transverse": draw_h_transverse(jax.random.fold_in(seeds[3], 71), 0),
    }


VELOCITIES = ((0, 0, 0), (1, 0, 0), (-1, 0, 0), (0, 1, 0), (0, -1, 0), (0, 0, 1), (0, 0, -1), (1, 1, 0), (-1, -1, 0), (1, -1, 0), (-1, 1, 0), (1, 0, 1), (-1, 0, -1), (1, 0, -1), (-1, 0, 1), (0, 1, 1), (0, -1, -1), (0, 1, -1), (0, -1, 1))
WEIGHTS = (1.0 / 3.0,) + (1.0 / 18.0,) * 6 + (1.0 / 36.0,) * 12
LANGEVIN_SCALE = 1.5
SATURATION = 1.0
KELVIN_COEF = 0.05
RELAX_TIME = 0.6

def langevin(applied):
    magnitude = jnp.sqrt(lax.optimization_barrier(jnp.sum(applied * applied, axis=0)))
    argument = LANGEVIN_SCALE * magnitude
    return SATURATION * (1.0 / jnp.tanh(argument) - 1.0 / argument) * applied / magnitude

def wavenumber(indices, count, dtype):
    return 2.0 * jnp.sin(jnp.pi * indices.astype(dtype) / count)

def demag_kernel(comp_x, comp_y, comp_z, wave_x, wave_y, wave_z, anchor):
    squared = wave_x * wave_x + wave_y * wave_y + wave_z * wave_z
    factor = jnp.where(anchor, 0.0, -1.0 / jnp.where(anchor, 1.0, squared))
    along = (wave_x * comp_x + wave_y * comp_y + wave_z * comp_z) * factor
    return (wave_x * along, wave_y * along, wave_z * along)

def kelvin(magnet, wide):
    centre = wide[:, 1:-1, 1:-1]
    grad_x = 0.5 * (wide[:, 2:, 1:-1] - wide[:, :-2, 1:-1])
    grad_y = 0.5 * (wide[:, 1:-1, 2:] - wide[:, 1:-1, :-2])
    grad_z = 0.5 * (jnp.roll(centre, -1, axis=3) - jnp.roll(centre, 1, axis=3))
    return KELVIN_COEF * (magnet[0:1] * grad_x + magnet[1:2] * grad_y + magnet[2:3] * grad_z)

def moments(popul, body_force):
    density = lax.optimization_barrier(jnp.sum(popul, axis=0))
    momentum = [0.5 * body_force[0], 0.5 * body_force[1], 0.5 * body_force[2]]
    for number in range(19):
        for column in range(3):
            if VELOCITIES[number][column] == 1:
                momentum[column] = momentum[column] + popul[number]
            elif VELOCITIES[number][column] == -1:
                momentum[column] = momentum[column] - popul[number]
    return (density, (momentum[0] / density, momentum[1] / density, momentum[2] / density))

def relax(popul_one, density, velocity, body_force, lattice, weight):
    vel_x, vel_y, vel_z = velocity
    along_u = lattice[0] * vel_x + lattice[1] * vel_y + lattice[2] * vel_z
    along_f = lattice[0] * body_force[0] + lattice[1] * body_force[1] + lattice[2] * body_force[2]
    u_dot_f = vel_x * body_force[0] + vel_y * body_force[1] + vel_z * body_force[2]
    u_square = vel_x * vel_x + vel_y * vel_y + vel_z * vel_z
    equilib = weight * density * (1.0 + 3.0 * along_u + 4.5 * along_u * along_u - 1.5 * u_square)
    source = (1.0 - 0.5 / RELAX_TIME) * weight * (3.0 * (along_f - u_dot_f) + 9.0 * along_u * along_f)
    return popul_one - (popul_one - equilib) / RELAX_TIME + source

def reference(populations, h_axial, h_transverse):
    dtype = populations.dtype
    grid = (NX, NY, NZ)
    applied = jnp.concatenate([h_transverse, h_axial[None]], axis=0).reshape((3,) + grid)
    magnet = langevin(applied)
    spectrum = jnp.fft.fftn(magnet, axes=(1, 2, 3))
    index_x = jnp.arange(NX, dtype=jnp.int32)
    index_y = jnp.arange(NY, dtype=jnp.int32)
    index_z = jnp.arange(NZ, dtype=jnp.int32)
    wave_x = wavenumber(index_x, NX, dtype)[:, None, None]
    wave_y = wavenumber(index_y, NY, dtype)[None, :, None]
    wave_z = wavenumber(index_z, NZ, dtype)[None, None, :]
    anchor = (index_x == 0)[:, None, None] & (index_y == 0)[None, :, None] & (index_z == 0)[None, None, :]
    comps = demag_kernel(spectrum[0], spectrum[1], spectrum[2], wave_x, wave_y, wave_z, anchor)
    demag = jnp.real(jnp.fft.ifftn(jnp.stack(comps), axes=(1, 2, 3))).astype(dtype)
    total_field = applied + demag
    wide = jnp.pad(total_field, ((0, 0), (1, 1), (1, 1), (0, 0)), mode='wrap')
    body_force = kelvin(magnet, wide)
    popul = populations.reshape((Q,) + grid)
    density, velocity = moments(popul, body_force)
    table_vel = jnp.array(VELOCITIES, dtype=jnp.int32)
    table_weight = jnp.array(WEIGHTS, dtype=dtype)

    def advance(inputs):
        popul_one, lattice_int, weight = inputs
        lattice = lattice_int.astype(dtype)
        post = relax(popul_one, density, velocity, body_force, lattice, weight)
        moved = jnp.roll(post, lattice_int[0], axis=0)
        moved = jnp.roll(moved, lattice_int[1], axis=1)
        return jnp.roll(moved, lattice_int[2], axis=2)
    result = lax.map(advance, (popul, table_vel, table_weight))
    return (result.reshape(Q, NX, NY * NZ), demag.reshape(3, NX, NY * NZ))
```

```python
import functools

import jax
import jax.numpy as jnp
import numpy as np
from jax import lax
from jax.experimental import pallas as pl
from jax.experimental.pallas import tpu as pltpu
from jax.sharding import PartitionSpec as P

NX, NY, NZ = 128, 512, 64
GX, GY = 16, 8
VELOCITIES = (
    (0, 0, 0),
    (1, 0, 0),
    (-1, 0, 0),
    (0, 1, 0),
    (0, -1, 0),
    (0, 0, 1),
    (0, 0, -1),
    (1, 1, 0),
    (-1, -1, 0),
    (1, -1, 0),
    (-1, 1, 0),
    (1, 0, 1),
    (-1, 0, -1),
    (1, 0, -1),
    (-1, 0, 1),
    (0, 1, 1),
    (0, -1, -1),
    (0, 1, -1),
    (0, -1, 1),
)
WEIGHTS = (1.0 / 3.0,) + (1.0 / 18.0,) * 6 + (1.0 / 36.0,) * 12
OMEGA = 1.0 / 0.6
HIGHEST = lax.Precision.HIGHEST
F32 = jnp.float32
VMEM_BYTES = 48 * 1024 * 1024

X_FACE = ((0, 0, 1, 2), (1, 0, 7, 10), (-1, 0, 9, 8), (0, 1, 11, 14), (0, -1, 13, 12))
Y_FACE = ((0, 0, 3, 4), (1, 0, 7, 9), (-1, 0, 10, 8), (0, 1, 15, 18), (0, -1, 17, 16))
X_SLOT = {n: s for s, row in enumerate(X_FACE) for n in row[2:]}

ROWS_FWD = 12
ROWS_BACK = 20
PITCH = 80


def cas(rows, cols, count):
    angle = 2.0 * np.pi * ((rows[:, None] * cols[None, :]) % count) / count
    return np.cos(angle) + np.sin(angle)


def wave(index, count):
    return 2.0 * np.sin(np.pi * index / count)


@functools.lru_cache(maxsize=None)
def tables():
    every_x, every_z = np.arange(NX), np.arange(NZ)
    half = np.arange(NY // 2)
    out = {}
    fwd_z = np.zeros((NZ, 128))
    fwd_z[:, :NZ] = cas(every_z, every_z, NZ)
    out["fwd_z"] = fwd_z
    out["back_z"] = np.tile(cas(every_z, every_z, NZ), (1, 2))
    fwd_x, back_x = [], []
    m = np.arange(8)
    for parity in range(2):
        order = []
        for side in (parity, 1 - parity):
            for x2 in range(2):
                for x4 in range(4):
                    order += list(8 * (2 * m + side) + 2 * x4 + x2)
        fwd_x.append(cas(every_x, np.array(order), NX))
        order = []
        for x2 in range(2):
            for x6 in range(6):
                order += list((8 * (2 * m + parity) - 2 + 2 * x6 + x2) % NX)
        back_x.append(cas(np.array(order), every_x, NX))
    out["fwd_x"] = np.stack(fwd_x)
    out["back_x"] = np.stack(back_x)
    even, odd = 2 * half, 2 * half + 1
    halo = np.array(
        [
            (64 * g + (-2, -1, 64, 65)[k]) % NY
            for g in range(GY)
            for c in range(4)
            for k in range(4)
        ]
    )
    out["even"] = cas(half, even, NY)
    out["odd"] = cas(half, odd, NY)
    out["back_even"] = np.concatenate([cas(even, half, NY), cas(even, halo, NY)], axis=1)
    out["back_odd"] = np.concatenate([cas(odd, half, NY), cas(odd, halo, NY)], axis=1)
    out["wave_x"] = np.repeat(wave(every_x, NX)[:, None], 128, axis=1)
    out["wave_y"] = np.stack([wave(even, NY), wave(odd, NY)])
    out["wave_z"] = np.repeat(wave(every_z, NZ)[:, None], 128, axis=1)
    return {name: np.asarray(value, np.float32) for name, value in out.items()}


def dot(a, b, dims=(1, 0)):
    return lax.dot_general(
        a, b, (((dims[0],), (dims[1],)), ((), ())), precision=HIGHEST, preferred_element_type=F32
    )


def langevin(hx, hy, hz):
    magnitude = jnp.sqrt(hx * hx + hy * hy + hz * hz)
    argument = 1.5 * magnitude
    decay = jnp.exp(-2.0 * argument)
    scale = ((1.0 + decay) / (1.0 - decay) - 1.0 / argument) / magnitude
    return hx * scale, hy * scale, hz * scale


def lanes(shape=(8, 128)):
    return lax.broadcasted_iota(jnp.int32, shape, len(shape) - 1)


def first_kernel(ht_ref, ha_ref, table_ref, magnet_ref, send_ref, rows_ref):
    magnet = langevin(ht_ref[0], ht_ref[1], ha_ref[...])
    for c in range(3):
        magnet_ref[c] = magnet[c]
        for pair in range(32):
            tile = magnet[c][:, pair * 128 : pair * 128 + 128]
            rows_ref[pl.ds(c * 512 + 2 * pair, 8, stride=64), :] = tile
            rows_ref[pl.ds(c * 512 + 2 * pair + 1, 8, stride=64), :] = pltpu.roll(tile, 64, 1)
    spectrum = dot(table_ref[...], rows_ref[...], (1, 1))
    for row in range(ROWS_FWD):
        send_ref[pl.ds(row, NZ, stride=ROWS_FWD), :] = spectrum[:, row * 128 : row * 128 + 128]


def transpose_blocks(tiles):
    block = lanes() // 16
    for bit in (1, 2, 4):
        low = (block & bit) == 0
        out = list(tiles)
        for i in range(8):
            if i & bit == 0:
                a, b = tiles[i], tiles[i | bit]
                out[i] = jnp.where(low, a, pltpu.roll(b, 16 * bit, 1))
                out[i | bit] = jnp.where(low, pltpu.roll(a, 128 - 16 * bit, 1), b)
        tiles = out
    return tiles


def plane_kernel(
    own_ref,
    other_ref,
    fwd_x_ref,
    back_x_ref,
    even_ref,
    odd_ref,
    back_even_ref,
    back_odd_ref,
    wave_x_ref,
    wave_y_ref,
    wave_z_ref,
    send_ref,
    cells_ref,
):
    row = lax.axis_index("gx")
    parity = lax.rem(row, 2)
    index_z = (row // 2) * GY + lax.axis_index("gy")
    left = lanes() < 64
    for side, ref in enumerate((own_ref, other_ref)):
        for c in range(3):
            for pair in range(4):
                for x4 in range(4):
                    start = 2 * pair * ROWS_FWD + c * 4 + x4
                    a = ref[pl.ds(start, 8, stride=GY * ROWS_FWD), :]
                    b = ref[pl.ds(start + ROWS_FWD, 8, stride=GY * ROWS_FWD), :]
                    at = side * 64 + x4 * 8
                    col = c * 512 + pair * 128
                    cells_ref[at : at + 8, col : col + 128] = jnp.where(
                        left, a, pltpu.roll(b, 64, 1)
                    )
                    cells_ref[at + 32 : at + 40, col : col + 128] = jnp.where(
                        left, pltpu.roll(a, 64, 1), b
                    )
    wave_x = wave_x_ref[:, 0:1]
    wave_z = wave_z_ref[pl.ds(index_z, 1), 0:1]
    spectrum = dot(fwd_x_ref[parity], cells_ref[...])
    along = wave_x * spectrum[:, :512] + wave_z * spectrum[:, 1024:]
    both = jnp.concatenate([along, spectrum[:, 512:1024]], axis=0)
    parts = (
        dot(both[:, :256] + both[:, 256:], even_ref[...]),
        dot(both[:, :256] - both[:, 256:], odd_ref[...]),
    )
    back = []
    for which in range(2):
        wave_y = wave_y_ref[which : which + 1, :]
        squared = wave_x * wave_x + wave_y * wave_y + wave_z * wave_z
        anchor = squared == 0.0
        factor = jnp.where(
            anchor, 0.0, (-1.0 / (NX * NY * NZ)) / jnp.where(anchor, 1.0, squared)
        )
        potential = (parts[which][:128] + wave_y * parts[which][128:]) * factor
        stacked = jnp.concatenate([potential, wave_y * potential], axis=0)
        back.append(dot(stacked, (back_even_ref, back_odd_ref)[which][...]))
    low, high = back[0] + back[1], back[0] - back[1]
    column = lanes((128, 128)) % 16
    halo_p, halo_q = low[:128, 256:], low[128:, 256:]
    halo = jnp.where(
        column < 4,
        wave_x * halo_p,
        jnp.where(column < 8, halo_q, jnp.where(column < 12, wave_z * halo_p, 0.0)),
    )
    potential = jnp.concatenate([low[:128, :256], high[:128, :256]], axis=1)
    fields = jnp.concatenate(
        [wave_x * potential, low[128:, :256], high[128:, :256], wave_z * potential, halo], axis=1
    )
    cells = dot(back_x_ref[parity], fields)
    step = GY * ROWS_BACK
    for x6 in range(6):
        for c in range(3):
            for pair in range(4):
                col = c * 512 + pair * 128
                a = cells[x6 * 8 : x6 * 8 + 8, col : col + 128]
                b = cells[48 + x6 * 8 : 56 + x6 * 8, col : col + 128]
                at = 2 * pair * ROWS_BACK + c * 6 + x6
                send_ref[pl.ds(at, 8, stride=step), :] = jnp.where(left, a, pltpu.roll(b, 64, 1))
                send_ref[pl.ds(at + ROWS_BACK, 8, stride=step), :] = jnp.where(
                    left, pltpu.roll(a, 64, 1), b
                )
    for part in range(2):
        tiles = []
        for x in range(part * 8, part * 8 + 8):
            if x < 12:
                at = (x % 2) * 48 + (x // 2) * 8
                tiles.append(cells[at : at + 8, 1536:])
            else:
                tiles.append(jnp.zeros((8, 128), F32))
        for g, tile in enumerate(transpose_blocks(tiles)):
            send_ref[pl.ds(g * ROWS_BACK + 18 + part, 8, stride=step), :] = tile


def macroscopic(density, momentum, force):
    inverse = 1.0 / density
    vel = [(momentum[k] + 0.5 * force[k]) * inverse for k in range(3)]
    u_square = vel[0] * vel[0] + vel[1] * vel[1] + vel[2] * vel[2]
    u_dot_f = vel[0] * force[0] + vel[1] * force[1] + vel[2] * force[2]
    scaled = OMEGA * density
    base = scaled * (1.0 - 1.5 * u_square) - 0.5 * u_dot_f
    return vel, scaled, base


def along(lattice, vector):
    total = None
    for sign, value in zip(lattice, vector):
        if isinstance(sign, int):
            if sign == 0:
                continue
            term = value if sign == 1 else -value
        else:
            term = sign * value
        total = term if total is None else total + term
    return total


def relax_terms(lattice, vel, force, scaled, base):
    along_u = along(lattice, vel)
    along_f = along(lattice, force)
    even = base + along_u * (4.5 * scaled * along_u + 1.5 * along_f)
    odd = 3.0 * scaled * along_u + 0.5 * along_f
    return even, odd


def shift_z(tile, step, lane):
    if step == 0:
        return tile
    if step == 1:
        return jnp.where(lane % 64 == 0, pltpu.roll(tile, 65, 1), pltpu.roll(tile, 1, 1))
    return jnp.where(lane % 64 == 63, pltpu.roll(tile, 63, 1), pltpu.roll(tile, 127, 1))


def cell_kernel(
    recv_ref,
    table_ref,
    applied_ref,
    magnet_ref,
    pop_ref,
    x_ref,
    y_ref,
    out_ref,
    demag_ref,
    field_ref,
    total_ref,
    post_ref,
    low_ref,
    high_ref,
):
    lane = lanes()
    left = lane < 64
    for row in range(ROWS_BACK):
        spectrum = recv_ref[pl.ds(row, NZ, stride=ROWS_BACK), :]
        field_ref[row * 128 : row * 128 + 128, :] = dot(spectrum, table_ref[...], (0, 0))
    for c in range(3):
        for x in range(12):
            at = (c * 12 + x) * PITCH
            src = (c * 12 + x) * 64
            total_ref[at + 8 : at + 72, :] = (
                field_ref[src : src + 64, :] + applied_ref[at + 8 : at + 72, :]
            )
            src = 2304 + x * 16 + c * 4
            total_ref[at + 6 : at + 8, :] = (
                field_ref[src : src + 2, :] + applied_ref[at + 6 : at + 8, :]
            )
            total_ref[at + 72 : at + 74, :] = (
                field_ref[src + 2 : src + 4, :] + applied_ref[at + 72 : at + 74, :]
            )

    def cells(c, x, y):
        return total_ref[pl.ds((c * 12 + 2 + x) * PITCH + 8 + y, 8, stride=PITCH), :]

    def force_at(magnet, ya, yb):
        force = []
        for c in range(3):
            d_x = jnp.where(left, cells(c, 1, ya), cells(c, 1, yb)) - jnp.where(
                left, cells(c, -1, ya), cells(c, -1, yb)
            )
            d_y = jnp.where(left, cells(c, 0, ya + 1), cells(c, 0, yb + 1)) - jnp.where(
                left, cells(c, 0, ya - 1), cells(c, 0, yb - 1)
            )
            a, b = cells(c, 0, ya), cells(c, 0, yb)
            d_z = jnp.where(left, pltpu.roll(a, 127, 1), pltpu.roll(b, 127, 1)) - jnp.where(
                left, pltpu.roll(a, 1, 1), pltpu.roll(b, 1, 1)
            )
            force.append(0.025 * (magnet[0] * d_x + magnet[1] * d_y + magnet[2] * d_z))
        return force

    applied = []
    for c in range(3):
        at = (c * 12 + 2) * PITCH + 8
        applied.append(
            jnp.where(
                left,
                applied_ref[pl.ds(at + 64, 8, stride=PITCH), :],
                applied_ref[pl.ds(at - 1, 8, stride=PITCH), :],
            )
        )
    sign = jnp.where(left, -1.0, 1.0)
    force = force_at(langevin(*applied), 64, -1)
    vel, scaled, base = macroscopic(y_ref[5], [y_ref[6], y_ref[7], y_ref[8]], force)
    for slot, (cx, cz, up, down) in enumerate(Y_FACE):
        even, odd = relax_terms((cx, sign, cz), vel, force, scaled, base)
        post = shift_z((1.0 - OMEGA) * y_ref[slot] + WEIGHTS[up] * (even + odd), cz, lane)
        post_ref[up, 0] = post
        post_ref[down, 33] = post

    for part in range(10):
        rows = 8 * part

        def edge(ref, c, xa, xb, shift=0):
            a = (c * 12 + 2 + xa) * PITCH + rows + shift
            b = (c * 12 + 2 + xb) * PITCH + rows + shift
            return ref[a : a + 8, :], ref[b : b + 8, :]

        magnet = langevin(*[jnp.where(left, *edge(applied_ref, c, -1, 8)) for c in range(3)])
        force = []
        for c in range(3):
            d_x = jnp.where(left, *edge(total_ref, c, 0, 9)) - jnp.where(
                left, *edge(total_ref, c, -2, 7)
            )
            d_y = jnp.where(left, *edge(total_ref, c, -1, 8, 1)) - jnp.where(
                left, *edge(total_ref, c, -1, 8, -1)
            )
            a, b = edge(total_ref, c, -1, 8)
            d_z = jnp.where(left, pltpu.roll(a, 127, 1), pltpu.roll(b, 127, 1)) - jnp.where(
                left, pltpu.roll(a, 1, 1), pltpu.roll(b, 1, 1)
            )
            force.append(0.025 * (magnet[0] * d_x + magnet[1] * d_y + magnet[2] * d_z))
        values = [x_ref[k, rows : rows + 8, :] for k in range(9)]
        vel, scaled, base = macroscopic(values[5], values[6:], force)
        for slot, (cy, cz, up, down) in enumerate(X_FACE):
            even, odd = relax_terms((-sign, cy, cz), vel, force, scaled, base)
            post = shift_z((1.0 - OMEGA) * values[slot] + WEIGHTS[up] * (even + odd), cz, lane)
            turned = pltpu.roll(post, 64, 1)
            low_ref[slot, rows : rows + 8, :] = jnp.where(left, post, turned)
            high_ref[slot, rows : rows + 8, :] = jnp.where(left, turned, post)

    def collide(pair, carry):
        ya = 2 * pair
        here = pl.ds(pl.multiple_of(pair * 128, 128), 128)
        for c in range(3):
            at = (c * 12 + 2) * 64 + ya
            demag_ref[c, :, here] = jnp.where(
                left,
                field_ref[pl.ds(at, 8, stride=64), :],
                field_ref[pl.ds(at + 1, 8, stride=64), :],
            )
        force = force_at([magnet_ref[c, :, here] for c in range(3)], ya, ya + 1)
        popul = [pop_ref[n, :, here] for n in range(19)]
        density = popul[0]
        for n in range(1, 19):
            density = density + popul[n]
        momentum = []
        for k in range(3):
            total = None
            for n in range(1, 19):
                if VELOCITIES[n][k] == 1:
                    total = popul[n] if total is None else total + popul[n]
                elif VELOCITIES[n][k] == -1:
                    total = total - popul[n]
            momentum.append(total)
        vel, scaled, base = macroscopic(density, momentum, force)
        post_ref[0, 1 + pair] = (1.0 - OMEGA) * popul[0] + WEIGHTS[0] * base
        for n in range(1, 19, 2):
            even, odd = relax_terms(VELOCITIES[n], vel, force, scaled, base)
            for number, value in ((n, even + odd), (n + 1, even - odd)):
                post = (1.0 - OMEGA) * popul[number] + WEIGHTS[n] * value
                post_ref[number, 1 + pair] = shift_z(post, VELOCITIES[number][2], lane)
        return carry

    lax.fori_loop(0, 32, collide, 0)
    row = lax.broadcasted_iota(jnp.int32, (8, 128), 0)

    def stream(pair, carry):
        here = pl.ds(pl.multiple_of(pair * 128, 128), 128)
        for n in range(19):
            cx, cy, _ = VELOCITIES[n]
            tile = post_ref[n, 1 + pair]
            if cy == 1:
                tile = pltpu.roll(jnp.where(left, tile, post_ref[n, pair]), 64, 1)
            elif cy == -1:
                tile = pltpu.roll(jnp.where(left, post_ref[n, 2 + pair], tile), 64, 1)
            if cx != 0:
                ref = low_ref if cx == 1 else high_ref
                at = 8 + 2 * pair - cy
                slot = X_SLOT[n]
                enters = jnp.where(
                    left[:1], ref[slot, pl.ds(at, 1), :], ref[slot, pl.ds(at + 1, 1), :]
                )
                tile = jnp.where(
                    row == (0 if cx == 1 else 7),
                    jnp.broadcast_to(enters, (8, 128)),
                    pltpu.roll(tile, 1 if cx == 1 else 7, 0),
                )
            out_ref[n, :, here] = tile
        return carry

    lax.fori_loop(0, 32, stream, 0)


def call(kernel, out, scratch, flops, moved):
    return pl.pallas_call(
        kernel,
        out_shape=[jax.ShapeDtypeStruct(shape, F32) for shape in out],
        scratch_shapes=[pltpu.VMEM(shape, F32) for shape in scratch],
        compiler_params=pltpu.CompilerParams(vmem_limit_bytes=VMEM_BYTES),
        cost_estimate=pl.CostEstimate(flops=flops, bytes_accessed=moved, transcendentals=0),
    )


def ring(values, axis, step):
    size = lax.axis_size(axis)
    return lax.ppermute(values, axis, [(i, (i + step) % size) for i in range(size)])


def edge_moments(popul):
    density = jnp.sum(popul, axis=0)
    momentum = []
    for k in range(3):
        momentum.append(
            sum(VELOCITIES[n][k] * popul[n] for n in range(19) if VELOCITIES[n][k] != 0)
        )
    return [density] + momentum


def neighbours(populations, applied):
    popul = populations.reshape(19, 8, 64, 64)
    field = applied.reshape(3, 8, 64, 64)

    def package(edge, numbers):
        return jnp.stack([edge[n] for n in numbers] + edge_moments(edge))

    up_y = package(popul[:, :, 63], [f[2] for f in Y_FACE])
    down_y = package(popul[:, :, 0], [f[3] for f in Y_FACE])
    up_y = jnp.concatenate([up_y, field[:, :, 62], field[:, :, 63]])
    down_y = jnp.concatenate([down_y, field[:, :, 0], field[:, :, 1]])
    before = ring(up_y, "gy", 1)
    after = ring(down_y, "gy", -1)
    y_side = jnp.concatenate([after[:9], before[:9]], axis=-1)
    field_y = jnp.concatenate(
        [
            before[9:12, :, None],
            before[12:, :, None],
            field,
            after[9:12, :, None],
            after[12:, :, None],
        ],
        axis=2,
    )
    zero = jnp.zeros((64,), F32)

    def package_x(x, numbers, slot):
        edge = popul[:, x]
        rows = package(edge, numbers)
        moments_low, moments_high = before[5:9, x], after[5:9, x]
        low = jnp.stack([zero, before[slot, x], zero, zero, zero] + list(moments_low))
        high = jnp.stack([zero, zero, after[slot, x], zero, zero] + list(moments_high))
        rows = jnp.concatenate([low[:, None], rows, high[:, None]], axis=1)
        return jnp.pad(rows, ((0, 0), (1, 1), (0, 0)))

    up_x = jnp.concatenate(
        [package_x(7, [f[2] for f in X_FACE], 1), field_y[:, 6], field_y[:, 7]]
    )
    down_x = jnp.concatenate(
        [package_x(0, [f[3] for f in X_FACE], 2), field_y[:, 0], field_y[:, 1]]
    )
    lower = ring(up_x, "gx", 1)
    upper = ring(down_x, "gx", -1)
    x_side = jnp.concatenate([lower[:9], upper[:9]], axis=-1)
    x_side = jnp.pad(x_side, ((0, 0), (6, 6), (0, 0)))
    wide = jnp.concatenate(
        [
            lower[9:12, None],
            lower[12:, None],
            field_y,
            upper[9:12, None],
            upper[12:, None],
        ],
        axis=1,
    )
    wide = jnp.pad(wide, ((0, 0), (0, 0), (6, 6), (0, 0)), constant_values=1.0)
    wide = jnp.concatenate([wide, wide], axis=-1).reshape(36 * PITCH, 128)
    return wide, x_side, y_side


GROUPS = [[(2 * m + core) * GY + g for m in range(8) for g in range(GY)] for core in range(2)]


def exchange(rows, count):
    blocks = rows.reshape(64, 1, count * 128)
    blocks = lax.all_to_all(
        blocks, ("gx", "gy"), 0, 0, axis_index_groups=GROUPS, tiled=True
    )
    return blocks.reshape(64 * count, 128)


def on_device(populations, h_axial, h_transverse):
    t = tables()
    magnet, rows = call(
        first_kernel,
        [(3, 8, 4096), (64 * ROWS_FWD, 128)],
        [(1536, 128)],
        30_000_000,
        1_600_000,
    )(h_transverse, h_axial, t["fwd_z"])
    own = exchange(rows, ROWS_FWD)
    other = lax.ppermute(own, "gx", [(i, i ^ 1) for i in range(GX)])
    (rows,) = call(
        plane_kernel, [(64 * ROWS_BACK, 128)], [(128, 1536)], 400_000_000, 3_000_000
    )(
        own,
        other,
        t["fwd_x"],
        t["back_x"],
        t["even"],
        t["odd"],
        t["back_even"],
        t["back_odd"],
        t["wave_x"],
        t["wave_y"],
        t["wave_z"],
    )
    recv = exchange(rows, ROWS_BACK)
    applied = jnp.concatenate([h_transverse, h_axial[None]], axis=0)
    wide, x_side, y_side = neighbours(populations, applied)
    result, demag = call(
        cell_kernel,
        [(19, 8, 4096), (3, 8, 4096)],
        [
            (ROWS_BACK * 128, 128),
            (36 * PITCH, 128),
            (19, 34, 8, 128),
            (5, PITCH, 128),
            (5, PITCH, 128),
        ],
        60_000_000,
        8_000_000,
    )(recv, t["back_z"], wide, magnet, populations, x_side, y_side)
    return result, demag


def solution(mesh):
    placed = (P(None, "gx", "gy"), P("gx", "gy"), P(None, "gx", "gy"))
    return jax.shard_map(
        on_device,
        mesh=mesh,
        in_specs=placed,
        out_specs=(P(None, "gx", "gy"), P(None, "gx", "gy")),
        check_vma=False,
    )
```

```python
import functools

import jax
import jax.numpy as jnp
import numpy as np
from jax import lax
from jax.experimental import pallas as pl
from jax.experimental.pallas import tpu as pltpu
from jax.sharding import PartitionSpec as P

NX, NY, NZ = 128, 512, 64
GX, GY = 16, 8
VELOCITIES = (
    (0, 0, 0),
    (1, 0, 0),
    (-1, 0, 0),
    (0, 1, 0),
    (0, -1, 0),
    (0, 0, 1),
    (0, 0, -1),
    (1, 1, 0),
    (-1, -1, 0),
    (1, -1, 0),
    (-1, 1, 0),
    (1, 0, 1),
    (-1, 0, -1),
    (1, 0, -1),
    (-1, 0, 1),
    (0, 1, 1),
    (0, -1, -1),
    (0, 1, -1),
    (0, -1, 1),
)
WEIGHTS = (1.0 / 3.0,) + (1.0 / 18.0,) * 6 + (1.0 / 36.0,) * 12
OMEGA = 1.0 / 0.6
HIGHEST = lax.Precision.HIGHEST
F32 = jnp.float32

X_FACE = ((0, 0, 1, 2), (1, 0, 7, 10), (-1, 0, 9, 8), (0, 1, 11, 14), (0, -1, 13, 12))
Y_FACE = ((0, 0, 3, 4), (1, 0, 7, 9), (-1, 0, 10, 8), (0, 1, 15, 18), (0, -1, 17, 16))
X_SLOT = {n: s for s, row in enumerate(X_FACE) for n in row[2:]}

ROWS_FWD = 12
ROWS_BACK = 20
CORNER = 480
FACE_ROWS = CORNER + 48
PITCH = 80


def cas(rows, cols, count):
    angle = 2.0 * np.pi * ((rows[:, None] * cols[None, :]) % count) / count
    return np.cos(angle) + np.sin(angle)


def wave(index, count):
    return 2.0 * np.sin(np.pi * index / count)


@functools.lru_cache(maxsize=None)
def tables():
    every_x, every_z = np.arange(NX), np.arange(NZ)
    half = np.arange(NY // 2)
    out = {}
    fwd_z = np.zeros((NZ, 128))
    fwd_z[:, :NZ] = cas(every_z, every_z, NZ)
    out["fwd_z"] = fwd_z
    out["back_z"] = np.tile(cas(every_z, every_z, NZ), (1, 2))
    fwd_x, back_x = [], []
    m = np.arange(8)
    for parity in range(2):
        order = []
        for side in (parity, 1 - parity):
            for x2 in range(2):
                for x4 in range(4):
                    order += list(8 * (2 * m + side) + 2 * x4 + x2)
        fwd_x.append(cas(every_x, np.array(order), NX))
        order = []
        for x2 in range(2):
            for x6 in range(6):
                order += list((8 * (2 * m + parity) - 2 + 2 * x6 + x2) % NX)
        back_x.append(cas(np.array(order), every_x, NX))
    out["fwd_x"] = np.stack(fwd_x)
    out["back_x"] = np.stack(back_x)
    even, odd = 2 * half, 2 * half + 1
    halo = np.array(
        [
            (64 * g + (-2, -1, 64, 65)[k]) % NY
            for g in range(GY)
            for c in range(4)
            for k in range(4)
        ]
    )
    out["even"] = cas(half, even, NY)
    out["odd"] = cas(half, odd, NY)
    out["back_even"] = np.concatenate([cas(even, half, NY), cas(even, halo, NY)], axis=1)
    out["back_odd"] = np.concatenate([cas(odd, half, NY), cas(odd, halo, NY)], axis=1)
    out["wave_x"] = np.repeat(wave(every_x, NX)[:, None], 128, axis=1)
    out["wave_y"] = np.stack([wave(even, NY), wave(odd, NY)])
    out["wave_z"] = np.repeat(wave(every_z, NZ)[:, None], 128, axis=1)
    return {name: np.asarray(value, np.float32) for name, value in out.items()}


def dot(a, b, dims=(1, 0)):
    return lax.dot_general(
        a, b, (((dims[0],), (dims[1],)), ((), ())), precision=HIGHEST, preferred_element_type=F32
    )


def langevin(hx, hy, hz):
    magnitude = jnp.sqrt(hx * hx + hy * hy + hz * hz)
    argument = 1.5 * magnitude
    decay = jnp.exp(-2.0 * argument)
    scale = ((1.0 + decay) / (1.0 - decay) - 1.0 / argument) / magnitude
    return hx * scale, hy * scale, hz * scale


def lanes(shape=(8, 128)):
    return lax.broadcasted_iota(jnp.int32, shape, len(shape) - 1)


def moments_of(popul):
    density = popul[0]
    for n in range(1, 19):
        density = density + popul[n]
    momentum = []
    for k in range(3):
        total = None
        for n in range(1, 19):
            if VELOCITIES[n][k] == 1:
                total = popul[n] if total is None else total + popul[n]
            elif VELOCITIES[n][k] == -1:
                total = total - popul[n]
        momentum.append(total)
    return density, momentum


def first_kernel(
    ht_ref, ha_ref, low_ref, high_ref, table_ref, magnet_ref, send_ref, up_ref, down_ref, rows_ref
):
    magnet = langevin(ht_ref[:256, :], ht_ref[256:, :], ha_ref[...])
    for c in range(3):
        magnet_ref[c * 256 : c * 256 + 256, :] = magnet[c]
        for pair in range(32):
            tile = magnet[c][pair * 8 : pair * 8 + 8, :]
            rows_ref[pl.ds(c * 512 + 2 * pair, 8, stride=64), :] = tile
            rows_ref[pl.ds(c * 512 + 2 * pair + 1, 8, stride=64), :] = pltpu.roll(tile, 64, 1)
    spectrum = dot(table_ref[...], rows_ref[...], (1, 1))
    for row in range(ROWS_FWD):
        send_ref[pl.ds(row, NZ, stride=ROWS_FWD), :] = spectrum[:, row * 128 : row * 128 + 128]
    for edge_ref, out_ref, which, pair in ((high_ref, up_ref, 2, 31), (low_ref, down_ref, 3, 0)):
        popul = [edge_ref[n, 0] for n in range(19)]
        density, momentum = moments_of(popul)
        tiles = [popul[face[which]] for face in Y_FACE] + [density] + momentum
        for ref, at in ((ht_ref, 0), (ht_ref, 256), (ha_ref, 0)):
            tiles.append(ref[at + pair * 8 : at + pair * 8 + 8, :])
        for k, tile in enumerate(tiles):
            out_ref[k * 8 : k * 8 + 8, :] = tile


def face_kernel(pop_ref, ht_ref, ha_ref, before_ref, after_ref, pair_ref, next_ref):
    parity = lax.rem(lax.axis_index("gx"), 2)
    for out_ref, up in ((pair_ref, parity == 0), (next_ref, parity == 1)):
        face = jnp.where(up, 7, 0)
        second = jnp.where(up, 6, 1)

        def line(ref, at):
            return ref[pl.ds(at, 32, stride=8), :]

        popul = [line(pop_ref, n * 256 + face) for n in range(19)]
        density, momentum = moments_of(popul)
        lines = [jnp.where(up, popul[f[2]], popul[f[3]]) for f in X_FACE] + [density] + momentum
        for x in (face, second):
            lines += [line(ht_ref, x), line(ht_ref, 256 + x), line(ha_ref, x)]
        for k, value in enumerate(lines):
            out_ref[k * 32 : k * 32 + 32, :] = value
        for ref, at in ((before_ref, CORNER), (after_ref, CORNER + 16)):
            out_ref[at : at + 16, :] = jnp.zeros((16, 128), F32)
            out_ref[at : at + 12, :] = ref[pl.ds(face, 12, stride=8), :]
        for ref, at in ((before_ref, CORNER + 32), (after_ref, CORNER + 40)):
            out_ref[at : at + 8, :] = jnp.zeros((8, 128), F32)
            out_ref[at : at + 3, :] = ref[pl.ds(72 + second, 3, stride=8), :]


def transpose_blocks(tiles):
    block = lanes() // 16
    for bit in (1, 2, 4):
        low = (block & bit) == 0
        out = list(tiles)
        for i in range(8):
            if i & bit == 0:
                a, b = tiles[i], tiles[i | bit]
                out[i] = jnp.where(low, a, pltpu.roll(b, 16 * bit, 1))
                out[i | bit] = jnp.where(low, pltpu.roll(a, 128 - 16 * bit, 1), b)
        tiles = out
    return tiles


def plane_kernel(
    own_ref,
    other_ref,
    fwd_x_ref,
    back_x_ref,
    even_ref,
    odd_ref,
    back_even_ref,
    back_odd_ref,
    wave_x_ref,
    wave_y_ref,
    wave_z_ref,
    send_ref,
    cells_ref,
):
    row = lax.axis_index("gx")
    parity = lax.rem(row, 2)
    index_z = (row // 2) * GY + lax.axis_index("gy")
    left = lanes() < 64
    for side, ref in enumerate((own_ref, other_ref)):
        for c in range(3):
            for pair in range(4):
                for x4 in range(4):
                    start = 2 * pair * ROWS_FWD + c * 4 + x4
                    a = ref[pl.ds(start, 8, stride=GY * ROWS_FWD), :]
                    b = ref[pl.ds(start + ROWS_FWD, 8, stride=GY * ROWS_FWD), :]
                    at = side * 64 + x4 * 8
                    col = c * 512 + pair * 128
                    cells_ref[at : at + 8, col : col + 128] = jnp.where(
                        left, a, pltpu.roll(b, 64, 1)
                    )
                    cells_ref[at + 32 : at + 40, col : col + 128] = jnp.where(
                        left, pltpu.roll(a, 64, 1), b
                    )
    wave_x = wave_x_ref[:, 0:1]
    wave_z = wave_z_ref[pl.ds(index_z, 1), 0:1]
    spectrum = dot(fwd_x_ref[parity], cells_ref[...])
    along = wave_x * spectrum[:, :512] + wave_z * spectrum[:, 1024:]
    both = jnp.concatenate([along, spectrum[:, 512:1024]], axis=0)
    parts = (
        dot(both[:, :256] + both[:, 256:], even_ref[...]),
        dot(both[:, :256] - both[:, 256:], odd_ref[...]),
    )
    back = []
    for which in range(2):
        wave_y = wave_y_ref[which : which + 1, :]
        squared = wave_x * wave_x + wave_y * wave_y + wave_z * wave_z
        anchor = squared == 0.0
        factor = jnp.where(
            anchor, 0.0, (-1.0 / (NX * NY * NZ)) / jnp.where(anchor, 1.0, squared)
        )
        potential = (parts[which][:128] + wave_y * parts[which][128:]) * factor
        stacked = jnp.concatenate([potential, wave_y * potential], axis=0)
        back.append(dot(stacked, (back_even_ref, back_odd_ref)[which][...]))
    low, high = back[0] + back[1], back[0] - back[1]
    column = lanes((128, 128)) % 16
    halo_p, halo_q = low[:128, 256:], low[128:, 256:]
    halo = jnp.where(
        column < 4,
        wave_x * halo_p,
        jnp.where(column < 8, halo_q, jnp.where(column < 12, wave_z * halo_p, 0.0)),
    )
    potential = jnp.concatenate([low[:128, :256], high[:128, :256]], axis=1)
    fields = jnp.concatenate(
        [wave_x * potential, low[128:, :256], high[128:, :256], wave_z * potential, halo], axis=1
    )
    cells = dot(back_x_ref[parity], fields)
    step = GY * ROWS_BACK
    for x6 in range(6):
        for c in range(3):
            for pair in range(4):
                col = c * 512 + pair * 128
                a = cells[x6 * 8 : x6 * 8 + 8, col : col + 128]
                b = cells[48 + x6 * 8 : 56 + x6 * 8, col : col + 128]
                at = 2 * pair * ROWS_BACK + c * 6 + x6
                send_ref[pl.ds(at, 8, stride=step), :] = jnp.where(left, a, pltpu.roll(b, 64, 1))
                send_ref[pl.ds(at + ROWS_BACK, 8, stride=step), :] = jnp.where(
                    left, pltpu.roll(a, 64, 1), b
                )
    for part in range(2):
        tiles = []
        for x in range(part * 8, part * 8 + 8):
            if x < 12:
                at = (x % 2) * 48 + (x // 2) * 8
                tiles.append(cells[at : at + 8, 1536:])
            else:
                tiles.append(jnp.zeros((8, 128), F32))
        for g, tile in enumerate(transpose_blocks(tiles)):
            send_ref[pl.ds(g * ROWS_BACK + 18 + part, 8, stride=step), :] = tile


def macroscopic(density, momentum, force):
    inverse = 1.0 / density
    vel = [(momentum[k] + 0.5 * force[k]) * inverse for k in range(3)]
    u_square = vel[0] * vel[0] + vel[1] * vel[1] + vel[2] * vel[2]
    u_dot_f = vel[0] * force[0] + vel[1] * force[1] + vel[2] * force[2]
    scaled = OMEGA * density
    base = scaled * (1.0 - 1.5 * u_square) - 0.5 * u_dot_f
    return vel, scaled, base


def along(lattice, vector):
    total = None
    for sign, value in zip(lattice, vector):
        if isinstance(sign, int):
            if sign == 0:
                continue
            term = value if sign == 1 else -value
        else:
            term = sign * value
        total = term if total is None else total + term
    return total


def relax_terms(lattice, vel, force, scaled, base):
    along_u = along(lattice, vel)
    along_f = along(lattice, force)
    even = base + along_u * (4.5 * scaled * along_u + 1.5 * along_f)
    odd = 3.0 * scaled * along_u + 0.5 * along_f
    return even, odd


def shift_z(tile, step, lane):
    if step == 0:
        return tile
    if step == 1:
        return jnp.where(lane % 64 == 0, pltpu.roll(tile, 65, 1), pltpu.roll(tile, 1, 1))
    return jnp.where(lane % 64 == 63, pltpu.roll(tile, 63, 1), pltpu.roll(tile, 127, 1))


def cell_kernel(
    recv_ref,
    table_ref,
    ht_ref,
    ha_ref,
    magnet_ref,
    pop_ref,
    pair_ref,
    next_ref,
    before_ref,
    after_ref,
    out_ref,
    demag_ref,
    field_ref,
    total_ref,
    post_ref,
    side_ref,
    enter_ref,
):
    lane = lanes()
    left = lane < 64
    left4 = lanes((32, 128)) < 64
    parity = lax.rem(lax.axis_index("gx"), 2)
    side_of = ((next_ref, pair_ref), (pair_ref, next_ref))

    def side(which, at, count):
        even, odd = side_of[which]
        return jnp.where(parity == 0, even[at : at + count, :], odd[at : at + count, :])

    def base(c, x):
        return (c * 12 + 2 + x) * PITCH + 8

    def both(tile):
        turned = pltpu.roll(tile, 64, 1)
        first = lanes(tile.shape) < 64
        return jnp.where(first, tile, turned), jnp.where(first, turned, tile)

    own = ((ht_ref, 0), (ht_ref, 256), (ha_ref, 0))
    for c in range(3):
        ref, at = own[c]
        for pair in range(32):
            for odd, tile in enumerate(both(ref[at + pair * 8 : at + pair * 8 + 8, :])):
                total_ref[pl.ds(base(c, 0) + 2 * pair + odd, 8, stride=PITCH), :] = tile
        for edge_ref, y in ((before_ref, -2), (after_ref, 64)):
            for odd, tile in enumerate(both(edge_ref[72 + c * 8 : 80 + c * 8, :])):
                total_ref[pl.ds(base(c, 0) + y + odd, 8, stride=PITCH), :] = tile
        for which, near, far in ((0, -1, -2), (1, 8, 9)):
            for x, k, corner in ((near, 9 + c, 9 + c), (far, 12 + c, 32 + c)):
                for odd, tile in enumerate(both(side(which, k * 32, 32))):
                    total_ref[pl.ds(base(c, x) + odd, 32, stride=2), :] = tile
                after = 16 if x == near else 8
                for y, at in ((-2, CORNER + corner), (64, CORNER + corner + after)):
                    for odd, tile in enumerate(both(side(which, at, 1))):
                        at_row = base(c, x) + y + odd
                        total_ref[at_row : at_row + 1, :] = tile

    for row in range(ROWS_BACK):
        spectrum = recv_ref[pl.ds(row, NZ, stride=ROWS_BACK), :]
        cells = dot(spectrum, table_ref[...], (0, 0))
        if row < 18:
            field_ref[row * 128 : row * 128 + 128, :] = cells
            for half in range(2):
                c, x = row // 6, 2 * (row % 6) + half - 2
                at = base(c, x)
                total_ref[at : at + 64, :] += cells[half * 64 : half * 64 + 64, :]
        else:
            for k in range(8):
                x = (row - 18) * 8 + k - 2
                if x < 10:
                    for c in range(3):
                        at, src = base(c, x), k * 16 + c * 4
                        total_ref[at - 2 : at, :] += cells[src : src + 2, :]
                        total_ref[at + 64 : at + 66, :] += cells[src + 2 : src + 4, :]

    def forces(magnet, read, first):
        force = []
        for c in range(3):
            d_x = jnp.where(first, *read(c, 1, 0)) - jnp.where(first, *read(c, -1, 0))
            d_y = jnp.where(first, *read(c, 0, 1)) - jnp.where(first, *read(c, 0, -1))
            a, b = read(c, 0, 0)
            d_z = jnp.where(first, pltpu.roll(a, 127, 1), pltpu.roll(b, 127, 1)) - jnp.where(
                first, pltpu.roll(a, 1, 1), pltpu.roll(b, 1, 1)
            )
            force.append(0.025 * (magnet[0] * d_x + magnet[1] * d_y + magnet[2] * d_z))
        return force

    def column(c, x, y):
        return total_ref[pl.ds(base(c, x) + y, 8, stride=PITCH), :]

    sign = jnp.where(left, -1.0, 1.0)
    values = [
        jnp.where(left, after_ref[k * 8 : k * 8 + 8, :], before_ref[k * 8 : k * 8 + 8, :])
        for k in range(12)
    ]
    force = forces(
        langevin(*values[9:]),
        lambda c, dx, dy: (column(c, dx, 64 + dy), column(c, dx, dy - 1)),
        left,
    )
    vel, scaled, rest = macroscopic(values[5], values[6:9], force)
    for slot, (cx, cz, up, down) in enumerate(Y_FACE):
        even, odd = relax_terms((cx, sign, cz), vel, force, scaled, rest)
        post = shift_z((1.0 - OMEGA) * values[slot] + WEIGHTS[up] * (even + odd), cz, lane)
        post_ref[up, 0] = post
        post_ref[down, 33] = post

    row = lax.broadcasted_iota(jnp.int32, (8, 128), 0)
    upper = row == 7

    def edge_rows(k_low, k_high):
        pair = []
        for which, k in ((0, k_low), (1, k_high)):
            value = jnp.where(
                left[:1], side(which, CORNER + 16 + k, 1), side(which, CORNER + k, 1)
            )
            pair.append(jnp.broadcast_to(value, (8, 128)))
        return jnp.where(upper, pair[1], pair[0])

    def corner(c, dx, y):
        return jnp.where(upper, column(c, 1 + dx, y), column(c, dx - 1, y))

    force = forces(
        langevin(*[edge_rows(k, k) for k in (9, 10, 11)]),
        lambda c, dx, dy: (corner(c, dx, 64 + dy), corner(c, dx, dy - 1)),
        left,
    )
    vel, scaled, rest = macroscopic(edge_rows(5, 5), [edge_rows(k, k) for k in (6, 7, 8)], force)
    even, odd = relax_terms((jnp.where(upper, -1.0, 1.0), sign, 0), vel, force, scaled, rest)
    edges = (1.0 - OMEGA) * edge_rows(1, 2) + WEIGHTS[7] * (even + odd)

    for which, x, step in ((0, -1, 1), (1, 8, -1)):

        def read(c, dx, dy):
            at = base(c, x + dx) + dy
            return (
                total_ref[pl.ds(at, 32, stride=2), :],
                total_ref[pl.ds(at + 1, 32, stride=2), :],
            )

        values = [side(which, k * 32, 32) for k in range(12)]
        force = forces(langevin(*values[9:]), read, left4)
        vel, scaled, rest = macroscopic(values[5], values[6:9], force)
        at_edge = 7 * which
        lane4 = lanes((32, 128))
        for slot, (cy, cz, up, down) in enumerate(X_FACE):
            even, odd = relax_terms((step, cy, cz), vel, force, scaled, rest)
            post = shift_z((1.0 - OMEGA) * values[slot] + WEIGHTS[up] * (even + odd), cz, lane4)
            if cy != 0:
                side_ref[8:40, :] = post
                if cy == 1:
                    side_ref[7:8, :] = edges[at_edge : at_edge + 1, :]
                    post = jnp.where(left4, post, side_ref[7:39, :])
                else:
                    side_ref[40:41, :] = edges[at_edge : at_edge + 1, :]
                    post = jnp.where(left4, side_ref[9:41, :], post)
                post = pltpu.roll(post, 64, 1)
            enter_ref[which, slot] = post

    def collide(pair, carry):
        ya = 2 * pair
        at = pl.multiple_of(pair * 8, 8)
        for c in range(3):
            src = (c * 12 + 2) * 64 + ya
            demag_ref[pl.ds(c * 256 + at, 8), :] = jnp.where(
                left,
                field_ref[pl.ds(src, 8, stride=64), :],
                field_ref[pl.ds(src + 1, 8, stride=64), :],
            )
        force = forces(
            [magnet_ref[pl.ds(c * 256 + at, 8), :] for c in range(3)],
            lambda c, dx, dy: (column(c, dx, ya + dy), column(c, dx, ya + 1 + dy)),
            left,
        )
        popul = [pop_ref[pl.ds(n * 256 + at, 8), :] for n in range(19)]
        density, momentum = moments_of(popul)
        vel, scaled, rest = macroscopic(density, momentum, force)
        post_ref[0, 1 + pair] = (1.0 - OMEGA) * popul[0] + WEIGHTS[0] * rest
        for n in range(1, 19, 2):
            even, odd = relax_terms(VELOCITIES[n], vel, force, scaled, rest)
            for number, value in ((n, even + odd), (n + 1, even - odd)):
                post = (1.0 - OMEGA) * popul[number] + WEIGHTS[n] * value
                post_ref[number, 1 + pair] = shift_z(post, VELOCITIES[number][2], lane)
        return carry

    lax.fori_loop(0, 32, collide, 0)

    def stream(pair, carry):
        at = pl.multiple_of(pair * 8, 8)
        for n in range(19):
            cx, cy, _ = VELOCITIES[n]
            tile = post_ref[n, 1 + pair]
            if cy == 1:
                tile = pltpu.roll(jnp.where(left, tile, post_ref[n, pair]), 64, 1)
            elif cy == -1:
                tile = pltpu.roll(jnp.where(left, post_ref[n, 2 + pair], tile), 64, 1)
            if cx != 0:
                enters = enter_ref[0 if cx == 1 else 1, X_SLOT[n], pl.ds(pair, 1), :]
                tile = jnp.where(
                    row == (0 if cx == 1 else 7),
                    jnp.broadcast_to(enters, (8, 128)),
                    pltpu.roll(tile, 1 if cx == 1 else 7, 0),
                )
            out_ref[pl.ds(n * 256 + at, 8), :] = tile
        return carry

    lax.fori_loop(0, 32, stream, 0)


def call(kernel, out, scratch, flops, moved, vmem, **more):
    return pl.pallas_call(
        kernel,
        out_shape=[jax.ShapeDtypeStruct(shape, F32) for shape in out],
        scratch_shapes=[pltpu.VMEM(shape, F32) for shape in scratch],
        compiler_params=pltpu.CompilerParams(vmem_limit_bytes=vmem * 1024 * 1024),
        cost_estimate=pl.CostEstimate(flops=flops, bytes_accessed=moved, transcendentals=0),
        **more,
    )


def ring(values, axis, step):
    size = lax.axis_size(axis)
    return lax.ppermute(values, axis, [(i, (i + step) % size) for i in range(size)])


GROUPS = [[(2 * m + core) * GY + g for m in range(8) for g in range(GY)] for core in range(2)]


def exchange(rows, count):
    blocks = rows.reshape(64, 1, count * 128)
    blocks = lax.all_to_all(
        blocks, ("gx", "gy"), 0, 0, axis_index_groups=GROUPS, tiled=True
    )
    return blocks.reshape(64 * count, 128)


def as_tiles(values):
    return values.reshape(-1, 8, 32, 128).transpose(0, 2, 1, 3)


def from_rows(rows):
    return rows.reshape(-1, 32, 8, 128).transpose(0, 2, 1, 3).reshape(-1, 8, 4096)


def on_device(populations, h_axial, h_transverse):
    t = tables()
    pop_tiles = as_tiles(populations)
    pop_rows = pop_tiles.reshape(19 * 256, 128)
    ht_rows = as_tiles(h_transverse).reshape(512, 128)
    ha_rows = as_tiles(h_axial).reshape(256, 128)
    whole = pl.BlockSpec(memory_space=pltpu.VMEM)
    magnet, rows, up, down = call(
        first_kernel,
        [(768, 128), (64 * ROWS_FWD, 128), (96, 128), (96, 128)],
        [(1536, 128)],
        30_000_000,
        1_800_000,
        8,
        grid=(1,),
        in_specs=[
            whole,
            whole,
            pl.BlockSpec((19, 1, 8, 128), lambda i: (0, 0, 0, 0)),
            pl.BlockSpec((19, 1, 8, 128), lambda i: (0, 31, 0, 0)),
            whole,
        ],
        out_specs=[whole] * 4,
    )(ht_rows, ha_rows, pop_tiles, pop_tiles, t["fwd_z"])
    own = exchange(rows, ROWS_FWD)
    before = ring(up, "gy", 1)
    after = ring(down, "gy", -1)
    to_pair, to_next = call(
        face_kernel,
        [(FACE_ROWS, 128), (FACE_ROWS, 128)],
        [],
        1_000_000,
        4_000_000,
        8,
    )(pop_rows, ht_rows, ha_rows, before, after)
    other = lax.ppermute(own, "gx", [(i, i ^ 1) for i in range(GX)])
    pair = lax.ppermute(to_pair, "gx", [(i, i ^ 1) for i in range(GX)])
    beyond = lax.ppermute(to_next, "gx", [(i, ((i + 1) ^ 1) - 1 & 15) for i in range(GX)])
    (rows,) = call(
        plane_kernel, [(64 * ROWS_BACK, 128)], [(128, 1536)], 400_000_000, 3_000_000, 16
    )(
        own,
        other,
        t["fwd_x"],
        t["back_x"],
        t["even"],
        t["odd"],
        t["back_even"],
        t["back_odd"],
        t["wave_x"],
        t["wave_y"],
        t["wave_z"],
    )
    recv = exchange(rows, ROWS_BACK)
    result, demag = call(
        cell_kernel,
        [(19 * 256, 128), (3 * 256, 128)],
        [
            (18 * 128, 128),
            (36 * PITCH, 128),
            (19, 34, 8, 128),
            (48, 128),
            (2, 5, 32, 128),
        ],
        60_000_000,
        8_000_000,
        24,
    )(recv, t["back_z"], ht_rows, ha_rows, magnet, pop_rows, pair, beyond, before, after)
    return from_rows(result), from_rows(demag)


def solution(mesh):
    placed = (P(None, "gx", "gy"), P("gx", "gy"), P(None, "gx", "gy"))
    return jax.shard_map(
        on_device,
        mesh=mesh,
        in_specs=placed,
        out_specs=(P(None, "gx", "gy"), P(None, "gx", "gy")),
        check_vma=False,
    )
```

```python
import functools

import jax
import jax.numpy as jnp
import numpy as np
from jax import lax
from jax.experimental import pallas as pl
from jax.experimental.pallas import tpu as pltpu
from jax.sharding import PartitionSpec as P

NX, NY, NZ = 128, 512, 64
GX, GY = 16, 8
VELOCITIES = (
    (0, 0, 0),
    (1, 0, 0),
    (-1, 0, 0),
    (0, 1, 0),
    (0, -1, 0),
    (0, 0, 1),
    (0, 0, -1),
    (1, 1, 0),
    (-1, -1, 0),
    (1, -1, 0),
    (-1, 1, 0),
    (1, 0, 1),
    (-1, 0, -1),
    (1, 0, -1),
    (-1, 0, 1),
    (0, 1, 1),
    (0, -1, -1),
    (0, 1, -1),
    (0, -1, 1),
)
WEIGHTS = (1.0 / 3.0,) + (1.0 / 18.0,) * 6 + (1.0 / 36.0,) * 12
OMEGA = 1.0 / 0.6
HIGHEST = lax.Precision.HIGHEST
F32 = jnp.float32

X_FACE = ((0, 0, 1, 2), (1, 0, 7, 10), (-1, 0, 9, 8), (0, 1, 11, 14), (0, -1, 13, 12))
Y_FACE = ((0, 0, 3, 4), (1, 0, 7, 9), (-1, 0, 10, 8), (0, 1, 15, 18), (0, -1, 17, 16))
X_SLOT = {n: s for s, row in enumerate(X_FACE) for n in row[2:]}

ROWS_FWD = 12
ROWS_BACK = 20
CORNER = 480
FACE_ROWS = CORNER + 48
PITCH = 80


def cas(rows, cols, count):
    angle = 2.0 * np.pi * ((rows[:, None] * cols[None, :]) % count) / count
    return np.cos(angle) + np.sin(angle)


def wave(index, count):
    return 2.0 * np.sin(np.pi * index / count)


@functools.lru_cache(maxsize=None)
def tables():
    every_x, every_z = np.arange(NX), np.arange(NZ)
    half = np.arange(NY // 2)
    out = {}
    fwd_z = np.zeros((NZ, 128))
    fwd_z[:, :NZ] = cas(every_z, every_z, NZ)
    out["fwd_z"] = fwd_z
    out["back_z"] = np.tile(cas(every_z, every_z, NZ), (1, 2))
    fwd_x, back_x = [], []
    m = np.arange(8)
    for parity in range(2):
        order = []
        for side in (parity, 1 - parity):
            for x2 in range(2):
                for x4 in range(4):
                    order += list(8 * (2 * m + side) + 2 * x4 + x2)
        fwd_x.append(cas(every_x, np.array(order), NX))
        order = []
        for x2 in range(2):
            for x6 in range(6):
                order += list((8 * (2 * m + parity) - 2 + 2 * x6 + x2) % NX)
        back_x.append(cas(np.array(order), every_x, NX))
    out["fwd_x"] = np.stack(fwd_x)
    out["back_x"] = np.stack(back_x)
    even, odd = 2 * half, 2 * half + 1
    halo = np.array(
        [
            (64 * g + (-2, -1, 64, 65)[k]) % NY
            for g in range(GY)
            for c in range(4)
            for k in range(4)
        ]
    )
    out["even"] = cas(half, even, NY)
    out["odd"] = cas(half, odd, NY)
    out["back_even"] = np.concatenate([cas(even, half, NY), cas(even, halo, NY)], axis=1)
    out["back_odd"] = np.concatenate([cas(odd, half, NY), cas(odd, halo, NY)], axis=1)
    out["wave_x"] = np.repeat(wave(every_x, NX)[:, None], 128, axis=1)
    out["wave_y"] = np.stack([wave(even, NY), wave(odd, NY)])
    out["wave_z"] = np.repeat(wave(every_z, NZ)[:, None], 128, axis=1)
    return {name: np.asarray(value, np.float32) for name, value in out.items()}


def dot(a, b, dims=(1, 0)):
    return lax.dot_general(
        a, b, (((dims[0],), (dims[1],)), ((), ())), precision=HIGHEST, preferred_element_type=F32
    )


def langevin(hx, hy, hz):
    magnitude = jnp.sqrt(hx * hx + hy * hy + hz * hz)
    argument = 1.5 * magnitude
    decay = jnp.exp(-2.0 * argument)
    scale = ((1.0 + decay) / (1.0 - decay) - 1.0 / argument) / magnitude
    return hx * scale, hy * scale, hz * scale


def lanes(shape=(8, 128)):
    return lax.broadcasted_iota(jnp.int32, shape, len(shape) - 1)


def moments_of(popul):
    density = popul[0]
    for n in range(1, 19):
        density = density + popul[n]
    momentum = []
    for k in range(3):
        total = None
        for n in range(1, 19):
            if VELOCITIES[n][k] == 1:
                total = popul[n] if total is None else total + popul[n]
            elif VELOCITIES[n][k] == -1:
                total = total - popul[n]
        momentum.append(total)
    return density, momentum


def start(*copies):
    started = [pltpu.make_async_copy(*copy) for copy in copies]
    for copy in started:
        copy.start()
    return started


def first_kernel(
    ht_hbm,
    ha_hbm,
    pop_hbm,
    table_hbm,
    send_ref,
    up_ref,
    down_ref,
    ht_ref,
    ha_ref,
    low_ref,
    high_ref,
    table_ref,
    rows_ref,
    sems,
):
    copies = start(
        (ht_hbm, ht_ref, sems.at[0]),
        (ha_hbm, ha_ref, sems.at[1]),
        (table_hbm, table_ref, sems.at[2]),
        (pop_hbm.at[:, 0], low_ref, sems.at[3]),
        (pop_hbm.at[:, 31], high_ref, sems.at[4]),
    )
    copies[0].wait()
    copies[1].wait()
    magnet = langevin(ht_ref[:256, :], ht_ref[256:, :], ha_ref[...])
    for c in range(3):
        for pair in range(32):
            tile = magnet[c][pair * 8 : pair * 8 + 8, :]
            rows_ref[pl.ds(c * 512 + 2 * pair, 8, stride=64), :] = tile
            rows_ref[pl.ds(c * 512 + 2 * pair + 1, 8, stride=64), :] = pltpu.roll(tile, 64, 1)
    copies[2].wait()
    spectrum = dot(table_ref[...], rows_ref[...], (1, 1))
    for row in range(ROWS_FWD):
        send_ref[pl.ds(row, NZ, stride=ROWS_FWD), :] = spectrum[:, row * 128 : row * 128 + 128]
    copies[3].wait()
    copies[4].wait()
    for edge_ref, out_ref, which, pair in ((high_ref, up_ref, 2, 31), (low_ref, down_ref, 3, 0)):
        popul = [edge_ref[n] for n in range(19)]
        density, momentum = moments_of(popul)
        tiles = [popul[face[which]] for face in Y_FACE] + [density] + momentum
        for ref, at in ((ht_ref, 0), (ht_ref, 256), (ha_ref, 0)):
            tiles.append(ref[at + pair * 8 : at + pair * 8 + 8, :])
        for k, tile in enumerate(tiles):
            out_ref[k * 8 : k * 8 + 8, :] = tile


def face_kernel(
    pop_hbm,
    ht_hbm,
    ha_hbm,
    before_ref,
    after_ref,
    pair_ref,
    next_ref,
    magnet_ref,
    pop_ref,
    ht_ref,
    ha_ref,
    sems,
):
    copies = start(
        (pop_hbm, pop_ref, sems.at[0]), (ht_hbm, ht_ref, sems.at[1]), (ha_hbm, ha_ref, sems.at[2])
    )
    copies[1].wait()
    copies[2].wait()
    magnet = langevin(ht_ref[:256, :], ht_ref[256:, :], ha_ref[...])
    for c in range(3):
        magnet_ref[c * 256 : c * 256 + 256, :] = magnet[c]
    copies[0].wait()
    parity = lax.rem(lax.axis_index("gx"), 2)
    for out_ref, up in ((pair_ref, parity == 0), (next_ref, parity == 1)):
        face = jnp.where(up, 7, 0)
        second = jnp.where(up, 6, 1)

        def line(ref, at):
            return ref[pl.ds(at, 32, stride=8), :]

        popul = [line(pop_ref, n * 256 + face) for n in range(19)]
        density, momentum = moments_of(popul)
        lines = [jnp.where(up, popul[f[2]], popul[f[3]]) for f in X_FACE] + [density] + momentum
        for x in (face, second):
            lines += [line(ht_ref, x), line(ht_ref, 256 + x), line(ha_ref, x)]
        for k, value in enumerate(lines):
            out_ref[k * 32 : k * 32 + 32, :] = value
        for ref, at in ((before_ref, CORNER), (after_ref, CORNER + 16)):
            out_ref[at : at + 16, :] = jnp.zeros((16, 128), F32)
            out_ref[at : at + 12, :] = ref[pl.ds(face, 12, stride=8), :]
        for ref, at in ((before_ref, CORNER + 32), (after_ref, CORNER + 40)):
            out_ref[at : at + 8, :] = jnp.zeros((8, 128), F32)
            out_ref[at : at + 3, :] = ref[pl.ds(72 + second, 3, stride=8), :]


def transpose_blocks(tiles):
    block = lanes() // 16
    for bit in (1, 2, 4):
        low = (block & bit) == 0
        out = list(tiles)
        for i in range(8):
            if i & bit == 0:
                a, b = tiles[i], tiles[i | bit]
                out[i] = jnp.where(low, a, pltpu.roll(b, 16 * bit, 1))
                out[i | bit] = jnp.where(low, pltpu.roll(a, 128 - 16 * bit, 1), b)
        tiles = out
    return tiles


def plane_kernel(
    own_ref,
    other_ref,
    fwd_x_ref,
    back_x_ref,
    even_ref,
    odd_ref,
    back_even_ref,
    back_odd_ref,
    wave_x_ref,
    wave_y_ref,
    wave_z_ref,
    send_ref,
    cells_ref,
):
    row = lax.axis_index("gx")
    parity = lax.rem(row, 2)
    index_z = (row // 2) * GY + lax.axis_index("gy")
    left = lanes() < 64
    for side, ref in enumerate((own_ref, other_ref)):
        for c in range(3):
            for pair in range(4):
                for x4 in range(4):
                    start = 2 * pair * ROWS_FWD + c * 4 + x4
                    a = ref[pl.ds(start, 8, stride=GY * ROWS_FWD), :]
                    b = ref[pl.ds(start + ROWS_FWD, 8, stride=GY * ROWS_FWD), :]
                    at = side * 64 + x4 * 8
                    col = c * 512 + pair * 128
                    cells_ref[at : at + 8, col : col + 128] = jnp.where(
                        left, a, pltpu.roll(b, 64, 1)
                    )
                    cells_ref[at + 32 : at + 40, col : col + 128] = jnp.where(
                        left, pltpu.roll(a, 64, 1), b
                    )
    wave_x = wave_x_ref[:, 0:1]
    wave_z = wave_z_ref[pl.ds(index_z, 1), 0:1]
    spectrum = dot(fwd_x_ref[parity], cells_ref[...])
    along = wave_x * spectrum[:, :512] + wave_z * spectrum[:, 1024:]
    both = jnp.concatenate([along, spectrum[:, 512:1024]], axis=0)
    parts = (
        dot(both[:, :256] + both[:, 256:], even_ref[...]),
        dot(both[:, :256] - both[:, 256:], odd_ref[...]),
    )
    back = []
    for which in range(2):
        wave_y = wave_y_ref[which : which + 1, :]
        squared = wave_x * wave_x + wave_y * wave_y + wave_z * wave_z
        anchor = squared == 0.0
        factor = jnp.where(
            anchor, 0.0, (-1.0 / (NX * NY * NZ)) / jnp.where(anchor, 1.0, squared)
        )
        potential = (parts[which][:128] + wave_y * parts[which][128:]) * factor
        stacked = jnp.concatenate([potential, wave_y * potential], axis=0)
        back.append(dot(stacked, (back_even_ref, back_odd_ref)[which][...]))
    low, high = back[0] + back[1], back[0] - back[1]
    column = lanes((128, 128)) % 16
    halo_p, halo_q = low[:128, 256:], low[128:, 256:]
    halo = jnp.where(
        column < 4,
        wave_x * halo_p,
        jnp.where(column < 8, halo_q, jnp.where(column < 12, wave_z * halo_p, 0.0)),
    )
    potential = jnp.concatenate([low[:128, :256], high[:128, :256]], axis=1)
    fields = jnp.concatenate(
        [wave_x * potential, low[128:, :256], high[128:, :256], wave_z * potential, halo], axis=1
    )
    cells = dot(back_x_ref[parity], fields)
    step = GY * ROWS_BACK
    for x6 in range(6):
        for c in range(3):
            for pair in range(4):
                col = c * 512 + pair * 128
                a = cells[x6 * 8 : x6 * 8 + 8, col : col + 128]
                b = cells[48 + x6 * 8 : 56 + x6 * 8, col : col + 128]
                at = 2 * pair * ROWS_BACK + c * 6 + x6
                send_ref[pl.ds(at, 8, stride=step), :] = jnp.where(left, a, pltpu.roll(b, 64, 1))
                send_ref[pl.ds(at + ROWS_BACK, 8, stride=step), :] = jnp.where(
                    left, pltpu.roll(a, 64, 1), b
                )
    for part in range(2):
        tiles = []
        for x in range(part * 8, part * 8 + 8):
            if x < 12:
                at = (x % 2) * 48 + (x // 2) * 8
                tiles.append(cells[at : at + 8, 1536:])
            else:
                tiles.append(jnp.zeros((8, 128), F32))
        for g, tile in enumerate(transpose_blocks(tiles)):
            send_ref[pl.ds(g * ROWS_BACK + 18 + part, 8, stride=step), :] = tile


def macroscopic(density, momentum, force):
    inverse = 1.0 / density
    vel = [(momentum[k] + 0.5 * force[k]) * inverse for k in range(3)]
    u_square = vel[0] * vel[0] + vel[1] * vel[1] + vel[2] * vel[2]
    u_dot_f = vel[0] * force[0] + vel[1] * force[1] + vel[2] * force[2]
    scaled = OMEGA * density
    base = scaled * (1.0 - 1.5 * u_square) - 0.5 * u_dot_f
    return vel, scaled, base


def along(lattice, vector):
    total = None
    for sign, value in zip(lattice, vector):
        if isinstance(sign, int):
            if sign == 0:
                continue
            term = value if sign == 1 else -value
        else:
            term = sign * value
        total = term if total is None else total + term
    return total


def relax_terms(lattice, vel, force, scaled, base):
    along_u = along(lattice, vel)
    along_f = along(lattice, force)
    even = base + along_u * (4.5 * scaled * along_u + 1.5 * along_f)
    odd = 3.0 * scaled * along_u + 0.5 * along_f
    return even, odd


def shift_z(tile, step, lane):
    if step == 0:
        return tile
    if step == 1:
        return jnp.where(lane % 64 == 0, pltpu.roll(tile, 65, 1), pltpu.roll(tile, 1, 1))
    return jnp.where(lane % 64 == 63, pltpu.roll(tile, 63, 1), pltpu.roll(tile, 127, 1))


def cell_kernel(
    recv_ref,
    table_ref,
    ht_ref,
    ha_ref,
    magnet_ref,
    pop_ref,
    pair_ref,
    next_ref,
    before_ref,
    after_ref,
    out_hbm,
    demag_hbm,
    out_ref,
    demag_ref,
    field_ref,
    total_ref,
    post_ref,
    side_ref,
    enter_ref,
    out_sems,
):
    lane = lanes()
    left = lane < 64
    left4 = lanes((32, 128)) < 64
    parity = lax.rem(lax.axis_index("gx"), 2)
    side_of = ((next_ref, pair_ref), (pair_ref, next_ref))

    def side(which, at, count):
        even, odd = side_of[which]
        return jnp.where(parity == 0, even[at : at + count, :], odd[at : at + count, :])

    def base(c, x):
        return (c * 12 + 2 + x) * PITCH + 8

    def both(tile):
        turned = pltpu.roll(tile, 64, 1)
        first = lanes(tile.shape) < 64
        return jnp.where(first, tile, turned), jnp.where(first, turned, tile)

    own = ((ht_ref, 0), (ht_ref, 256), (ha_ref, 0))
    for c in range(3):
        ref, at = own[c]
        for pair in range(32):
            for odd, tile in enumerate(both(ref[at + pair * 8 : at + pair * 8 + 8, :])):
                total_ref[pl.ds(base(c, 0) + 2 * pair + odd, 8, stride=PITCH), :] = tile
        for edge_ref, y in ((before_ref, -2), (after_ref, 64)):
            for odd, tile in enumerate(both(edge_ref[72 + c * 8 : 80 + c * 8, :])):
                total_ref[pl.ds(base(c, 0) + y + odd, 8, stride=PITCH), :] = tile
        for which, near, far in ((0, -1, -2), (1, 8, 9)):
            for x, k, corner in ((near, 9 + c, 9 + c), (far, 12 + c, 32 + c)):
                for odd, tile in enumerate(both(side(which, k * 32, 32))):
                    total_ref[pl.ds(base(c, x) + odd, 32, stride=2), :] = tile
                after = 16 if x == near else 8
                for y, at in ((-2, CORNER + corner), (64, CORNER + corner + after)):
                    for odd, tile in enumerate(both(side(which, at, 1))):
                        at_row = base(c, x) + y + odd
                        total_ref[at_row : at_row + 1, :] = tile

    for row in range(ROWS_BACK):
        spectrum = recv_ref[pl.ds(row, NZ, stride=ROWS_BACK), :]
        cells = dot(spectrum, table_ref[...], (0, 0))
        if row < 18:
            field_ref[row * 128 : row * 128 + 128, :] = cells
            for half in range(2):
                c, x = row // 6, 2 * (row % 6) + half - 2
                at = base(c, x)
                total_ref[at : at + 64, :] += cells[half * 64 : half * 64 + 64, :]
        else:
            for k in range(8):
                x = (row - 18) * 8 + k - 2
                if x < 10:
                    for c in range(3):
                        at, src = base(c, x), k * 16 + c * 4
                        total_ref[at - 2 : at, :] += cells[src : src + 2, :]
                        total_ref[at + 64 : at + 66, :] += cells[src + 2 : src + 4, :]

    def forces(magnet, read, first):
        force = []
        for c in range(3):
            d_x = jnp.where(first, *read(c, 1, 0)) - jnp.where(first, *read(c, -1, 0))
            d_y = jnp.where(first, *read(c, 0, 1)) - jnp.where(first, *read(c, 0, -1))
            a, b = read(c, 0, 0)
            d_z = jnp.where(first, pltpu.roll(a, 127, 1), pltpu.roll(b, 127, 1)) - jnp.where(
                first, pltpu.roll(a, 1, 1), pltpu.roll(b, 1, 1)
            )
            force.append(0.025 * (magnet[0] * d_x + magnet[1] * d_y + magnet[2] * d_z))
        return force

    def column(c, x, y):
        return total_ref[pl.ds(base(c, x) + y, 8, stride=PITCH), :]

    sign = jnp.where(left, -1.0, 1.0)
    values = [
        jnp.where(left, after_ref[k * 8 : k * 8 + 8, :], before_ref[k * 8 : k * 8 + 8, :])
        for k in range(12)
    ]
    force = forces(
        langevin(*values[9:]),
        lambda c, dx, dy: (column(c, dx, 64 + dy), column(c, dx, dy - 1)),
        left,
    )
    vel, scaled, rest = macroscopic(values[5], values[6:9], force)
    for slot, (cx, cz, up, down) in enumerate(Y_FACE):
        even, odd = relax_terms((cx, sign, cz), vel, force, scaled, rest)
        post = shift_z((1.0 - OMEGA) * values[slot] + WEIGHTS[up] * (even + odd), cz, lane)
        post_ref[up, 0] = post
        post_ref[down, 33] = post

    row = lax.broadcasted_iota(jnp.int32, (8, 128), 0)
    upper = row == 7

    def edge_rows(k_low, k_high):
        pair = []
        for which, k in ((0, k_low), (1, k_high)):
            value = jnp.where(
                left[:1], side(which, CORNER + 16 + k, 1), side(which, CORNER + k, 1)
            )
            pair.append(jnp.broadcast_to(value, (8, 128)))
        return jnp.where(upper, pair[1], pair[0])

    def corner(c, dx, y):
        return jnp.where(upper, column(c, 1 + dx, y), column(c, dx - 1, y))

    force = forces(
        langevin(*[edge_rows(k, k) for k in (9, 10, 11)]),
        lambda c, dx, dy: (corner(c, dx, 64 + dy), corner(c, dx, dy - 1)),
        left,
    )
    vel, scaled, rest = macroscopic(edge_rows(5, 5), [edge_rows(k, k) for k in (6, 7, 8)], force)
    even, odd = relax_terms((jnp.where(upper, -1.0, 1.0), sign, 0), vel, force, scaled, rest)
    edges = (1.0 - OMEGA) * edge_rows(1, 2) + WEIGHTS[7] * (even + odd)

    for which, x, step in ((0, -1, 1), (1, 8, -1)):

        def read(c, dx, dy):
            at = base(c, x + dx) + dy
            return (
                total_ref[pl.ds(at, 32, stride=2), :],
                total_ref[pl.ds(at + 1, 32, stride=2), :],
            )

        values = [side(which, k * 32, 32) for k in range(12)]
        force = forces(langevin(*values[9:]), read, left4)
        vel, scaled, rest = macroscopic(values[5], values[6:9], force)
        at_edge = 7 * which
        lane4 = lanes((32, 128))
        for slot, (cy, cz, up, down) in enumerate(X_FACE):
            even, odd = relax_terms((step, cy, cz), vel, force, scaled, rest)
            post = shift_z((1.0 - OMEGA) * values[slot] + WEIGHTS[up] * (even + odd), cz, lane4)
            if cy != 0:
                side_ref[8:40, :] = post
                if cy == 1:
                    side_ref[7:8, :] = edges[at_edge : at_edge + 1, :]
                    post = jnp.where(left4, post, side_ref[7:39, :])
                else:
                    side_ref[40:41, :] = edges[at_edge : at_edge + 1, :]
                    post = jnp.where(left4, side_ref[9:41, :], post)
                post = pltpu.roll(post, 64, 1)
            enter_ref[which, slot] = post

    def collide(pair, carry):
        ya = 2 * pair
        at = pl.multiple_of(pair * 8, 8)
        for c in range(3):
            src = (c * 12 + 2) * 64 + ya
            demag_ref[pl.ds(c * 256 + at, 8), :] = jnp.where(
                left,
                field_ref[pl.ds(src, 8, stride=64), :],
                field_ref[pl.ds(src + 1, 8, stride=64), :],
            )
        force = forces(
            [magnet_ref[pl.ds(c * 256 + at, 8), :] for c in range(3)],
            lambda c, dx, dy: (column(c, dx, ya + dy), column(c, dx, ya + 1 + dy)),
            left,
        )
        popul = [pop_ref[n, pl.ds(at, 8), :] for n in range(19)]
        density, momentum = moments_of(popul)
        vel, scaled, rest = macroscopic(density, momentum, force)
        post_ref[0, 1 + pair] = (1.0 - OMEGA) * popul[0] + WEIGHTS[0] * rest
        for n in range(1, 19, 2):
            even, odd = relax_terms(VELOCITIES[n], vel, force, scaled, rest)
            for number, value in ((n, even + odd), (n + 1, even - odd)):
                post = (1.0 - OMEGA) * popul[number] + WEIGHTS[n] * value
                post_ref[number, 1 + pair] = shift_z(post, VELOCITIES[number][2], lane)
        return carry

    lax.fori_loop(0, 32, collide, 0, unroll=4)
    sent = start((demag_ref, demag_hbm, out_sems.at[4]))

    def stream(pair, carry):
        at = pl.multiple_of(pair * 8, 8)
        for n in range(19):
            cx, cy, _ = VELOCITIES[n]
            tile = post_ref[n, 1 + pair]
            if cy == 1:
                tile = pltpu.roll(jnp.where(left, tile, post_ref[n, pair]), 64, 1)
            elif cy == -1:
                tile = pltpu.roll(jnp.where(left, post_ref[n, 2 + pair], tile), 64, 1)
            if cx != 0:
                enters = enter_ref[0 if cx == 1 else 1, X_SLOT[n], pl.ds(pair, 1), :]
                tile = jnp.where(
                    row == (0 if cx == 1 else 7),
                    jnp.broadcast_to(enters, (8, 128)),
                    pltpu.roll(tile, 1 if cx == 1 else 7, 0),
                )
            out_ref[n, pl.ds(at, 8), :] = tile
        return carry

    for part in range(4):
        lax.fori_loop(8 * part, 8 * part + 8, stream, 0, unroll=4)
        rows = pl.ds(64 * part, 64)
        sent += start((out_ref.at[:, rows], out_hbm.at[:, rows], out_sems.at[part]))
    for copy in sent:
        copy.wait()


HBM = pl.BlockSpec(memory_space=pltpu.HBM)
ANY = pl.BlockSpec(memory_space=pl.ANY)
VMEM = pl.BlockSpec(memory_space=pltpu.VMEM)


def call(kernel, ins, outs, scratch, sems, flops, moved, vmem=60):
    return pl.pallas_call(
        kernel,
        out_shape=[jax.ShapeDtypeStruct(shape, F32) for shape, _ in outs],
        in_specs=ins,
        out_specs=[spec for _, spec in outs],
        scratch_shapes=[pltpu.VMEM(shape, F32) for shape in scratch]
        + [pltpu.SemaphoreType.DMA((count,)) for count in sems],
        compiler_params=pltpu.CompilerParams(vmem_limit_bytes=vmem * 1024 * 1024),
        cost_estimate=pl.CostEstimate(flops=flops, bytes_accessed=moved, transcendentals=0),
    )


def ring(values, axis, step):
    size = lax.axis_size(axis)
    return lax.ppermute(values, axis, [(i, (i + step) % size) for i in range(size)])


GROUPS = [[(2 * m + core) * GY + g for m in range(8) for g in range(GY)] for core in range(2)]


def exchange(rows, count):
    blocks = rows.reshape(64, 1, count * 128)
    blocks = lax.all_to_all(
        blocks, ("gx", "gy"), 0, 0, axis_index_groups=GROUPS, tiled=True
    )
    return blocks.reshape(64 * count, 128)


def as_tiles(values):
    return values.reshape(-1, 8, 32, 128).transpose(0, 2, 1, 3)


def from_rows(rows):
    return rows.reshape(-1, 32, 8, 128).transpose(0, 2, 1, 3).reshape(-1, 8, 4096)


def on_device(populations, h_axial, h_transverse):
    t = tables()
    pop_tiles = as_tiles(populations)
    pop_rows = pop_tiles.reshape(19 * 256, 128)
    ht_rows = as_tiles(h_transverse).reshape(512, 128)
    ha_rows = as_tiles(h_axial).reshape(256, 128)
    rows, up, down = call(
        first_kernel,
        [HBM] * 4,
        [((64 * ROWS_FWD, 128), VMEM), ((96, 128), VMEM), ((96, 128), VMEM)],
        [(512, 128), (256, 128), (19, 8, 128), (19, 8, 128), (64, 128), (1536, 128)],
        [5],
        30_000_000,
        1_800_000,
    )(ht_rows, ha_rows, pop_tiles, t["fwd_z"])
    own = exchange(rows, ROWS_FWD)
    before = ring(up, "gy", 1)
    after = ring(down, "gy", -1)
    to_pair, to_next, magnet = call(
        face_kernel,
        [HBM, HBM, HBM, VMEM, VMEM],
        [((FACE_ROWS, 128), VMEM), ((FACE_ROWS, 128), VMEM), ((768, 128), VMEM)],
        [(19 * 256, 128), (512, 128), (256, 128)],
        [3],
        1_000_000,
        4_000_000,
    )(pop_rows, ht_rows, ha_rows, before, after)
    own, to_pair, to_next = lax.optimization_barrier((own, to_pair, to_next))
    pair = lax.ppermute(to_pair, "gx", [(i, i ^ 1) for i in range(GX)])
    beyond = lax.ppermute(to_next, "gx", [(i, ((i + 1) ^ 1) - 1 & 15) for i in range(GX)])
    other = lax.ppermute(own, "gx", [(i, i ^ 1) for i in range(GX)])
    (rows,) = call(
        plane_kernel,
        [VMEM] * 11,
        [((64 * ROWS_BACK, 128), VMEM)],
        [(128, 1536)],
        [],
        400_000_000,
        3_000_000,
    )(
        own,
        other,
        t["fwd_x"],
        t["back_x"],
        t["even"],
        t["odd"],
        t["back_even"],
        t["back_odd"],
        t["wave_x"],
        t["wave_y"],
        t["wave_z"],
    )
    rows, pair, beyond = lax.optimization_barrier((rows, pair, beyond))
    recv = exchange(rows, ROWS_BACK)
    result, demag = call(
        cell_kernel,
        [VMEM] * 10,
        [((19, 256, 128), HBM), ((3 * 256, 128), HBM)],
        [
            (19, 256, 128),
            (768, 128),
            (18 * 128, 128),
            (36 * PITCH, 128),
            (19, 34, 8, 128),
            (48, 128),
            (2, 5, 32, 128),
        ],
        [5],
        60_000_000,
        8_000_000,
        24,
    )(
        recv,
        t["back_z"],
        ht_rows,
        ha_rows,
        magnet,
        pop_rows.reshape(19, 256, 128),
        pair,
        beyond,
        before,
        after,
    )
    return from_rows(result), from_rows(demag)


def solution(mesh):
    placed = (P(None, "gx", "gy"), P("gx", "gy"), P(None, "gx", "gy"))
    return jax.shard_map(
        on_device,
        mesh=mesh,
        in_specs=placed,
        out_specs=(P(None, "gx", "gy"), P(None, "gx", "gy")),
        check_vma=False,
    )
```

```python
import functools

import jax
import jax.numpy as jnp
import ml_dtypes
import numpy as np
from jax import lax
from jax.experimental import pallas as pl
from jax.experimental.pallas import tpu as pltpu
from jax.sharding import PartitionSpec as P

NX, NY, NZ = 128, 512, 64
GX, GY = 16, 8
VELOCITIES = (
    (0, 0, 0),
    (1, 0, 0),
    (-1, 0, 0),
    (0, 1, 0),
    (0, -1, 0),
    (0, 0, 1),
    (0, 0, -1),
    (1, 1, 0),
    (-1, -1, 0),
    (1, -1, 0),
    (-1, 1, 0),
    (1, 0, 1),
    (-1, 0, -1),
    (1, 0, -1),
    (-1, 0, 1),
    (0, 1, 1),
    (0, -1, -1),
    (0, 1, -1),
    (0, -1, 1),
)
WEIGHTS = (1.0 / 3.0,) + (1.0 / 18.0,) * 6 + (1.0 / 36.0,) * 12
OMEGA = 1.0 / 0.6
F32 = jnp.float32

X_FACE = ((0, 0, 1, 2), (1, 0, 7, 10), (-1, 0, 9, 8), (0, 1, 11, 14), (0, -1, 13, 12))
Y_FACE = ((0, 0, 3, 4), (1, 0, 7, 9), (-1, 0, 10, 8), (0, 1, 15, 18), (0, -1, 17, 16))
X_SLOT = {n: s for s, row in enumerate(X_FACE) for n in row[2:]}

ROWS_FWD = 12
ROWS_BACK = 20
CORNER = 480
FACE_ROWS = CORNER + 48
PITCH = 80


def cas(rows, cols, count):
    angle = 2.0 * np.pi * ((rows[:, None] * cols[None, :]) % count) / count
    return np.cos(angle) + np.sin(angle)


def wave(index, count):
    return 2.0 * np.sin(np.pi * index / count)


@functools.lru_cache(maxsize=None)
def tables():
    every_x, every_z = np.arange(NX), np.arange(NZ)
    half = np.arange(NY // 2)
    out = {}
    fwd_z = np.zeros((NZ, 128))
    fwd_z[:, :NZ] = cas(every_z, every_z, NZ)
    out["fwd_z"] = fwd_z
    out["back_z"] = np.tile(cas(every_z, every_z, NZ), (1, 2))
    fwd_x, back_x = [], []
    m = np.arange(8)
    for parity in range(2):
        order = []
        for side in (parity, 1 - parity):
            for x2 in range(2):
                for x4 in range(4):
                    order += list(8 * (2 * m + side) + 2 * x4 + x2)
        fwd_x.append(cas(every_x, np.array(order), NX))
        order = []
        for x2 in range(2):
            for x6 in range(6):
                order += list((8 * (2 * m + parity) - 2 + 2 * x6 + x2) % NX)
        back_x.append(cas(np.array(order), every_x, NX))
    out["fwd_x"] = np.stack(fwd_x)
    out["back_x"] = np.stack(back_x)
    even, odd = 2 * half, 2 * half + 1
    halo = np.array(
        [
            (64 * g + (-2, -1, 64, 65)[k]) % NY
            for g in range(GY)
            for c in range(4)
            for k in range(4)
        ]
    )
    out["even"] = cas(half, even, NY)
    out["odd"] = cas(half, odd, NY)
    out["back_even"] = np.concatenate([cas(even, half, NY), cas(even, halo, NY)], axis=1)
    out["back_odd"] = np.concatenate([cas(odd, half, NY), cas(odd, halo, NY)], axis=1)
    out["wave_x"] = np.repeat(wave(every_x, NX)[:, None], 128, axis=1)
    out["wave_y"] = np.stack([wave(even, NY), wave(odd, NY)])
    out["wave_z"] = np.repeat(wave(every_z, NZ)[:, None], 128, axis=1)
    out = {name: np.asarray(value, np.float32) for name, value in out.items()}
    for name, axis in SPLIT_TABLES.items():
        high = out[name].astype(ml_dtypes.bfloat16)
        low = (out[name] - high.astype(np.float32)).astype(ml_dtypes.bfloat16)
        out[name] = np.concatenate([high, low, high], axis=axis)
    return out


SPLIT_TABLES = {
    "fwd_z": 1,
    "back_z": 0,
    "fwd_x": 2,
    "back_x": 2,
    "even": 0,
    "odd": 0,
    "back_even": 0,
    "back_odd": 0,
}


def terms(values, axis):
    high = values.astype(jnp.bfloat16)
    low = (values - high.astype(F32)).astype(jnp.bfloat16)
    return jnp.concatenate([high, high, low], axis=axis)


def product(a, b, dims):
    return lax.dot_general(a, b, (((dims[0],), (dims[1],)), ((), ())), preferred_element_type=F32)


def apply_left(table, values, axis=0):
    return product(table, terms(values, axis), (1, axis))


def apply_right(values, table, axis=1):
    return product(terms(values, axis), table, (axis, 0))


def langevin(hx, hy, hz):
    magnitude = jnp.sqrt(hx * hx + hy * hy + hz * hz)
    argument = 1.5 * magnitude
    decay = jnp.exp(-2.0 * argument)
    scale = ((1.0 + decay) / (1.0 - decay) - 1.0 / argument) / magnitude
    return hx * scale, hy * scale, hz * scale


def lanes(shape=(8, 128)):
    return lax.broadcasted_iota(jnp.int32, shape, len(shape) - 1)


def moments_of(popul):
    density = popul[0]
    for n in range(1, 19):
        density = density + popul[n]
    momentum = []
    for k in range(3):
        total = None
        for n in range(1, 19):
            if VELOCITIES[n][k] == 1:
                total = popul[n] if total is None else total + popul[n]
            elif VELOCITIES[n][k] == -1:
                total = total - popul[n]
        momentum.append(total)
    return density, momentum


def start(*copies):
    started = [pltpu.make_async_copy(*copy) for copy in copies]
    for copy in started:
        copy.start()
    return started


def edge_kernel(pop_hbm, ht_hbm, ha_hbm, up_ref, down_ref, pop_ref, sems):
    copies = start(
        (pop_hbm.at[:, 31], pop_ref.at[0], sems.at[0]),
        (pop_hbm.at[:, 0], pop_ref.at[1], sems.at[1]),
        (ht_hbm.at[pl.ds(31 * 8, 8)], up_ref.at[pl.ds(72, 8)], sems.at[2]),
        (ht_hbm.at[pl.ds(256 + 31 * 8, 8)], up_ref.at[pl.ds(80, 8)], sems.at[3]),
        (ha_hbm.at[pl.ds(31 * 8, 8)], up_ref.at[pl.ds(88, 8)], sems.at[4]),
        (ht_hbm.at[pl.ds(0, 8)], down_ref.at[pl.ds(72, 8)], sems.at[5]),
        (ht_hbm.at[pl.ds(256, 8)], down_ref.at[pl.ds(80, 8)], sems.at[6]),
        (ha_hbm.at[pl.ds(0, 8)], down_ref.at[pl.ds(88, 8)], sems.at[7]),
    )
    for copy in copies:
        copy.wait()
    for side, (out_ref, which) in enumerate(((up_ref, 2), (down_ref, 3))):
        popul = [pop_ref[side, n] for n in range(19)]
        density, momentum = moments_of(popul)
        for k, tile in enumerate([popul[face[which]] for face in Y_FACE] + [density] + momentum):
            out_ref[k * 8 : k * 8 + 8, :] = tile


def first_kernel(ht_ref, ha_ref, table_ref, send_ref, rows_ref):
    magnet = langevin(ht_ref[:256, :], ht_ref[256:, :], ha_ref[...])
    for c in range(3):
        for pair in range(32):
            tile = magnet[c][pair * 8 : pair * 8 + 8, :]
            rows_ref[pl.ds(c * 512 + 2 * pair, 8, stride=64), :] = tile
            rows_ref[pl.ds(c * 512 + 2 * pair + 1, 8, stride=64), :] = pltpu.roll(tile, 64, 1)
    spectrum = apply_left(table_ref[...], rows_ref[...], 1)
    for row in range(ROWS_FWD):
        send_ref[pl.ds(row, NZ, stride=ROWS_FWD), :] = spectrum[:, row * 128 : row * 128 + 128]


def face_kernel(
    pop_ref, ht_ref, ha_ref, before_ref, after_ref, pair_ref, next_ref, magnet_ref
):
    magnet = langevin(ht_ref[:256, :], ht_ref[256:, :], ha_ref[...])
    for c in range(3):
        magnet_ref[c * 256 : c * 256 + 256, :] = magnet[c]
    parity = lax.rem(lax.axis_index("gx"), 2)
    for out_ref, up in ((pair_ref, parity == 0), (next_ref, parity == 1)):
        face = jnp.where(up, 7, 0)
        second = jnp.where(up, 6, 1)

        def line(ref, at):
            return ref[pl.ds(at, 32, stride=8), :]

        popul = [line(pop_ref, n * 256 + face) for n in range(19)]
        density, momentum = moments_of(popul)
        lines = [jnp.where(up, popul[f[2]], popul[f[3]]) for f in X_FACE] + [density] + momentum
        for x in (face, second):
            lines += [line(ht_ref, x), line(ht_ref, 256 + x), line(ha_ref, x)]
        for k, value in enumerate(lines):
            out_ref[k * 32 : k * 32 + 32, :] = value
        for ref, at in ((before_ref, CORNER), (after_ref, CORNER + 16)):
            out_ref[at : at + 16, :] = jnp.zeros((16, 128), F32)
            out_ref[at : at + 12, :] = ref[pl.ds(face, 12, stride=8), :]
        for ref, at in ((before_ref, CORNER + 32), (after_ref, CORNER + 40)):
            out_ref[at : at + 8, :] = jnp.zeros((8, 128), F32)
            out_ref[at : at + 3, :] = ref[pl.ds(72 + second, 3, stride=8), :]


def transpose_blocks(tiles):
    block = lanes() // 16
    for bit in (1, 2, 4):
        low = (block & bit) == 0
        out = list(tiles)
        for i in range(8):
            if i & bit == 0:
                a, b = tiles[i], tiles[i | bit]
                out[i] = jnp.where(low, a, pltpu.roll(b, 16 * bit, 1))
                out[i | bit] = jnp.where(low, pltpu.roll(a, 128 - 16 * bit, 1), b)
        tiles = out
    return tiles


def plane_kernel(
    own_ref,
    other_ref,
    fwd_x_ref,
    back_x_ref,
    even_ref,
    odd_ref,
    back_even_ref,
    back_odd_ref,
    wave_x_ref,
    wave_y_ref,
    wave_z_ref,
    send_ref,
    cells_ref,
):
    row = lax.axis_index("gx")
    parity = lax.rem(row, 2)
    index_z = (row // 2) * GY + lax.axis_index("gy")
    left = lanes() < 64
    for side, ref in enumerate((own_ref, other_ref)):
        for c in range(3):
            for pair in range(4):
                for x4 in range(4):
                    start = 2 * pair * ROWS_FWD + c * 4 + x4
                    a = ref[pl.ds(start, 8, stride=GY * ROWS_FWD), :]
                    b = ref[pl.ds(start + ROWS_FWD, 8, stride=GY * ROWS_FWD), :]
                    at = side * 64 + x4 * 8
                    col = c * 512 + pair * 128
                    cells_ref[at : at + 8, col : col + 128] = jnp.where(
                        left, a, pltpu.roll(b, 64, 1)
                    )
                    cells_ref[at + 32 : at + 40, col : col + 128] = jnp.where(
                        left, pltpu.roll(a, 64, 1), b
                    )
    wave_x = wave_x_ref[:, 0:1]
    wave_z = wave_z_ref[pl.ds(index_z, 1), 0:1]
    spectrum = apply_left(fwd_x_ref[parity], cells_ref[...])
    along = wave_x * spectrum[:, :512] + wave_z * spectrum[:, 1024:]
    both = jnp.concatenate([along, spectrum[:, 512:1024]], axis=0)
    parts = (
        apply_right(both[:, :256] + both[:, 256:], even_ref[...]),
        apply_right(both[:, :256] - both[:, 256:], odd_ref[...]),
    )
    back = []
    for which in range(2):
        wave_y = wave_y_ref[which : which + 1, :]
        squared = wave_x * wave_x + wave_y * wave_y + wave_z * wave_z
        anchor = squared == 0.0
        factor = jnp.where(
            anchor, 0.0, (-1.0 / (NX * NY * NZ)) / jnp.where(anchor, 1.0, squared)
        )
        potential = (parts[which][:128] + wave_y * parts[which][128:]) * factor
        stacked = jnp.concatenate([potential, wave_y * potential], axis=0)
        back.append(apply_right(stacked, (back_even_ref, back_odd_ref)[which][...]))
    low, high = back[0] + back[1], back[0] - back[1]
    column = lanes((128, 128)) % 16
    halo_p, halo_q = low[:128, 256:], low[128:, 256:]
    halo = jnp.where(
        column < 4,
        wave_x * halo_p,
        jnp.where(column < 8, halo_q, jnp.where(column < 12, wave_z * halo_p, 0.0)),
    )
    potential = jnp.concatenate([low[:128, :256], high[:128, :256]], axis=1)
    fields = jnp.concatenate(
        [wave_x * potential, low[128:, :256], high[128:, :256], wave_z * potential, halo], axis=1
    )
    cells = apply_left(back_x_ref[parity], fields)
    step = GY * ROWS_BACK
    for x6 in range(6):
        for c in range(3):
            for pair in range(4):
                col = c * 512 + pair * 128
                a = cells[x6 * 8 : x6 * 8 + 8, col : col + 128]
                b = cells[48 + x6 * 8 : 56 + x6 * 8, col : col + 128]
                at = 2 * pair * ROWS_BACK + c * 6 + x6
                send_ref[pl.ds(at, 8, stride=step), :] = jnp.where(left, a, pltpu.roll(b, 64, 1))
                send_ref[pl.ds(at + ROWS_BACK, 8, stride=step), :] = jnp.where(
                    left, pltpu.roll(a, 64, 1), b
                )
    for part in range(2):
        tiles = []
        for x in range(part * 8, part * 8 + 8):
            if x < 12:
                at = (x % 2) * 48 + (x // 2) * 8
                tiles.append(cells[at : at + 8, 1536:])
            else:
                tiles.append(jnp.zeros((8, 128), F32))
        for g, tile in enumerate(transpose_blocks(tiles)):
            send_ref[pl.ds(g * ROWS_BACK + 18 + part, 8, stride=step), :] = tile


def macroscopic(density, momentum, force):
    inverse = 1.0 / density
    vel = [(momentum[k] + 0.5 * force[k]) * inverse for k in range(3)]
    u_square = vel[0] * vel[0] + vel[1] * vel[1] + vel[2] * vel[2]
    u_dot_f = vel[0] * force[0] + vel[1] * force[1] + vel[2] * force[2]
    scaled = OMEGA * density
    base = scaled * (1.0 - 1.5 * u_square) - 0.5 * u_dot_f
    return vel, scaled, base


def along(lattice, vector):
    total = None
    for sign, value in zip(lattice, vector):
        if isinstance(sign, int):
            if sign == 0:
                continue
            term = value if sign == 1 else -value
        else:
            term = sign * value
        total = term if total is None else total + term
    return total


def relax_terms(lattice, vel, force, scaled, base):
    along_u = along(lattice, vel)
    along_f = along(lattice, force)
    even = base + along_u * (4.5 * scaled * along_u + 1.5 * along_f)
    odd = 3.0 * scaled * along_u + 0.5 * along_f
    return even, odd


def shift_z(tile, step, lane):
    if step == 0:
        return tile
    if step == 1:
        return jnp.where(lane % 64 == 0, pltpu.roll(tile, 65, 1), pltpu.roll(tile, 1, 1))
    return jnp.where(lane % 64 == 63, pltpu.roll(tile, 63, 1), pltpu.roll(tile, 127, 1))


def cell_kernel(
    recv_ref,
    table_ref,
    ht_ref,
    ha_ref,
    magnet_ref,
    pop_ref,
    pair_ref,
    next_ref,
    before_ref,
    after_ref,
    out_hbm,
    demag_hbm,
    out_ref,
    demag_ref,
    field_ref,
    total_ref,
    post_ref,
    side_ref,
    enter_ref,
    out_sems,
):
    lane = lanes()
    left = lane < 64
    left4 = lanes((32, 128)) < 64
    parity = lax.rem(lax.axis_index("gx"), 2)
    side_of = ((next_ref, pair_ref), (pair_ref, next_ref))

    def side(which, at, count):
        even, odd = side_of[which]
        return jnp.where(parity == 0, even[at : at + count, :], odd[at : at + count, :])

    def base(c, x):
        return (c * 12 + 2 + x) * PITCH + 8

    def both(tile):
        turned = pltpu.roll(tile, 64, 1)
        first = lanes(tile.shape) < 64
        return jnp.where(first, tile, turned), jnp.where(first, turned, tile)

    own = ((ht_ref, 0), (ht_ref, 256), (ha_ref, 0))
    for c in range(3):
        ref, at = own[c]
        for pair in range(32):
            for odd, tile in enumerate(both(ref[at + pair * 8 : at + pair * 8 + 8, :])):
                total_ref[pl.ds(base(c, 0) + 2 * pair + odd, 8, stride=PITCH), :] = tile
        for edge_ref, y in ((before_ref, -2), (after_ref, 64)):
            for odd, tile in enumerate(both(edge_ref[72 + c * 8 : 80 + c * 8, :])):
                total_ref[pl.ds(base(c, 0) + y + odd, 8, stride=PITCH), :] = tile
        for which, near, far in ((0, -1, -2), (1, 8, 9)):
            for x, k, corner in ((near, 9 + c, 9 + c), (far, 12 + c, 32 + c)):
                for odd, tile in enumerate(both(side(which, k * 32, 32))):
                    total_ref[pl.ds(base(c, x) + odd, 32, stride=2), :] = tile
                after = 16 if x == near else 8
                for y, at in ((-2, CORNER + corner), (64, CORNER + corner + after)):
                    for odd, tile in enumerate(both(side(which, at, 1))):
                        at_row = base(c, x) + y + odd
                        total_ref[at_row : at_row + 1, :] = tile

    for row in range(ROWS_BACK):
        spectrum = recv_ref[pl.ds(row, NZ, stride=ROWS_BACK), :]
        cells = apply_right(spectrum, table_ref[...], 0)
        if row < 18:
            field_ref[row * 128 : row * 128 + 128, :] = cells
            for half in range(2):
                c, x = row // 6, 2 * (row % 6) + half - 2
                at = base(c, x)
                total_ref[at : at + 64, :] += cells[half * 64 : half * 64 + 64, :]
        else:
            for k in range(8):
                x = (row - 18) * 8 + k - 2
                if x < 10:
                    for c in range(3):
                        at, src = base(c, x), k * 16 + c * 4
                        total_ref[at - 2 : at, :] += cells[src : src + 2, :]
                        total_ref[at + 64 : at + 66, :] += cells[src + 2 : src + 4, :]

    def forces(magnet, read, first):
        force = []
        for c in range(3):
            d_x = jnp.where(first, *read(c, 1, 0)) - jnp.where(first, *read(c, -1, 0))
            d_y = jnp.where(first, *read(c, 0, 1)) - jnp.where(first, *read(c, 0, -1))
            a, b = read(c, 0, 0)
            d_z = jnp.where(first, pltpu.roll(a, 127, 1), pltpu.roll(b, 127, 1)) - jnp.where(
                first, pltpu.roll(a, 1, 1), pltpu.roll(b, 1, 1)
            )
            force.append(0.025 * (magnet[0] * d_x + magnet[1] * d_y + magnet[2] * d_z))
        return force

    def column(c, x, y):
        return total_ref[pl.ds(base(c, x) + y, 8, stride=PITCH), :]

    sign = jnp.where(left, -1.0, 1.0)
    values = [
        jnp.where(left, after_ref[k * 8 : k * 8 + 8, :], before_ref[k * 8 : k * 8 + 8, :])
        for k in range(12)
    ]
    force = forces(
        langevin(*values[9:]),
        lambda c, dx, dy: (column(c, dx, 64 + dy), column(c, dx, dy - 1)),
        left,
    )
    vel, scaled, rest = macroscopic(values[5], values[6:9], force)
    for slot, (cx, cz, up, down) in enumerate(Y_FACE):
        even, odd = relax_terms((cx, sign, cz), vel, force, scaled, rest)
        post = shift_z((1.0 - OMEGA) * values[slot] + WEIGHTS[up] * (even + odd), cz, lane)
        post_ref[up, 0] = post
        post_ref[down, 33] = post

    row = lax.broadcasted_iota(jnp.int32, (8, 128), 0)
    upper = row == 7

    def edge_rows(k_low, k_high):
        pair = []
        for which, k in ((0, k_low), (1, k_high)):
            value = jnp.where(
                left[:1], side(which, CORNER + 16 + k, 1), side(which, CORNER + k, 1)
            )
            pair.append(jnp.broadcast_to(value, (8, 128)))
        return jnp.where(upper, pair[1], pair[0])

    def corner(c, dx, y):
        return jnp.where(upper, column(c, 1 + dx, y), column(c, dx - 1, y))

    force = forces(
        langevin(*[edge_rows(k, k) for k in (9, 10, 11)]),
        lambda c, dx, dy: (corner(c, dx, 64 + dy), corner(c, dx, dy - 1)),
        left,
    )
    vel, scaled, rest = macroscopic(edge_rows(5, 5), [edge_rows(k, k) for k in (6, 7, 8)], force)
    even, odd = relax_terms((jnp.where(upper, -1.0, 1.0), sign, 0), vel, force, scaled, rest)
    edges = (1.0 - OMEGA) * edge_rows(1, 2) + WEIGHTS[7] * (even + odd)

    for which, x, step in ((0, -1, 1), (1, 8, -1)):

        def read(c, dx, dy):
            at = base(c, x + dx) + dy
            return (
                total_ref[pl.ds(at, 32, stride=2), :],
                total_ref[pl.ds(at + 1, 32, stride=2), :],
            )

        values = [side(which, k * 32, 32) for k in range(12)]
        force = forces(langevin(*values[9:]), read, left4)
        vel, scaled, rest = macroscopic(values[5], values[6:9], force)
        at_edge = 7 * which
        lane4 = lanes((32, 128))
        for slot, (cy, cz, up, down) in enumerate(X_FACE):
            even, odd = relax_terms((step, cy, cz), vel, force, scaled, rest)
            post = shift_z((1.0 - OMEGA) * values[slot] + WEIGHTS[up] * (even + odd), cz, lane4)
            if cy != 0:
                side_ref[8:40, :] = post
                if cy == 1:
                    side_ref[7:8, :] = edges[at_edge : at_edge + 1, :]
                    post = jnp.where(left4, post, side_ref[7:39, :])
                else:
                    side_ref[40:41, :] = edges[at_edge : at_edge + 1, :]
                    post = jnp.where(left4, side_ref[9:41, :], post)
                post = pltpu.roll(post, 64, 1)
            enter_ref[which, slot] = post

    def collide(pair, carry):
        ya = 2 * pair
        at = pl.multiple_of(pair * 8, 8)
        for c in range(3):
            src = (c * 12 + 2) * 64 + ya
            demag_ref[pl.ds(c * 256 + at, 8), :] = jnp.where(
                left,
                field_ref[pl.ds(src, 8, stride=64), :],
                field_ref[pl.ds(src + 1, 8, stride=64), :],
            )
        force = forces(
            [magnet_ref[pl.ds(c * 256 + at, 8), :] for c in range(3)],
            lambda c, dx, dy: (column(c, dx, ya + dy), column(c, dx, ya + 1 + dy)),
            left,
        )
        popul = [pop_ref[n, pl.ds(at, 8), :] for n in range(19)]
        density, momentum = moments_of(popul)
        vel, scaled, rest = macroscopic(density, momentum, force)
        post_ref[0, 1 + pair] = (1.0 - OMEGA) * popul[0] + WEIGHTS[0] * rest
        for n in range(1, 19, 2):
            even, odd = relax_terms(VELOCITIES[n], vel, force, scaled, rest)
            for number, value in ((n, even + odd), (n + 1, even - odd)):
                post = (1.0 - OMEGA) * popul[number] + WEIGHTS[n] * value
                post_ref[number, 1 + pair] = shift_z(post, VELOCITIES[number][2], lane)
        return carry

    lax.fori_loop(0, 32, collide, 0, unroll=4)
    sent = start((demag_ref, demag_hbm, out_sems.at[4]))

    def stream(pair, carry):
        at = pl.multiple_of(pair * 8, 8)
        for n in range(19):
            cx, cy, _ = VELOCITIES[n]
            tile = post_ref[n, 1 + pair]
            if cy == 1:
                tile = pltpu.roll(jnp.where(left, tile, post_ref[n, pair]), 64, 1)
            elif cy == -1:
                tile = pltpu.roll(jnp.where(left, post_ref[n, 2 + pair], tile), 64, 1)
            if cx != 0:
                enters = enter_ref[0 if cx == 1 else 1, X_SLOT[n], pl.ds(pair, 1), :]
                tile = jnp.where(
                    row == (0 if cx == 1 else 7),
                    jnp.broadcast_to(enters, (8, 128)),
                    pltpu.roll(tile, 1 if cx == 1 else 7, 0),
                )
            out_ref[n, pl.ds(at, 8), :] = tile
        return carry

    for part in range(4):
        lax.fori_loop(8 * part, 8 * part + 8, stream, 0, unroll=8)
        rows = pl.ds(64 * part, 64)
        sent += start((out_ref.at[:, rows], out_hbm.at[:, rows], out_sems.at[part]))
    for copy in sent:
        copy.wait()


HBM = pl.BlockSpec(memory_space=pltpu.HBM)
ANY = pl.BlockSpec(memory_space=pl.ANY)
VMEM = pl.BlockSpec(memory_space=pltpu.VMEM)


def call(kernel, ins, outs, scratch, sems, flops, moved, vmem=60):
    return pl.pallas_call(
        kernel,
        out_shape=[jax.ShapeDtypeStruct(shape, F32) for shape, _ in outs],
        in_specs=ins,
        out_specs=[spec for _, spec in outs],
        scratch_shapes=[pltpu.VMEM(shape, F32) for shape in scratch]
        + [pltpu.SemaphoreType.DMA((count,)) for count in sems],
        compiler_params=pltpu.CompilerParams(vmem_limit_bytes=vmem * 1024 * 1024),
        cost_estimate=pl.CostEstimate(flops=flops, bytes_accessed=moved, transcendentals=0),
    )


def ring(values, axis, step):
    size = lax.axis_size(axis)
    return lax.ppermute(values, axis, [(i, (i + step) % size) for i in range(size)])


GROUPS = [[(2 * m + core) * GY + g for m in range(8) for g in range(GY)] for core in range(2)]


def exchange(rows, count):
    blocks = rows.reshape(64, 1, count * 128)
    blocks = lax.all_to_all(
        blocks, ("gx", "gy"), 0, 0, axis_index_groups=GROUPS, tiled=True
    )
    return blocks.reshape(64 * count, 128)


def as_tiles(values):
    return values.reshape(-1, 8, 32, 128).transpose(0, 2, 1, 3)


def from_rows(rows):
    return rows.reshape(-1, 32, 8, 128).transpose(0, 2, 1, 3).reshape(-1, 8, 4096)


def on_device(populations, h_axial, h_transverse):
    t = tables()
    pop_tiles = as_tiles(populations)
    pop_rows = pop_tiles.reshape(19 * 256, 128)
    ht_rows = as_tiles(h_transverse).reshape(512, 128)
    ha_rows = as_tiles(h_axial).reshape(256, 128)
    up, down = call(
        edge_kernel,
        [HBM] * 3,
        [((96, 128), VMEM), ((96, 128), VMEM)],
        [(2, 19, 8, 128)],
        [8],
        100_000,
        300_000,
    )(pop_tiles, ht_rows, ha_rows)
    before = ring(up, "gy", 1)
    after = ring(down, "gy", -1)
    (rows,) = call(
        first_kernel,
        [VMEM] * 3,
        [((64 * ROWS_FWD, 128), VMEM)],
        [(1536, 128)],
        [],
        30_000_000,
        1_800_000,
        8,
    )(ht_rows, ha_rows, t["fwd_z"])
    to_pair, to_next, magnet = call(
        face_kernel,
        [VMEM] * 5,
        [((FACE_ROWS, 128), VMEM), ((FACE_ROWS, 128), VMEM), ((768, 128), VMEM)],
        [],
        [],
        1_000_000,
        4_000_000,
        8,
    )(pop_rows, ht_rows, ha_rows, before, after)
    rows, to_pair, to_next = lax.optimization_barrier((rows, to_pair, to_next))
    own = exchange(rows, ROWS_FWD)
    other = lax.ppermute(own, "gx", [(i, i ^ 1) for i in range(GX)])
    pair = lax.ppermute(to_pair, "gx", [(i, i ^ 1) for i in range(GX)])
    beyond = lax.ppermute(to_next, "gx", [(i, ((i + 1) ^ 1) - 1 & 15) for i in range(GX)])
    (rows,) = call(
        plane_kernel,
        [VMEM] * 11,
        [((64 * ROWS_BACK, 128), VMEM)],
        [(128, 1536)],
        [],
        1_000,
        1_000,
        16,
    )(
        own,
        other,
        t["fwd_x"],
        t["back_x"],
        t["even"],
        t["odd"],
        t["back_even"],
        t["back_odd"],
        t["wave_x"],
        t["wave_y"],
        t["wave_z"],
    )
    rows, pair, beyond = lax.optimization_barrier((rows, pair, beyond))
    recv = exchange(rows, ROWS_BACK)
    result, demag = call(
        cell_kernel,
        [VMEM] * 10,
        [((19, 256, 128), HBM), ((3 * 256, 128), HBM)],
        [
            (19, 256, 128),
            (768, 128),
            (18 * 128, 128),
            (36 * PITCH, 128),
            (19, 34, 8, 128),
            (48, 128),
            (2, 5, 32, 128),
        ],
        [5],
        60_000_000,
        8_000_000,
        24,
    )(
        recv,
        t["back_z"],
        ht_rows,
        ha_rows,
        magnet,
        pop_rows.reshape(19, 256, 128),
        pair,
        beyond,
        before,
        after,
    )
    return from_rows(result), from_rows(demag)


def solution(mesh):
    placed = (P(None, "gx", "gy"), P("gx", "gy"), P(None, "gx", "gy"))
    return jax.shard_map(
        on_device,
        mesh=mesh,
        in_specs=placed,
        out_specs=(P(None, "gx", "gy"), P(None, "gx", "gy")),
        check_vma=False,
    )
```

```python
import functools

import jax
import jax.numpy as jnp
import ml_dtypes
import numpy as np
from jax import lax
from jax.experimental import pallas as pl
from jax.experimental.pallas import tpu as pltpu
from jax.sharding import PartitionSpec as P

NX, NY, NZ = 128, 512, 64
GX, GY = 16, 8
VELOCITIES = (
    (0, 0, 0),
    (1, 0, 0),
    (-1, 0, 0),
    (0, 1, 0),
    (0, -1, 0),
    (0, 0, 1),
    (0, 0, -1),
    (1, 1, 0),
    (-1, -1, 0),
    (1, -1, 0),
    (-1, 1, 0),
    (1, 0, 1),
    (-1, 0, -1),
    (1, 0, -1),
    (-1, 0, 1),
    (0, 1, 1),
    (0, -1, -1),
    (0, 1, -1),
    (0, -1, 1),
)
WEIGHTS = (1.0 / 3.0,) + (1.0 / 18.0,) * 6 + (1.0 / 36.0,) * 12
OMEGA = 1.0 / 0.6
F32 = jnp.float32

X_FACE = ((0, 0, 1, 2), (1, 0, 7, 10), (-1, 0, 9, 8), (0, 1, 11, 14), (0, -1, 13, 12))
Y_FACE = ((0, 0, 3, 4), (1, 0, 7, 9), (-1, 0, 10, 8), (0, 1, 15, 18), (0, -1, 17, 16))
X_SLOT = {n: s for s, row in enumerate(X_FACE) for n in row[2:]}

ROWS_FWD = 12
ROWS_BACK = 20
CORNER = 480
FACE_ROWS = CORNER + 48
PITCH = 69
OWN_PITCH = 65


def cas(rows, cols, count):
    angle = 2.0 * np.pi * ((rows[:, None] * cols[None, :]) % count) / count
    return np.cos(angle) + np.sin(angle)


def wave(index, count):
    return 2.0 * np.sin(np.pi * index / count)


@functools.lru_cache(maxsize=None)
def tables():
    every_x, every_z = np.arange(NX), np.arange(NZ)
    half = np.arange(NY // 2)
    out = {}
    fwd_z = np.zeros((NZ, 128))
    fwd_z[:, :NZ] = cas(every_z, every_z, NZ)
    out["fwd_z"] = fwd_z
    out["back_z"] = np.tile(cas(every_z, every_z, NZ), (1, 2))
    fwd_x, back_x = [], []
    m = np.arange(8)
    for parity in range(2):
        order = []
        for side in (parity, 1 - parity):
            for x2 in range(2):
                for x4 in range(4):
                    order += list(8 * (2 * m + side) + 2 * x4 + x2)
        fwd_x.append(cas(every_x, np.array(order), NX))
        order = []
        for x2 in range(2):
            for x6 in range(6):
                order += list((8 * (2 * m + parity) - 2 + 2 * x6 + x2) % NX)
        back_x.append(cas(np.array(order), every_x, NX))
    out["fwd_x"] = np.stack(fwd_x)
    out["back_x"] = np.stack(back_x)
    even, odd = 2 * half, 2 * half + 1
    halo = np.array(
        [
            (64 * g + (-2, -1, 64, 65)[k]) % NY
            for g in range(GY)
            for c in range(4)
            for k in range(4)
        ]
    )
    out["even"] = cas(half, even, NY)
    out["odd"] = cas(half, odd, NY)
    out["back_even"] = np.concatenate([cas(even, half, NY), cas(even, halo, NY)], axis=1)
    out["back_odd"] = np.concatenate([cas(odd, half, NY), cas(odd, halo, NY)], axis=1)
    out["wave_x"] = np.repeat(wave(every_x, NX)[:, None], 128, axis=1)
    out["wave_y"] = np.stack([wave(even, NY), wave(odd, NY)])
    out["wave_z"] = np.repeat(wave(every_z, NZ)[:, None], 128, axis=1)
    out = {name: np.asarray(value, np.float32) for name, value in out.items()}
    for name, axis in SPLIT_TABLES.items():
        high = out[name].astype(ml_dtypes.bfloat16)
        low = (out[name] - high.astype(np.float32)).astype(ml_dtypes.bfloat16)
        out[name] = np.concatenate([high, low, high], axis=axis)
    return out


SPLIT_TABLES = {
    "fwd_z": 1,
    "back_z": 0,
    "fwd_x": 2,
    "back_x": 2,
    "even": 0,
    "odd": 0,
    "back_even": 0,
    "back_odd": 0,
}


def terms(values, axis):
    high = values.astype(jnp.bfloat16)
    low = (values - high.astype(F32)).astype(jnp.bfloat16)
    return jnp.concatenate([high, high, low], axis=axis)


def product(a, b, dims):
    return lax.dot_general(a, b, (((dims[0],), (dims[1],)), ((), ())), preferred_element_type=F32)


def apply_left(table, values, axis=0):
    return product(table, terms(values, axis), (1, axis))


def apply_right(values, table, axis=1):
    return product(terms(values, axis), table, (axis, 0))


def langevin(hx, hy, hz):
    magnitude = jnp.sqrt(hx * hx + hy * hy + hz * hz)
    argument = 1.5 * magnitude
    decay = jnp.exp(-2.0 * argument)
    scale = ((1.0 + decay) / (1.0 - decay) - 1.0 / argument) / magnitude
    return hx * scale, hy * scale, hz * scale


def lanes(shape=(8, 128)):
    return lax.broadcasted_iota(jnp.int32, shape, len(shape) - 1)


def moments_of(popul):
    density = popul[0]
    for n in range(1, 19):
        density = density + popul[n]
    momentum = []
    for k in range(3):
        total = None
        for n in range(1, 19):
            if VELOCITIES[n][k] == 1:
                total = popul[n] if total is None else total + popul[n]
            elif VELOCITIES[n][k] == -1:
                total = total - popul[n]
        momentum.append(total)
    return density, momentum


def start(*copies):
    started = [pltpu.make_async_copy(*copy) for copy in copies]
    for copy in started:
        copy.start()
    return started


def edge_kernel(pop_hbm, ht_hbm, ha_hbm, up_ref, down_ref, pop_ref, sems):
    copies = start(
        (pop_hbm.at[:, 31], pop_ref.at[0], sems.at[0]),
        (pop_hbm.at[:, 0], pop_ref.at[1], sems.at[1]),
        (ht_hbm.at[pl.ds(31 * 8, 8)], up_ref.at[pl.ds(72, 8)], sems.at[2]),
        (ht_hbm.at[pl.ds(256 + 31 * 8, 8)], up_ref.at[pl.ds(80, 8)], sems.at[3]),
        (ha_hbm.at[pl.ds(31 * 8, 8)], up_ref.at[pl.ds(88, 8)], sems.at[4]),
        (ht_hbm.at[pl.ds(0, 8)], down_ref.at[pl.ds(72, 8)], sems.at[5]),
        (ht_hbm.at[pl.ds(256, 8)], down_ref.at[pl.ds(80, 8)], sems.at[6]),
        (ha_hbm.at[pl.ds(0, 8)], down_ref.at[pl.ds(88, 8)], sems.at[7]),
    )
    for copy in copies:
        copy.wait()
    for side, (out_ref, which) in enumerate(((up_ref, 2), (down_ref, 3))):
        popul = [pop_ref[side, n] for n in range(19)]
        density, momentum = moments_of(popul)
        for k, tile in enumerate([popul[face[which]] for face in Y_FACE] + [density] + momentum):
            out_ref[k * 8 : k * 8 + 8, :] = tile


def first_kernel(ht_ref, ha_ref, table_ref, send_ref, rows_ref):
    magnet = langevin(ht_ref[:256, :], ht_ref[256:, :], ha_ref[...])
    for c in range(3):
        for pair in range(32):
            tile = magnet[c][pair * 8 : pair * 8 + 8, :]
            rows_ref[pl.ds(c * 512 + 2 * pair, 8, stride=64), :] = tile
            rows_ref[pl.ds(c * 512 + 2 * pair + 1, 8, stride=64), :] = pltpu.roll(tile, 64, 1)
    spectrum = apply_left(table_ref[...], rows_ref[...], 1)
    for row in range(ROWS_FWD):
        send_ref[pl.ds(row, NZ, stride=ROWS_FWD), :] = spectrum[:, row * 128 : row * 128 + 128]


def face_kernel(
    pop_ref, ht_ref, ha_ref, before_ref, after_ref, pair_ref, next_ref, magnet_ref
):
    magnet = langevin(ht_ref[:256, :], ht_ref[256:, :], ha_ref[...])
    for c in range(3):
        magnet_ref[c * 256 : c * 256 + 256, :] = magnet[c]
    parity = lax.rem(lax.axis_index("gx"), 2)
    for out_ref, up in ((pair_ref, parity == 0), (next_ref, parity == 1)):
        face = jnp.where(up, 7, 0)
        second = jnp.where(up, 6, 1)

        def line(ref, at):
            return ref[pl.ds(at, 32, stride=8), :]

        popul = [line(pop_ref, n * 256 + face) for n in range(19)]
        density, momentum = moments_of(popul)
        lines = [jnp.where(up, popul[f[2]], popul[f[3]]) for f in X_FACE] + [density] + momentum
        for x in (face, second):
            lines += [line(ht_ref, x), line(ht_ref, 256 + x), line(ha_ref, x)]
        for k, value in enumerate(lines):
            out_ref[k * 32 : k * 32 + 32, :] = value
        for ref, at in ((before_ref, CORNER), (after_ref, CORNER + 16)):
            out_ref[at : at + 16, :] = jnp.zeros((16, 128), F32)
            out_ref[at : at + 12, :] = ref[pl.ds(face, 12, stride=8), :]
        for ref, at in ((before_ref, CORNER + 32), (after_ref, CORNER + 40)):
            out_ref[at : at + 8, :] = jnp.zeros((8, 128), F32)
            out_ref[at : at + 3, :] = ref[pl.ds(72 + second, 3, stride=8), :]


def transpose_blocks(tiles):
    block = lanes() // 16
    for bit in (1, 2, 4):
        low = (block & bit) == 0
        out = list(tiles)
        for i in range(8):
            if i & bit == 0:
                a, b = tiles[i], tiles[i | bit]
                out[i] = jnp.where(low, a, pltpu.roll(b, 16 * bit, 1))
                out[i | bit] = jnp.where(low, pltpu.roll(a, 128 - 16 * bit, 1), b)
        tiles = out
    return tiles


def cells_kernel(recv_ref, cells_ref):
    left = lanes() < 64
    for c in range(3):
        for pair in range(4):
            for x4 in range(4):
                start = 16 * pair * ROWS_FWD + c * 4 + x4
                a = recv_ref[pl.ds(start, 8, stride=ROWS_FWD), :]
                b = recv_ref[pl.ds(start + 8 * ROWS_FWD, 8, stride=ROWS_FWD), :]
                at, col = x4 * 8, c * 512 + pair * 128
                cells_ref[at : at + 8, col : col + 128] = jnp.where(left, a, pltpu.roll(b, 64, 1))
                cells_ref[at + 32 : at + 40, col : col + 128] = jnp.where(
                    left, pltpu.roll(a, 64, 1), b
                )


def plane_kernel(
    own_ref,
    other_ref,
    fwd_x_ref,
    back_x_ref,
    even_ref,
    odd_ref,
    back_even_ref,
    back_odd_ref,
    wave_x_ref,
    wave_y_ref,
    wave_z_ref,
    send_ref,
):
    row = lax.axis_index("gx")
    parity = lax.rem(row, 2)
    index_z = lax.axis_index("gy") * 8 + row // 2
    left = lanes() < 64
    wave_x = wave_x_ref[:, 0:1]
    wave_z = wave_z_ref[pl.ds(index_z, 1), 0:1]
    cells = jnp.concatenate([own_ref[...], other_ref[...]], axis=0)
    spectrum = apply_left(fwd_x_ref[parity], cells)
    along = wave_x * spectrum[:, :512] + wave_z * spectrum[:, 1024:]
    both = jnp.concatenate([along, spectrum[:, 512:1024]], axis=0)
    parts = (
        apply_right(both[:, :256] + both[:, 256:], even_ref[...]),
        apply_right(both[:, :256] - both[:, 256:], odd_ref[...]),
    )
    back = []
    for which in range(2):
        wave_y = wave_y_ref[which : which + 1, :]
        squared = wave_x * wave_x + wave_y * wave_y + wave_z * wave_z
        anchor = squared == 0.0
        factor = jnp.where(
            anchor, 0.0, (-1.0 / (NX * NY * NZ)) / jnp.where(anchor, 1.0, squared)
        )
        potential = (parts[which][:128] + wave_y * parts[which][128:]) * factor
        stacked = jnp.concatenate([potential, wave_y * potential], axis=0)
        back.append(apply_right(stacked, (back_even_ref, back_odd_ref)[which][...]))
    low, high = back[0] + back[1], back[0] - back[1]
    column = lanes((128, 128)) % 16
    halo_p, halo_q = low[:128, 256:], low[128:, 256:]
    halo = jnp.where(
        column < 4,
        wave_x * halo_p,
        jnp.where(column < 8, halo_q, jnp.where(column < 12, wave_z * halo_p, 0.0)),
    )
    potential = jnp.concatenate([low[:128, :256], high[:128, :256]], axis=1)
    fields = jnp.concatenate(
        [wave_x * potential, low[128:, :256], high[128:, :256], wave_z * potential, halo], axis=1
    )
    cells = apply_left(back_x_ref[parity], fields)
    for x6 in range(6):
        for c in range(3):
            for pair in range(4):
                col = c * 512 + pair * 128
                a = cells[x6 * 8 : x6 * 8 + 8, col : col + 128]
                b = cells[48 + x6 * 8 : 56 + x6 * 8, col : col + 128]
                at = 16 * pair * ROWS_BACK + c * 6 + x6
                send_ref[pl.ds(at, 8, stride=ROWS_BACK), :] = jnp.where(left, a, pltpu.roll(b, 64, 1))
                send_ref[pl.ds(at + 8 * ROWS_BACK, 8, stride=ROWS_BACK), :] = jnp.where(
                    left, pltpu.roll(a, 64, 1), b
                )
    for part in range(2):
        tiles = []
        for x in range(part * 8, part * 8 + 8):
            if x < 12:
                at = (x % 2) * 48 + (x // 2) * 8
                tiles.append(cells[at : at + 8, 1536:])
            else:
                tiles.append(jnp.zeros((8, 128), F32))
        for g, tile in enumerate(transpose_blocks(tiles)):
            at = 8 * g * ROWS_BACK + 18 + part
            send_ref[pl.ds(at, 8, stride=ROWS_BACK), :] = tile


def macroscopic(density, momentum, force):
    inverse = 1.0 / density
    vel = [(momentum[k] + 0.5 * force[k]) * inverse for k in range(3)]
    u_square = vel[0] * vel[0] + vel[1] * vel[1] + vel[2] * vel[2]
    u_dot_f = vel[0] * force[0] + vel[1] * force[1] + vel[2] * force[2]
    scaled = OMEGA * density
    base = scaled * (1.0 - 1.5 * u_square) - 0.5 * u_dot_f
    return vel, scaled, base


def along(lattice, vector):
    total = None
    for sign, value in zip(lattice, vector):
        if isinstance(sign, int):
            if sign == 0:
                continue
            term = value if sign == 1 else -value
        else:
            term = sign * value
        total = term if total is None else total + term
    return total


def relax_terms(lattice, vel, force, scaled, base):
    along_u = along(lattice, vel)
    along_f = along(lattice, force)
    even = base + along_u * (4.5 * scaled * along_u + 1.5 * along_f)
    odd = 3.0 * scaled * along_u + 0.5 * along_f
    return even, odd


def shift_z(tile, step, lane):
    if step == 0:
        return tile
    if step == 1:
        return jnp.where(lane % 64 == 0, pltpu.roll(tile, 65, 1), pltpu.roll(tile, 1, 1))
    return jnp.where(lane % 64 == 63, pltpu.roll(tile, 63, 1), pltpu.roll(tile, 127, 1))


def cell_kernel(
    recv_ref,
    table_ref,
    ht_ref,
    ha_ref,
    magnet_ref,
    pop_ref,
    pair_ref,
    next_ref,
    before_ref,
    after_ref,
    out_hbm,
    demag_hbm,
    out_ref,
    demag_ref,
    field_ref,
    total_ref,
    post_ref,
    side_ref,
    enter_ref,
    out_sems,
):
    lane = lanes()
    left = lane < 64
    left4 = lanes((32, 128)) < 64
    parity = lax.rem(lax.axis_index("gx"), 2)
    side_of = ((next_ref, pair_ref), (pair_ref, next_ref))

    def side(which, at, count):
        even, odd = side_of[which]
        return jnp.where(parity == 0, even[at : at + count, :], odd[at : at + count, :])

    def base(c, x):
        return (c * 12 + 2 + x) * PITCH + 2

    def both(tile):
        turned = pltpu.roll(tile, 64, 1)
        first = lanes(tile.shape) < 64
        return jnp.where(first, tile, turned), jnp.where(first, turned, tile)

    own = ((ht_ref, 0), (ht_ref, 256), (ha_ref, 0))
    for c in range(3):
        ref, at = own[c]
        for pair in range(32):
            for odd, tile in enumerate(both(ref[at + pair * 8 : at + pair * 8 + 8, :])):
                total_ref[pl.ds(base(c, 0) + 2 * pair + odd, 8, stride=PITCH), :] = tile
        for edge_ref, y in ((before_ref, -2), (after_ref, 64)):
            for odd, tile in enumerate(both(edge_ref[72 + c * 8 : 80 + c * 8, :])):
                total_ref[pl.ds(base(c, 0) + y + odd, 8, stride=PITCH), :] = tile
        for which, near, far in ((0, -1, -2), (1, 8, 9)):
            for x, k, corner in ((near, 9 + c, 9 + c), (far, 12 + c, 32 + c)):
                for odd, tile in enumerate(both(side(which, k * 32, 32))):
                    total_ref[pl.ds(base(c, x) + odd, 32, stride=2), :] = tile
                after = 16 if x == near else 8
                for y, at in ((-2, CORNER + corner), (64, CORNER + corner + after)):
                    for odd, tile in enumerate(both(side(which, at, 1))):
                        at_row = base(c, x) + y + odd
                        total_ref[at_row : at_row + 1, :] = tile

    for row in range(ROWS_BACK):
        spectrum = recv_ref[pl.ds(row, NZ, stride=ROWS_BACK), :]
        cells = apply_right(spectrum, table_ref[...], 0)
        if row < 18:
            for half in range(2):
                c, x = row // 6, 2 * (row % 6) + half - 2
                at = base(c, x)
                part = cells[half * 64 : half * 64 + 64, :]
                total_ref[at : at + 64, :] += part
                if 0 <= x < 8:
                    at = (c * 8 + x) * OWN_PITCH
                    field_ref[at : at + 64, :] = part
        else:
            for k in range(8):
                x = (row - 18) * 8 + k - 2
                if x < 10:
                    for c in range(3):
                        at, src = base(c, x), k * 16 + c * 4
                        total_ref[at - 2 : at, :] += cells[src : src + 2, :]
                        total_ref[at + 64 : at + 66, :] += cells[src + 2 : src + 4, :]

    def forces(magnet, read, first):
        force = []
        for c in range(3):
            d_x = jnp.where(first, *read(c, 1, 0)) - jnp.where(first, *read(c, -1, 0))
            d_y = jnp.where(first, *read(c, 0, 1)) - jnp.where(first, *read(c, 0, -1))
            a, b = read(c, 0, 0)
            d_z = jnp.where(first, pltpu.roll(a, 127, 1), pltpu.roll(b, 127, 1)) - jnp.where(
                first, pltpu.roll(a, 1, 1), pltpu.roll(b, 1, 1)
            )
            force.append(0.025 * (magnet[0] * d_x + magnet[1] * d_y + magnet[2] * d_z))
        return force

    def column(c, x, y):
        return total_ref[pl.ds(base(c, x) + y, 8, stride=PITCH), :]

    sign = jnp.where(left, -1.0, 1.0)
    values = [
        jnp.where(left, after_ref[k * 8 : k * 8 + 8, :], before_ref[k * 8 : k * 8 + 8, :])
        for k in range(12)
    ]
    force = forces(
        langevin(*values[9:]),
        lambda c, dx, dy: (column(c, dx, 64 + dy), column(c, dx, dy - 1)),
        left,
    )
    vel, scaled, rest = macroscopic(values[5], values[6:9], force)
    for slot, (cx, cz, up, down) in enumerate(Y_FACE):
        even, odd = relax_terms((cx, sign, cz), vel, force, scaled, rest)
        post = shift_z((1.0 - OMEGA) * values[slot] + WEIGHTS[up] * (even + odd), cz, lane)
        post_ref[up, 0] = post
        post_ref[down, 33] = post

    row = lax.broadcasted_iota(jnp.int32, (8, 128), 0)
    upper = row == 7

    def edge_rows(k_low, k_high):
        pair = []
        for which, k in ((0, k_low), (1, k_high)):
            value = jnp.where(
                left[:1], side(which, CORNER + 16 + k, 1), side(which, CORNER + k, 1)
            )
            pair.append(jnp.broadcast_to(value, (8, 128)))
        return jnp.where(upper, pair[1], pair[0])

    def corner(c, dx, y):
        return jnp.where(upper, column(c, 1 + dx, y), column(c, dx - 1, y))

    force = forces(
        langevin(*[edge_rows(k, k) for k in (9, 10, 11)]),
        lambda c, dx, dy: (corner(c, dx, 64 + dy), corner(c, dx, dy - 1)),
        left,
    )
    vel, scaled, rest = macroscopic(edge_rows(5, 5), [edge_rows(k, k) for k in (6, 7, 8)], force)
    even, odd = relax_terms((jnp.where(upper, -1.0, 1.0), sign, 0), vel, force, scaled, rest)
    edges = (1.0 - OMEGA) * edge_rows(1, 2) + WEIGHTS[7] * (even + odd)

    for which, x, step in ((0, -1, 1), (1, 8, -1)):

        def read(c, dx, dy):
            at = base(c, x + dx) + dy
            return (
                total_ref[pl.ds(at, 32, stride=2), :],
                total_ref[pl.ds(at + 1, 32, stride=2), :],
            )

        values = [side(which, k * 32, 32) for k in range(12)]
        force = forces(langevin(*values[9:]), read, left4)
        vel, scaled, rest = macroscopic(values[5], values[6:9], force)
        at_edge = 7 * which
        lane4 = lanes((32, 128))
        for slot, (cy, cz, up, down) in enumerate(X_FACE):
            even, odd = relax_terms((step, cy, cz), vel, force, scaled, rest)
            post = shift_z((1.0 - OMEGA) * values[slot] + WEIGHTS[up] * (even + odd), cz, lane4)
            if cy != 0:
                side_ref[8:40, :] = post
                if cy == 1:
                    side_ref[7:8, :] = edges[at_edge : at_edge + 1, :]
                    post = jnp.where(left4, post, side_ref[7:39, :])
                else:
                    side_ref[40:41, :] = edges[at_edge : at_edge + 1, :]
                    post = jnp.where(left4, side_ref[9:41, :], post)
                post = pltpu.roll(post, 64, 1)
            enter_ref[which, slot] = post

    def collide(pair, carry):
        ya = 2 * pair
        at = pl.multiple_of(pair * 8, 8)
        for c in range(3):
            src = c * 8 * OWN_PITCH + ya
            demag_ref[pl.ds(c * 256 + at, 8), :] = jnp.where(
                left,
                field_ref[pl.ds(src, 8, stride=OWN_PITCH), :],
                field_ref[pl.ds(src + 1, 8, stride=OWN_PITCH), :],
            )
        force = forces(
            [magnet_ref[pl.ds(c * 256 + at, 8), :] for c in range(3)],
            lambda c, dx, dy: (column(c, dx, ya + dy), column(c, dx, ya + 1 + dy)),
            left,
        )
        popul = [pop_ref[n, pl.ds(at, 8), :] for n in range(19)]
        density, momentum = moments_of(popul)
        vel, scaled, rest = macroscopic(density, momentum, force)
        post_ref[0, 1 + pair] = (1.0 - OMEGA) * popul[0] + WEIGHTS[0] * rest
        for n in range(1, 19, 2):
            even, odd = relax_terms(VELOCITIES[n], vel, force, scaled, rest)
            for number, value in ((n, even + odd), (n + 1, even - odd)):
                post = (1.0 - OMEGA) * popul[number] + WEIGHTS[n] * value
                post_ref[number, 1 + pair] = shift_z(post, VELOCITIES[number][2], lane)
        return carry

    lax.fori_loop(0, 32, collide, 0, unroll=4)
    sent = start((demag_ref, demag_hbm, out_sems.at[4]))

    def stream(pair, carry):
        at = pl.multiple_of(pair * 8, 8)
        for n in range(19):
            cx, cy, _ = VELOCITIES[n]
            tile = post_ref[n, 1 + pair]
            if cy == 1:
                tile = pltpu.roll(jnp.where(left, tile, post_ref[n, pair]), 64, 1)
            elif cy == -1:
                tile = pltpu.roll(jnp.where(left, post_ref[n, 2 + pair], tile), 64, 1)
            if cx != 0:
                enters = enter_ref[0 if cx == 1 else 1, X_SLOT[n], pl.ds(pair, 1), :]
                tile = jnp.where(
                    row == (0 if cx == 1 else 7),
                    jnp.broadcast_to(enters, (8, 128)),
                    pltpu.roll(tile, 1 if cx == 1 else 7, 0),
                )
            out_ref[n, pl.ds(at, 8), :] = tile
        return carry

    for part in range(4):
        lax.fori_loop(8 * part, 8 * part + 8, stream, 0, unroll=8)
        rows = pl.ds(64 * part, 64)
        sent += start((out_ref.at[:, rows], out_hbm.at[:, rows], out_sems.at[part]))
    for copy in sent:
        copy.wait()


HBM = pl.BlockSpec(memory_space=pltpu.HBM)
ANY = pl.BlockSpec(memory_space=pl.ANY)
VMEM = pl.BlockSpec(memory_space=pltpu.VMEM)


def call(kernel, ins, outs, scratch, sems, flops, moved, vmem=60):
    return pl.pallas_call(
        kernel,
        out_shape=[jax.ShapeDtypeStruct(shape, F32) for shape, _ in outs],
        in_specs=ins,
        out_specs=[spec for _, spec in outs],
        scratch_shapes=[pltpu.VMEM(shape, F32) for shape in scratch]
        + [pltpu.SemaphoreType.DMA((count,)) for count in sems],
        compiler_params=pltpu.CompilerParams(vmem_limit_bytes=vmem * 1024 * 1024),
        cost_estimate=pl.CostEstimate(flops=flops, bytes_accessed=moved, transcendentals=0),
    )


def ring(values, axis, step):
    size = lax.axis_size(axis)
    return lax.ppermute(values, axis, [(i, (i + step) % size) for i in range(size)])


GROUPS = [[(2 * m + core) * GY + g for g in range(GY) for m in range(8)] for core in range(2)]


def exchange(rows, count):
    blocks = rows.reshape(64, 1, count * 128)
    blocks = lax.all_to_all(
        blocks, ("gx", "gy"), 0, 0, axis_index_groups=GROUPS, tiled=True
    )
    return blocks.reshape(64 * count, 128)


def as_tiles(values):
    return values.reshape(-1, 8, 32, 128).transpose(0, 2, 1, 3)


def from_rows(rows):
    return rows.reshape(-1, 32, 8, 128).transpose(0, 2, 1, 3).reshape(-1, 8, 4096)


def on_device(populations, h_axial, h_transverse):
    t = tables()
    pop_tiles = as_tiles(populations)
    pop_rows = pop_tiles.reshape(19 * 256, 128)
    ht_rows = as_tiles(h_transverse).reshape(512, 128)
    ha_rows = as_tiles(h_axial).reshape(256, 128)
    up, down = call(
        edge_kernel,
        [HBM] * 3,
        [((96, 128), VMEM), ((96, 128), VMEM)],
        [(2, 19, 8, 128)],
        [8],
        100_000,
        300_000,
    )(pop_tiles, ht_rows, ha_rows)
    before = ring(up, "gy", 1)
    after = ring(down, "gy", -1)
    (rows,) = call(
        first_kernel,
        [VMEM] * 3,
        [((64 * ROWS_FWD, 128), VMEM)],
        [(1536, 128)],
        [],
        30_000_000,
        1_800_000,
        8,
    )(ht_rows, ha_rows, t["fwd_z"])
    to_pair, to_next, magnet = call(
        face_kernel,
        [VMEM] * 5,
        [((FACE_ROWS, 128), VMEM), ((FACE_ROWS, 128), VMEM), ((768, 128), VMEM)],
        [],
        [],
        1_000_000,
        4_000_000,
        8,
    )(pop_rows, ht_rows, ha_rows, before, after)
    rows, to_pair, to_next = lax.optimization_barrier((rows, to_pair, to_next))
    own = exchange(rows, ROWS_FWD)
    (own,) = call(
        cells_kernel, [VMEM], [((64, 1536), VMEM)], [], [], 1_000, 40000000, 8
    )(own)
    other = lax.ppermute(own, "gx", [(i, i ^ 1) for i in range(GX)])
    pair = lax.ppermute(to_pair, "gx", [(i, i ^ 1) for i in range(GX)])
    beyond = lax.ppermute(to_next, "gx", [(i, ((i + 1) ^ 1) - 1 & 15) for i in range(GX)])
    (rows,) = call(
        plane_kernel,
        [VMEM] * 11,
        [((64 * ROWS_BACK, 128), VMEM)],
        [],
        [],
        1_000,
        1_000,
        16,
    )(
        own,
        other,
        t["fwd_x"],
        t["back_x"],
        t["even"],
        t["odd"],
        t["back_even"],
        t["back_odd"],
        t["wave_x"],
        t["wave_y"],
        t["wave_z"],
    )
    rows, pair, beyond = lax.optimization_barrier((rows, pair, beyond))
    recv = exchange(rows, ROWS_BACK)
    result, demag = call(
        cell_kernel,
        [VMEM] * 10,
        [((19, 256, 128), HBM), ((3 * 256, 128), HBM)],
        [
            (19, 256, 128),
            (768, 128),
            (24 * OWN_PITCH, 128),
            (36 * PITCH, 128),
            (19, 34, 8, 128),
            (48, 128),
            (2, 5, 32, 128),
        ],
        [5],
        60_000_000,
        8_000_000,
        24,
    )(
        recv,
        t["back_z"],
        ht_rows,
        ha_rows,
        magnet,
        pop_rows.reshape(19, 256, 128),
        pair,
        beyond,
        before,
        after,
    )
    return from_rows(result), from_rows(demag)


def solution(mesh):
    placed = (P(None, "gx", "gy"), P("gx", "gy"), P(None, "gx", "gy"))
    return jax.shard_map(
        on_device,
        mesh=mesh,
        in_specs=placed,
        out_specs=(P(None, "gx", "gy"), P(None, "gx", "gy")),
        check_vma=False,
    )
```

```python
import functools

import jax
import jax.numpy as jnp
import ml_dtypes
import numpy as np
from jax import lax
from jax.experimental import pallas as pl
from jax.experimental.pallas import tpu as pltpu
from jax.sharding import PartitionSpec as P

NX, NY, NZ = 128, 512, 64
GX, GY = 16, 8
VELOCITIES = (
    (0, 0, 0),
    (1, 0, 0),
    (-1, 0, 0),
    (0, 1, 0),
    (0, -1, 0),
    (0, 0, 1),
    (0, 0, -1),
    (1, 1, 0),
    (-1, -1, 0),
    (1, -1, 0),
    (-1, 1, 0),
    (1, 0, 1),
    (-1, 0, -1),
    (1, 0, -1),
    (-1, 0, 1),
    (0, 1, 1),
    (0, -1, -1),
    (0, 1, -1),
    (0, -1, 1),
)
WEIGHTS = (1.0 / 3.0,) + (1.0 / 18.0,) * 6 + (1.0 / 36.0,) * 12
OMEGA = 1.0 / 0.6
PULL = 0.05 / 2
F32 = jnp.float32

X_FACE = ((0, 0, 1, 2), (1, 0, 7, 10), (-1, 0, 9, 8), (0, 1, 11, 14), (0, -1, 13, 12))
Y_FACE = ((0, 0, 3, 4), (1, 0, 7, 9), (-1, 0, 10, 8), (0, 1, 15, 18), (0, -1, 17, 16))
X_SLOT = {n: s for s, row in enumerate(X_FACE) for n in row[2:]}

ROWS_FWD = 12
ROWS_BACK = 20
CORNER = 480
FACE_ROWS = CORNER + 48
PITCH = 69
OWN_PITCH = 65


def cas(rows, cols, count):
    angle = 2.0 * np.pi * ((rows[:, None] * cols[None, :]) % count) / count
    return np.cos(angle) + np.sin(angle)


def wave(index, count):
    return 2.0 * np.sin(np.pi * index / count)


@functools.lru_cache(maxsize=None)
def tables():
    every_x, every_z = np.arange(NX), np.arange(NZ)
    half = np.arange(NY // 2)
    out = {}
    fwd_z = np.zeros((NZ, 128))
    fwd_z[:, :NZ] = cas(every_z, every_z, NZ)
    out["fwd_z"] = fwd_z
    out["back_z"] = np.tile(cas(every_z, every_z, NZ), (1, 2))
    fwd_x, back_x = [], []
    m = np.arange(8)
    for parity in range(2):
        order = []
        for side in (parity, 1 - parity):
            for x2 in range(2):
                for x4 in range(4):
                    order += list(8 * (2 * m + side) + 2 * x4 + x2)
        fwd_x.append(cas(every_x, np.array(order), NX))
        order = []
        for x2 in range(2):
            for x6 in range(6):
                order += list((8 * (2 * m + parity) - 2 + 2 * x6 + x2) % NX)
        back_x.append(cas(np.array(order), every_x, NX))
    out["fwd_x"] = np.stack(fwd_x)
    out["back_x"] = np.stack(back_x)
    even, odd = 2 * half, 2 * half + 1
    halo = np.array(
        [
            (64 * g + (-2, -1, 64, 65)[k]) % NY
            for g in range(GY)
            for c in range(4)
            for k in range(4)
        ]
    )
    out["even"] = cas(half, even, NY)
    out["odd"] = cas(half, odd, NY)
    out["back_even"] = np.concatenate([cas(even, half, NY), cas(even, halo, NY)], axis=1)
    out["back_odd"] = np.concatenate([cas(odd, half, NY), cas(odd, halo, NY)], axis=1)
    out["wave_x"] = np.repeat(wave(every_x, NX)[:, None], 128, axis=1)
    out["wave_y"] = np.stack([wave(even, NY), wave(odd, NY)])
    out["wave_z"] = np.repeat(wave(every_z, NZ)[:, None], 128, axis=1)
    out = {name: np.asarray(value, np.float32) for name, value in out.items()}
    for name, axis in SPLIT_TABLES.items():
        high = out[name].astype(ml_dtypes.bfloat16)
        low = (out[name] - high.astype(np.float32)).astype(ml_dtypes.bfloat16)
        out[name] = np.concatenate([high, low, high], axis=axis)
    return out


SPLIT_TABLES = {
    "fwd_z": 1,
    "back_z": 0,
    "fwd_x": 2,
    "back_x": 2,
    "even": 0,
    "odd": 0,
    "back_even": 0,
    "back_odd": 0,
}


def terms(values, axis):
    high = values.astype(jnp.bfloat16)
    low = (values - high.astype(F32)).astype(jnp.bfloat16)
    return jnp.concatenate([high, high, low], axis=axis)


def product(a, b, dims):
    return lax.dot_general(a, b, (((dims[0],), (dims[1],)), ((), ())), preferred_element_type=F32)


def apply_left(table, values, axis=0):
    return product(table, terms(values, axis), (1, axis))


def apply_right(values, table, axis=1):
    return product(terms(values, axis), table, (axis, 0))


def langevin(hx, hy, hz):
    magnitude = jnp.sqrt(hx * hx + hy * hy + hz * hz)
    argument = 1.5 * magnitude
    decay = jnp.exp(-2.0 * argument)
    scale = ((1.0 + decay) / (1.0 - decay) - 1.0 / argument) / magnitude
    return hx * scale, hy * scale, hz * scale


def lanes(shape=(8, 128)):
    return lax.broadcasted_iota(jnp.int32, shape, len(shape) - 1)


def moments_of(popul):
    density = popul[0]
    for n in range(1, 19):
        density = density + popul[n]
    momentum = []
    for k in range(3):
        total = None
        for n in range(1, 19):
            if VELOCITIES[n][k] == 1:
                total = popul[n] if total is None else total + popul[n]
            elif VELOCITIES[n][k] == -1:
                total = total - popul[n]
        momentum.append(total)
    return density, momentum


def start(*copies):
    started = [pltpu.make_async_copy(*copy) for copy in copies]
    for copy in started:
        copy.start()
    return started


def edge_kernel(pop_hbm, ht_hbm, ha_hbm, up_ref, down_ref, pop_ref, sems):
    copies = start(
        (pop_hbm.at[:, 31], pop_ref.at[0], sems.at[0]),
        (pop_hbm.at[:, 0], pop_ref.at[1], sems.at[1]),
        (ht_hbm.at[pl.ds(31 * 8, 8)], up_ref.at[pl.ds(72, 8)], sems.at[2]),
        (ht_hbm.at[pl.ds(256 + 31 * 8, 8)], up_ref.at[pl.ds(80, 8)], sems.at[3]),
        (ha_hbm.at[pl.ds(31 * 8, 8)], up_ref.at[pl.ds(88, 8)], sems.at[4]),
        (ht_hbm.at[pl.ds(0, 8)], down_ref.at[pl.ds(72, 8)], sems.at[5]),
        (ht_hbm.at[pl.ds(256, 8)], down_ref.at[pl.ds(80, 8)], sems.at[6]),
        (ha_hbm.at[pl.ds(0, 8)], down_ref.at[pl.ds(88, 8)], sems.at[7]),
    )
    for copy in copies:
        copy.wait()
    for side, (out_ref, which) in enumerate(((up_ref, 2), (down_ref, 3))):
        popul = [pop_ref[side, n] for n in range(19)]
        density, momentum = moments_of(popul)
        for k, tile in enumerate([popul[face[which]] for face in Y_FACE] + [density] + momentum):
            out_ref[k * 8 : k * 8 + 8, :] = tile


def first_kernel(ht_ref, ha_ref, table_ref, send_ref, rows_ref):
    magnet = langevin(ht_ref[:256, :], ht_ref[256:, :], ha_ref[...])
    for c in range(3):
        for pair in range(32):
            tile = magnet[c][pair * 8 : pair * 8 + 8, :]
            rows_ref[pl.ds(c * 512 + 2 * pair, 8, stride=64), :] = tile
            rows_ref[pl.ds(c * 512 + 2 * pair + 1, 8, stride=64), :] = pltpu.roll(tile, 64, 1)
    spectrum = apply_left(table_ref[...], rows_ref[...], 1)
    for row in range(ROWS_FWD):
        send_ref[pl.ds(row, NZ, stride=ROWS_FWD), :] = spectrum[:, row * 128 : row * 128 + 128]


def face_kernel(
    pop_ref, ht_ref, ha_ref, before_ref, after_ref, pair_ref, next_ref, magnet_ref
):
    magnet = langevin(ht_ref[:256, :], ht_ref[256:, :], ha_ref[...])
    for c in range(3):
        magnet_ref[c * 256 : c * 256 + 256, :] = PULL * magnet[c]
    parity = lax.rem(lax.axis_index("gx"), 2)
    for out_ref, up in ((pair_ref, parity == 0), (next_ref, parity == 1)):
        face = jnp.where(up, 7, 0)
        second = jnp.where(up, 6, 1)

        def line(ref, at):
            return ref[pl.ds(at, 32, stride=8), :]

        popul = [line(pop_ref, n * 256 + face) for n in range(19)]
        density, momentum = moments_of(popul)
        lines = [jnp.where(up, popul[f[2]], popul[f[3]]) for f in X_FACE] + [density] + momentum
        for x in (face, second):
            lines += [line(ht_ref, x), line(ht_ref, 256 + x), line(ha_ref, x)]
        for k, value in enumerate(lines):
            out_ref[k * 32 : k * 32 + 32, :] = value
        for ref, at in ((before_ref, CORNER), (after_ref, CORNER + 16)):
            out_ref[at : at + 16, :] = jnp.zeros((16, 128), F32)
            out_ref[at : at + 12, :] = ref[pl.ds(face, 12, stride=8), :]
        for ref, at in ((before_ref, CORNER + 32), (after_ref, CORNER + 40)):
            out_ref[at : at + 8, :] = jnp.zeros((8, 128), F32)
            out_ref[at : at + 3, :] = ref[pl.ds(72 + second, 3, stride=8), :]


def transpose_blocks(tiles):
    block = lanes() // 16
    for bit in (1, 2, 4):
        low = (block & bit) == 0
        out = list(tiles)
        for i in range(8):
            if i & bit == 0:
                a, b = tiles[i], tiles[i | bit]
                out[i] = jnp.where(low, a, pltpu.roll(b, 16 * bit, 1))
                out[i | bit] = jnp.where(low, pltpu.roll(a, 128 - 16 * bit, 1), b)
        tiles = out
    return tiles


def cells_kernel(recv_ref, cells_ref):
    left = lanes() < 64
    for c in range(3):
        for pair in range(4):
            for x4 in range(4):
                start = 16 * pair * ROWS_FWD + c * 4 + x4
                a = recv_ref[pl.ds(start, 8, stride=ROWS_FWD), :]
                b = recv_ref[pl.ds(start + 8 * ROWS_FWD, 8, stride=ROWS_FWD), :]
                at, col = x4 * 8, c * 512 + pair * 128
                cells_ref[at : at + 8, col : col + 128] = jnp.where(left, a, pltpu.roll(b, 64, 1))
                cells_ref[at + 32 : at + 40, col : col + 128] = jnp.where(
                    left, pltpu.roll(a, 64, 1), b
                )


def plane_kernel(
    own_ref,
    other_ref,
    fwd_x_ref,
    back_x_ref,
    even_ref,
    odd_ref,
    back_even_ref,
    back_odd_ref,
    wave_x_ref,
    wave_y_ref,
    wave_z_ref,
    send_ref,
):
    row = lax.axis_index("gx")
    parity = lax.rem(row, 2)
    index_z = lax.axis_index("gy") * 8 + row // 2
    left = lanes() < 64
    wave_x = wave_x_ref[:, 0:1]
    wave_z = wave_z_ref[pl.ds(index_z, 1), 0:1]
    cells = jnp.concatenate([own_ref[...], other_ref[...]], axis=0)
    spectrum = apply_left(fwd_x_ref[parity], cells)
    along = wave_x * spectrum[:, :512] + wave_z * spectrum[:, 1024:]
    both = jnp.concatenate([along, spectrum[:, 512:1024]], axis=0)
    parts = (
        apply_right(both[:, :256] + both[:, 256:], even_ref[...]),
        apply_right(both[:, :256] - both[:, 256:], odd_ref[...]),
    )
    back = []
    for which in range(2):
        wave_y = wave_y_ref[which : which + 1, :]
        squared = wave_x * wave_x + wave_y * wave_y + wave_z * wave_z
        anchor = squared == 0.0
        factor = jnp.where(
            anchor, 0.0, (-1.0 / (NX * NY * NZ)) / jnp.where(anchor, 1.0, squared)
        )
        potential = (parts[which][:128] + wave_y * parts[which][128:]) * factor
        stacked = jnp.concatenate([potential, wave_y * potential], axis=0)
        back.append(apply_right(stacked, (back_even_ref, back_odd_ref)[which][...]))
    low, high = back[0] + back[1], back[0] - back[1]
    column = lanes((128, 128)) % 16
    halo_p, halo_q = low[:128, 256:], low[128:, 256:]
    halo = jnp.where(
        column < 4,
        wave_x * halo_p,
        jnp.where(column < 8, halo_q, jnp.where(column < 12, wave_z * halo_p, 0.0)),
    )
    potential = jnp.concatenate([low[:128, :256], high[:128, :256]], axis=1)
    fields = jnp.concatenate(
        [wave_x * potential, low[128:, :256], high[128:, :256], wave_z * potential, halo], axis=1
    )
    cells = apply_left(back_x_ref[parity], fields)
    for x6 in range(6):
        for c in range(3):
            for pair in range(4):
                col = c * 512 + pair * 128
                a = cells[x6 * 8 : x6 * 8 + 8, col : col + 128]
                b = cells[48 + x6 * 8 : 56 + x6 * 8, col : col + 128]
                at = 16 * pair * ROWS_BACK + c * 6 + x6
                send_ref[pl.ds(at, 8, stride=ROWS_BACK), :] = jnp.where(left, a, pltpu.roll(b, 64, 1))
                send_ref[pl.ds(at + 8 * ROWS_BACK, 8, stride=ROWS_BACK), :] = jnp.where(
                    left, pltpu.roll(a, 64, 1), b
                )
    for part in range(2):
        tiles = []
        for x in range(part * 8, part * 8 + 8):
            if x < 12:
                at = (x % 2) * 48 + (x // 2) * 8
                tiles.append(cells[at : at + 8, 1536:])
            else:
                tiles.append(jnp.zeros((8, 128), F32))
        for g, tile in enumerate(transpose_blocks(tiles)):
            at = 8 * g * ROWS_BACK + 18 + part
            send_ref[pl.ds(at, 8, stride=ROWS_BACK), :] = tile


def macroscopic(density, momentum, force):
    inverse = 1.0 / density
    vel = [(momentum[k] + 0.5 * force[k]) * inverse for k in range(3)]
    u_square = vel[0] * vel[0] + vel[1] * vel[1] + vel[2] * vel[2]
    u_dot_f = vel[0] * force[0] + vel[1] * force[1] + vel[2] * force[2]
    scaled = OMEGA * density
    base = scaled * (1.0 - 1.5 * u_square) - 0.5 * u_dot_f
    return vel, scaled, base


def along(lattice, vector):
    total = None
    for sign, value in zip(lattice, vector):
        if isinstance(sign, int):
            if sign == 0:
                continue
            term = value if sign == 1 else -value
        else:
            term = sign * value
        total = term if total is None else total + term
    return total


def relax_terms(lattice, vel, force, scaled, base):
    along_u = along(lattice, vel)
    along_f = along(lattice, force)
    even = base + along_u * (4.5 * scaled * along_u + 1.5 * along_f)
    odd = 3.0 * scaled * along_u + 0.5 * along_f
    return even, odd


def shift_z(tile, step, lane):
    if step == 0:
        return tile
    if step == 1:
        return jnp.where(lane % 64 == 0, pltpu.roll(tile, 65, 1), pltpu.roll(tile, 1, 1))
    return jnp.where(lane % 64 == 63, pltpu.roll(tile, 63, 1), pltpu.roll(tile, 127, 1))


def cell_kernel(
    recv_ref,
    table_ref,
    ht_ref,
    ha_ref,
    magnet_ref,
    pop_ref,
    pair_ref,
    next_ref,
    before_ref,
    after_ref,
    out_hbm,
    demag_hbm,
    out_ref,
    demag_ref,
    field_ref,
    total_ref,
    post_ref,
    side_ref,
    enter_ref,
    out_sems,
):
    lane = lanes()
    left = lane < 64
    left4 = lanes((32, 128)) < 64
    parity = lax.rem(lax.axis_index("gx"), 2)
    side_of = ((next_ref, pair_ref), (pair_ref, next_ref))

    def side(which, at, count):
        even, odd = side_of[which]
        return jnp.where(parity == 0, even[at : at + count, :], odd[at : at + count, :])

    def base(c, x):
        return (c * 12 + 2 + x) * PITCH + 2

    def both(tile):
        turned = pltpu.roll(tile, 64, 1)
        first = lanes(tile.shape) < 64
        return jnp.where(first, tile, turned), jnp.where(first, turned, tile)

    own = ((ht_ref, 0), (ht_ref, 256), (ha_ref, 0))
    for c in range(3):
        ref, at = own[c]
        for pair in range(32):
            for odd, tile in enumerate(both(ref[at + pair * 8 : at + pair * 8 + 8, :])):
                total_ref[pl.ds(base(c, 0) + 2 * pair + odd, 8, stride=PITCH), :] = tile
        for edge_ref, y in ((before_ref, -2), (after_ref, 64)):
            for odd, tile in enumerate(both(edge_ref[72 + c * 8 : 80 + c * 8, :])):
                total_ref[pl.ds(base(c, 0) + y + odd, 8, stride=PITCH), :] = tile
        for which, near, far in ((0, -1, -2), (1, 8, 9)):
            for x, k, corner in ((near, 9 + c, 9 + c), (far, 12 + c, 32 + c)):
                for odd, tile in enumerate(both(side(which, k * 32, 32))):
                    total_ref[pl.ds(base(c, x) + odd, 32, stride=2), :] = tile
                after = 16 if x == near else 8
                for y, at in ((-2, CORNER + corner), (64, CORNER + corner + after)):
                    for odd, tile in enumerate(both(side(which, at, 1))):
                        at_row = base(c, x) + y + odd
                        total_ref[at_row : at_row + 1, :] = tile

    for row in range(ROWS_BACK):
        spectrum = recv_ref[pl.ds(row, NZ, stride=ROWS_BACK), :]
        cells = apply_right(spectrum, table_ref[...], 0)
        if row < 18:
            for half in range(2):
                c, x = row // 6, 2 * (row % 6) + half - 2
                at = base(c, x)
                part = cells[half * 64 : half * 64 + 64, :]
                total_ref[at : at + 64, :] += part
                if 0 <= x < 8:
                    at = (c * 8 + x) * OWN_PITCH
                    field_ref[at : at + 64, :] = part
        else:
            for k in range(8):
                x = (row - 18) * 8 + k - 2
                if x < 10:
                    for c in range(3):
                        at, src = base(c, x), k * 16 + c * 4
                        total_ref[at - 2 : at, :] += cells[src : src + 2, :]
                        total_ref[at + 64 : at + 66, :] += cells[src + 2 : src + 4, :]

    def forces(magnet, read, first):
        force = []
        for c in range(3):
            d_x = jnp.where(first, *read(c, 1, 0)) - jnp.where(first, *read(c, -1, 0))
            d_y = jnp.where(first, *read(c, 0, 1)) - jnp.where(first, *read(c, 0, -1))
            a, b = read(c, 0, 0)
            d_z = jnp.where(first, pltpu.roll(a, 127, 1), pltpu.roll(b, 127, 1)) - jnp.where(
                first, pltpu.roll(a, 1, 1), pltpu.roll(b, 1, 1)
            )
            force.append(magnet[0] * d_x + magnet[1] * d_y + magnet[2] * d_z)
        return force

    def column(c, x, y):
        return total_ref[pl.ds(base(c, x) + y, 8, stride=PITCH), :]

    sign = jnp.where(left, -1.0, 1.0)
    values = [
        jnp.where(left, after_ref[k * 8 : k * 8 + 8, :], before_ref[k * 8 : k * 8 + 8, :])
        for k in range(12)
    ]
    force = forces(
        [PULL * value for value in langevin(*values[9:])],
        lambda c, dx, dy: (column(c, dx, 64 + dy), column(c, dx, dy - 1)),
        left,
    )
    vel, scaled, rest = macroscopic(values[5], values[6:9], force)
    for slot, (cx, cz, up, down) in enumerate(Y_FACE):
        even, odd = relax_terms((cx, sign, cz), vel, force, scaled, rest)
        post = (1.0 - OMEGA) * values[slot] + WEIGHTS[up] * (even + odd)
        post_ref[up, 0] = post
        post_ref[down, 33] = post

    row = lax.broadcasted_iota(jnp.int32, (8, 128), 0)
    upper = row == 7

    def edge_rows(k_low, k_high):
        pair = []
        for which, k in ((0, k_low), (1, k_high)):
            value = jnp.where(
                left[:1], side(which, CORNER + 16 + k, 1), side(which, CORNER + k, 1)
            )
            pair.append(jnp.broadcast_to(value, (8, 128)))
        return jnp.where(upper, pair[1], pair[0])

    def corner(c, dx, y):
        return jnp.where(upper, column(c, 1 + dx, y), column(c, dx - 1, y))

    force = forces(
        [PULL * value for value in langevin(*[edge_rows(k, k) for k in (9, 10, 11)])],
        lambda c, dx, dy: (corner(c, dx, 64 + dy), corner(c, dx, dy - 1)),
        left,
    )
    vel, scaled, rest = macroscopic(edge_rows(5, 5), [edge_rows(k, k) for k in (6, 7, 8)], force)
    even, odd = relax_terms((jnp.where(upper, -1.0, 1.0), sign, 0), vel, force, scaled, rest)
    edges = (1.0 - OMEGA) * edge_rows(1, 2) + WEIGHTS[7] * (even + odd)

    for which, x, step in ((0, -1, 1), (1, 8, -1)):

        def read(c, dx, dy):
            at = base(c, x + dx) + dy
            return (
                total_ref[pl.ds(at, 32, stride=2), :],
                total_ref[pl.ds(at + 1, 32, stride=2), :],
            )

        values = [side(which, k * 32, 32) for k in range(12)]
        force = forces([PULL * value for value in langevin(*values[9:])], read, left4)
        vel, scaled, rest = macroscopic(values[5], values[6:9], force)
        at_edge = 7 * which
        lane4 = lanes((32, 128))
        for slot, (cy, cz, up, down) in enumerate(X_FACE):
            even, odd = relax_terms((step, cy, cz), vel, force, scaled, rest)
            post = shift_z((1.0 - OMEGA) * values[slot] + WEIGHTS[up] * (even + odd), cz, lane4)
            if cy != 0:
                side_ref[8:40, :] = post
                if cy == 1:
                    side_ref[7:8, :] = edges[at_edge : at_edge + 1, :]
                    post = jnp.where(left4, post, side_ref[7:39, :])
                else:
                    side_ref[40:41, :] = edges[at_edge : at_edge + 1, :]
                    post = jnp.where(left4, side_ref[9:41, :], post)
                post = pltpu.roll(post, 64, 1)
            enter_ref[which, slot] = post

    def collide(pair, carry):
        ya = 2 * pair
        at = pl.multiple_of(pair * 8, 8)
        for c in range(3):
            src = c * 8 * OWN_PITCH + ya
            demag_ref[pl.ds(c * 256 + at, 8), :] = jnp.where(
                left,
                field_ref[pl.ds(src, 8, stride=OWN_PITCH), :],
                field_ref[pl.ds(src + 1, 8, stride=OWN_PITCH), :],
            )
        force = forces(
            [magnet_ref[pl.ds(c * 256 + at, 8), :] for c in range(3)],
            lambda c, dx, dy: (column(c, dx, ya + dy), column(c, dx, ya + 1 + dy)),
            left,
        )
        rest_popul = pop_ref[0, pl.ds(at, 8), :]
        sums, diffs, density = {}, {}, rest_popul
        for n in range(1, 19, 2):
            up, down = pop_ref[n, pl.ds(at, 8), :], pop_ref[n + 1, pl.ds(at, 8), :]
            sums[n], diffs[n] = up + down, up - down
            density = density + sums[n]
        momentum = []
        for k in range(3):
            signs = [(VELOCITIES[n][k], diffs[n]) for n in range(1, 19, 2)]
            total = None
            for sign_of, value in sorted(signs, key=lambda item: -item[0]):
                if sign_of == 1:
                    total = value if total is None else total + value
                elif sign_of == -1:
                    total = total - value
            momentum.append(total)
        vel, scaled, rest = macroscopic(density, momentum, force)
        post_ref[0, 1 + pair] = (1.0 - OMEGA) * rest_popul + WEIGHTS[0] * rest
        half = 0.5 * (1.0 - OMEGA)
        for first, last in ((1, 7), (7, 19)):
            weight = WEIGHTS[first]
            rest_w = weight * rest
            slope, curve = (3.0 * weight) * scaled, (4.5 * weight) * scaled
            pull = [(0.5 * weight) * value for value in force]
            push = [(1.5 * weight) * value for value in force]
            for n in range(first, last, 2):
                along_u = along(VELOCITIES[n], vel)
                even = rest_w + along_u * (curve * along_u + along(VELOCITIES[n], push))
                odd = slope * along_u + along(VELOCITIES[n], pull)
                even, odd = half * sums[n] + even, half * diffs[n] + odd
                for number, post in ((n, even + odd), (n + 1, even - odd)):
                    cz = 0 if number > 14 else VELOCITIES[number][2]
                    post_ref[number, 1 + pair] = shift_z(post, cz, lane)
        return carry

    lax.fori_loop(0, 32, collide, 0, unroll=8)
    sent = start((demag_ref, demag_hbm, out_sems.at[4]))

    def stream(pair, carry):
        at = pl.multiple_of(pair * 8, 8)
        for n in range(19):
            cx, cy, cz = VELOCITIES[n]
            tile = post_ref[n, 1 + pair]
            if cy == 1:
                tile = jnp.where(left, tile, post_ref[n, pair])
            elif cy == -1:
                tile = jnp.where(left, post_ref[n, 2 + pair], tile)
            if cy != 0 and cz == 0:
                tile = pltpu.roll(tile, 64, 1)
            elif cy != 0:
                edge = lane % 64 == (0 if cz == 1 else 63)
                near, far = (1, 65) if cz == 1 else (127, 63)
                tile = jnp.where(edge, pltpu.roll(tile, near, 1), pltpu.roll(tile, far, 1))
            if cx != 0:
                enters = enter_ref[0 if cx == 1 else 1, X_SLOT[n], pl.ds(pair, 1), :]
                tile = jnp.where(
                    row == (0 if cx == 1 else 7),
                    jnp.broadcast_to(enters, (8, 128)),
                    pltpu.roll(tile, 1 if cx == 1 else 7, 0),
                )
            out_ref[n, pl.ds(at, 8), :] = tile
        return carry

    for part in range(4):
        lax.fori_loop(8 * part, 8 * part + 8, stream, 0, unroll=8)
        rows = pl.ds(64 * part, 64)
        sent += start((out_ref.at[:, rows], out_hbm.at[:, rows], out_sems.at[part]))
    for copy in sent:
        copy.wait()


HBM = pl.BlockSpec(memory_space=pltpu.HBM)
ANY = pl.BlockSpec(memory_space=pl.ANY)
VMEM = pl.BlockSpec(memory_space=pltpu.VMEM)


def call(kernel, ins, outs, scratch, sems, flops, moved, vmem=60):
    return pl.pallas_call(
        kernel,
        out_shape=[jax.ShapeDtypeStruct(shape, F32) for shape, _ in outs],
        in_specs=ins,
        out_specs=[spec for _, spec in outs],
        scratch_shapes=[pltpu.VMEM(shape, F32) for shape in scratch]
        + [pltpu.SemaphoreType.DMA((count,)) for count in sems],
        compiler_params=pltpu.CompilerParams(vmem_limit_bytes=vmem * 1024 * 1024),
        cost_estimate=pl.CostEstimate(flops=flops, bytes_accessed=moved, transcendentals=0),
    )


def ring(values, axis, step):
    size = lax.axis_size(axis)
    return lax.ppermute(values, axis, [(i, (i + step) % size) for i in range(size)])


GROUPS = [[(2 * m + core) * GY + g for g in range(GY) for m in range(8)] for core in range(2)]


def exchange(rows, count):
    blocks = rows.reshape(64, 1, count * 128)
    blocks = lax.all_to_all(
        blocks, ("gx", "gy"), 0, 0, axis_index_groups=GROUPS, tiled=True
    )
    return blocks.reshape(64 * count, 128)


def as_tiles(values):
    return values.reshape(-1, 8, 32, 128).transpose(0, 2, 1, 3)


def from_rows(rows):
    return rows.reshape(-1, 32, 8, 128).transpose(0, 2, 1, 3).reshape(-1, 8, 4096)


def on_device(populations, h_axial, h_transverse):
    t = tables()
    pop_tiles = as_tiles(populations)
    pop_rows = pop_tiles.reshape(19 * 256, 128)
    ht_rows = as_tiles(h_transverse).reshape(512, 128)
    ha_rows = as_tiles(h_axial).reshape(256, 128)
    up, down = call(
        edge_kernel,
        [HBM] * 3,
        [((96, 128), VMEM), ((96, 128), VMEM)],
        [(2, 19, 8, 128)],
        [8],
        100_000,
        300_000,
    )(pop_tiles, ht_rows, ha_rows)
    before = ring(up, "gy", 1)
    after = ring(down, "gy", -1)
    (rows,) = call(
        first_kernel,
        [VMEM] * 3,
        [((64 * ROWS_FWD, 128), VMEM)],
        [(1536, 128)],
        [],
        30_000_000,
        1_800_000,
        8,
    )(ht_rows, ha_rows, t["fwd_z"])
    to_pair, to_next, magnet = call(
        face_kernel,
        [VMEM] * 5,
        [((FACE_ROWS, 128), VMEM), ((FACE_ROWS, 128), VMEM), ((768, 128), VMEM)],
        [],
        [],
        1_000_000,
        4_000_000,
        8,
    )(pop_rows, ht_rows, ha_rows, before, after)
    rows, to_pair, to_next = lax.optimization_barrier((rows, to_pair, to_next))
    own = exchange(rows, ROWS_FWD)
    (own,) = call(
        cells_kernel, [VMEM], [((64, 1536), VMEM)], [], [], 1_000, 40000000, 8
    )(own)
    other = lax.ppermute(own, "gx", [(i, i ^ 1) for i in range(GX)])
    pair = lax.ppermute(to_pair, "gx", [(i, i ^ 1) for i in range(GX)])
    beyond = lax.ppermute(to_next, "gx", [(i, ((i + 1) ^ 1) - 1 & 15) for i in range(GX)])
    (rows,) = call(
        plane_kernel,
        [VMEM] * 11,
        [((64 * ROWS_BACK, 128), VMEM)],
        [],
        [],
        1_000,
        1_000,
        16,
    )(
        own,
        other,
        t["fwd_x"],
        t["back_x"],
        t["even"],
        t["odd"],
        t["back_even"],
        t["back_odd"],
        t["wave_x"],
        t["wave_y"],
        t["wave_z"],
    )
    rows, pair, beyond = lax.optimization_barrier((rows, pair, beyond))
    recv = exchange(rows, ROWS_BACK)
    result, demag = call(
        cell_kernel,
        [VMEM] * 10,
        [((19, 256, 128), HBM), ((3 * 256, 128), HBM)],
        [
            (19, 256, 128),
            (768, 128),
            (24 * OWN_PITCH, 128),
            (36 * PITCH, 128),
            (19, 34, 8, 128),
            (48, 128),
            (2, 5, 32, 128),
        ],
        [5],
        60_000_000,
        8_000_000,
        24,
    )(
        recv,
        t["back_z"],
        ht_rows,
        ha_rows,
        magnet,
        pop_rows.reshape(19, 256, 128),
        pair,
        beyond,
        before,
        after,
    )
    return from_rows(result), from_rows(demag)


def solution(mesh):
    placed = (P(None, "gx", "gy"), P("gx", "gy"), P(None, "gx", "gy"))
    return jax.shard_map(
        on_device,
        mesh=mesh,
        in_specs=placed,
        out_specs=(P(None, "gx", "gy"), P(None, "gx", "gy")),
        check_vma=False,
    )
```

```python
import functools

import jax
import jax.numpy as jnp
import ml_dtypes
import numpy as np
from jax import lax
from jax.experimental import pallas as pl
from jax.experimental.pallas import tpu as pltpu
from jax.sharding import PartitionSpec as P

NX, NY, NZ = 128, 512, 64
GX, GY = 16, 8
VELOCITIES = (
    (0, 0, 0),
    (1, 0, 0),
    (-1, 0, 0),
    (0, 1, 0),
    (0, -1, 0),
    (0, 0, 1),
    (0, 0, -1),
    (1, 1, 0),
    (-1, -1, 0),
    (1, -1, 0),
    (-1, 1, 0),
    (1, 0, 1),
    (-1, 0, -1),
    (1, 0, -1),
    (-1, 0, 1),
    (0, 1, 1),
    (0, -1, -1),
    (0, 1, -1),
    (0, -1, 1),
)
WEIGHTS = (1.0 / 3.0,) + (1.0 / 18.0,) * 6 + (1.0 / 36.0,) * 12
OMEGA = 1.0 / 0.6
PULL = 0.05 / 2
F32 = jnp.float32

X_FACE = ((0, 0, 1, 2), (1, 0, 7, 10), (-1, 0, 9, 8), (0, 1, 11, 14), (0, -1, 13, 12))
Y_FACE = ((0, 0, 3, 4), (1, 0, 7, 9), (-1, 0, 10, 8), (0, 1, 15, 18), (0, -1, 17, 16))
X_SLOT = {n: s for s, row in enumerate(X_FACE) for n in row[2:]}

ROWS_FWD = 12
ROWS_BACK = 20
CORNER = 480
FACE_ROWS = CORNER + 32
PITCH = 69
OWN_PITCH = 65


def cas(rows, cols, count):
    angle = 2.0 * np.pi * ((rows[:, None] * cols[None, :]) % count) / count
    return np.cos(angle) + np.sin(angle)


def wave(index, count):
    return 2.0 * np.sin(np.pi * index / count)


@functools.lru_cache(maxsize=None)
def tables():
    every_x, every_z = np.arange(NX), np.arange(NZ)
    half = np.arange(NY // 2)
    out = {}
    fwd_z = np.zeros((NZ, 128))
    fwd_z[:, :NZ] = cas(every_z, every_z, NZ)
    out["fwd_z"] = fwd_z
    out["back_z"] = np.tile(cas(every_z, every_z, NZ), (1, 2))
    fwd_x, back_x = [], []
    m = np.arange(8)
    for parity in range(2):
        order = []
        for side in (parity, 1 - parity):
            for x2 in range(2):
                for x4 in range(4):
                    order += list(8 * (2 * m + side) + 2 * x4 + x2)
        fwd_x.append(cas(every_x, np.array(order), NX))
        order = []
        for x2 in range(2):
            for x6 in range(6):
                order += list((8 * (2 * m + parity) - 2 + 2 * x6 + x2) % NX)
        back_x.append(cas(np.array(order), every_x, NX))
    out["fwd_x"] = np.stack(fwd_x)
    out["back_x"] = np.stack(back_x)
    even, odd = 2 * half, 2 * half + 1
    halo = np.array(
        [
            (64 * g + (-2, -1, 64, 65)[k]) % NY
            for g in range(GY)
            for c in range(4)
            for k in range(4)
        ]
    )
    out["even"] = cas(half, even, NY)
    out["odd"] = cas(half, odd, NY)
    out["back_even"] = np.concatenate([cas(even, half, NY), cas(even, halo, NY)], axis=1)
    out["back_odd"] = np.concatenate([cas(odd, half, NY), cas(odd, halo, NY)], axis=1)
    out["wave_x"] = np.repeat(wave(every_x, NX)[:, None], 128, axis=1)
    out["wave_y"] = np.stack([wave(even, NY), wave(odd, NY)])
    out["wave_z"] = np.repeat(wave(every_z, NZ)[:, None], 128, axis=1)
    out = {name: np.asarray(value, np.float32) for name, value in out.items()}
    for name, axis in SPLIT_TABLES.items():
        high = out[name].astype(ml_dtypes.bfloat16)
        low = (out[name] - high.astype(np.float32)).astype(ml_dtypes.bfloat16)
        out[name] = np.concatenate([high, low, high], axis=axis)
    return out


SPLIT_TABLES = {
    "fwd_z": 1,
    "back_z": 0,
    "fwd_x": 2,
    "back_x": 2,
    "even": 0,
    "odd": 0,
    "back_even": 0,
    "back_odd": 0,
}


def terms(values, axis):
    high = values.astype(jnp.bfloat16)
    low = (values - high.astype(F32)).astype(jnp.bfloat16)
    return jnp.concatenate([high, high, low], axis=axis)


def product(a, b, dims):
    return lax.dot_general(a, b, (((dims[0],), (dims[1],)), ((), ())), preferred_element_type=F32)


def apply_left(table, values, axis=0):
    return product(table, terms(values, axis), (1, axis))


def apply_right(values, table, axis=1):
    return product(terms(values, axis), table, (axis, 0))


def langevin(hx, hy, hz):
    magnitude = jnp.sqrt(hx * hx + hy * hy + hz * hz)
    argument = 1.5 * magnitude
    decay = jnp.exp(-2.0 * argument)
    scale = ((1.0 + decay) / (1.0 - decay) - 1.0 / argument) / magnitude
    return hx * scale, hy * scale, hz * scale


def lanes(shape=(8, 128)):
    return lax.broadcasted_iota(jnp.int32, shape, len(shape) - 1)


def moments_of(popul):
    density = popul[0]
    for n in range(1, 19):
        density = density + popul[n]
    momentum = []
    for k in range(3):
        total = None
        for n in range(1, 19):
            if VELOCITIES[n][k] == 1:
                total = popul[n] if total is None else total + popul[n]
            elif VELOCITIES[n][k] == -1:
                total = total - popul[n]
        momentum.append(total)
    return density, momentum


def start(*copies):
    started = [pltpu.make_async_copy(*copy) for copy in copies]
    for copy in started:
        copy.start()
    return started


def edge_kernel(pop_hbm, ht_hbm, ha_hbm, up_ref, down_ref, pop_ref, sems):
    copies = start(
        (pop_hbm.at[:, 31], pop_ref.at[0], sems.at[0]),
        (pop_hbm.at[:, 0], pop_ref.at[1], sems.at[1]),
        (ht_hbm.at[pl.ds(31 * 8, 8)], up_ref.at[pl.ds(72, 8)], sems.at[2]),
        (ht_hbm.at[pl.ds(256 + 31 * 8, 8)], up_ref.at[pl.ds(80, 8)], sems.at[3]),
        (ha_hbm.at[pl.ds(31 * 8, 8)], up_ref.at[pl.ds(88, 8)], sems.at[4]),
        (ht_hbm.at[pl.ds(0, 8)], down_ref.at[pl.ds(72, 8)], sems.at[5]),
        (ht_hbm.at[pl.ds(256, 8)], down_ref.at[pl.ds(80, 8)], sems.at[6]),
        (ha_hbm.at[pl.ds(0, 8)], down_ref.at[pl.ds(88, 8)], sems.at[7]),
    )
    for copy in copies:
        copy.wait()
    for side, (out_ref, which) in enumerate(((up_ref, 2), (down_ref, 3))):
        popul = [pop_ref[side, n] for n in range(19)]
        density, momentum = moments_of(popul)
        for k, tile in enumerate([popul[face[which]] for face in Y_FACE] + [density] + momentum):
            out_ref[k * 8 : k * 8 + 8, :] = tile


def first_kernel(ht_ref, ha_ref, table_ref, send_ref, rows_ref):
    magnet = langevin(ht_ref[:256, :], ht_ref[256:, :], ha_ref[...])
    for c in range(3):
        for pair in range(32):
            tile = magnet[c][pair * 8 : pair * 8 + 8, :]
            rows_ref[pl.ds(c * 512 + 2 * pair, 8, stride=64), :] = tile
            rows_ref[pl.ds(c * 512 + 2 * pair + 1, 8, stride=64), :] = pltpu.roll(tile, 64, 1)
    spectrum = apply_left(table_ref[...], rows_ref[...], 1)
    for row in range(ROWS_FWD):
        send_ref[pl.ds(row, NZ, stride=ROWS_FWD), :] = spectrum[:, row * 128 : row * 128 + 128]


def face_kernel(
    pop_ref, ht_ref, ha_ref, before_ref, after_ref, pair_ref, next_ref, magnet_ref
):
    magnet = langevin(ht_ref[:256, :], ht_ref[256:, :], ha_ref[...])
    for c in range(3):
        magnet_ref[c * 256 : c * 256 + 256, :] = PULL * magnet[c]
    parity = lax.rem(lax.axis_index("gx"), 2)
    for out_ref, up in ((pair_ref, parity == 0), (next_ref, parity == 1)):
        face = jnp.where(up, 7, 0)
        second = jnp.where(up, 6, 1)

        def line(ref, at):
            return ref[pl.ds(at, 32, stride=8), :]

        popul = [line(pop_ref, n * 256 + face) for n in range(19)]
        density, momentum = moments_of(popul)
        lines = [jnp.where(up, popul[f[2]], popul[f[3]]) for f in X_FACE] + [density] + momentum
        for x in (face, second):
            lines += [line(ht_ref, x), line(ht_ref, 256 + x), line(ha_ref, x)]
        for k, value in enumerate(lines):
            out_ref[k * 32 : k * 32 + 32, :] = value
        out_ref[CORNER + 24 : CORNER + 32, :] = jnp.zeros((8, 128), F32)
        for ref, at in ((before_ref, CORNER), (after_ref, CORNER + 12)):
            out_ref[at : at + 12, :] = ref[pl.ds(face, 12, stride=8), :]
        for ref, at in ((before_ref, CORNER + 24), (after_ref, CORNER + 27)):
            out_ref[at : at + 3, :] = ref[pl.ds(72 + second, 3, stride=8), :]


def transpose_blocks(tiles):
    block = lanes() // 16
    for bit in (1, 2, 4):
        low = (block & bit) == 0
        out = list(tiles)
        for i in range(8):
            if i & bit == 0:
                a, b = tiles[i], tiles[i | bit]
                out[i] = jnp.where(low, a, pltpu.roll(b, 16 * bit, 1))
                out[i | bit] = jnp.where(low, pltpu.roll(a, 128 - 16 * bit, 1), b)
        tiles = out
    return tiles


def cells_kernel(recv_ref, cells_ref):
    left = lanes() < 64
    for c in range(3):
        for pair in range(4):
            for x4 in range(4):
                start = 16 * pair * ROWS_FWD + c * 4 + x4
                a = recv_ref[pl.ds(start, 8, stride=ROWS_FWD), :]
                b = recv_ref[pl.ds(start + 8 * ROWS_FWD, 8, stride=ROWS_FWD), :]
                at, col = x4 * 8, c * 512 + pair * 128
                cells_ref[at : at + 8, col : col + 128] = jnp.where(left, a, pltpu.roll(b, 64, 1))
                cells_ref[at + 32 : at + 40, col : col + 128] = jnp.where(
                    left, pltpu.roll(a, 64, 1), b
                )


def plane_kernel(
    own_ref,
    other_ref,
    fwd_x_ref,
    back_x_ref,
    even_ref,
    odd_ref,
    back_even_ref,
    back_odd_ref,
    wave_x_ref,
    wave_y_ref,
    wave_z_ref,
    send_ref,
):
    row = lax.axis_index("gx")
    parity = lax.rem(row, 2)
    index_z = lax.axis_index("gy") * 8 + row // 2
    left = lanes() < 64
    wave_x = wave_x_ref[:, 0:1]
    wave_z = wave_z_ref[pl.ds(index_z, 1), 0:1]
    cells = jnp.concatenate([own_ref[...], other_ref[...]], axis=0)
    spectrum = apply_left(fwd_x_ref[parity], cells)
    along = wave_x * spectrum[:, :512] + wave_z * spectrum[:, 1024:]
    both = jnp.concatenate([along, spectrum[:, 512:1024]], axis=0)
    parts = (
        apply_right(both[:, :256] + both[:, 256:], even_ref[...]),
        apply_right(both[:, :256] - both[:, 256:], odd_ref[...]),
    )
    back = []
    for which in range(2):
        wave_y = wave_y_ref[which : which + 1, :]
        squared = wave_x * wave_x + wave_y * wave_y + wave_z * wave_z
        anchor = squared == 0.0
        factor = jnp.where(
            anchor, 0.0, (-1.0 / (NX * NY * NZ)) / jnp.where(anchor, 1.0, squared)
        )
        potential = (parts[which][:128] + wave_y * parts[which][128:]) * factor
        stacked = jnp.concatenate([potential, wave_y * potential], axis=0)
        back.append(apply_right(stacked, (back_even_ref, back_odd_ref)[which][...]))
    low, high = back[0] + back[1], back[0] - back[1]
    column = lanes((128, 128)) % 16
    halo_p, halo_q = low[:128, 256:], low[128:, 256:]
    halo = jnp.where(
        column < 4,
        wave_x * halo_p,
        jnp.where(column < 8, halo_q, jnp.where(column < 12, wave_z * halo_p, 0.0)),
    )
    potential = jnp.concatenate([low[:128, :256], high[:128, :256]], axis=1)
    fields = jnp.concatenate(
        [wave_x * potential, low[128:, :256], high[128:, :256], wave_z * potential, halo], axis=1
    )
    cells = apply_left(back_x_ref[parity], fields)
    for x6 in range(6):
        for c in range(3):
            for pair in range(4):
                col = c * 512 + pair * 128
                a = cells[x6 * 8 : x6 * 8 + 8, col : col + 128]
                b = cells[48 + x6 * 8 : 56 + x6 * 8, col : col + 128]
                at = 16 * pair * ROWS_BACK + c * 6 + x6
                send_ref[pl.ds(at, 8, stride=ROWS_BACK), :] = jnp.where(left, a, pltpu.roll(b, 64, 1))
                send_ref[pl.ds(at + 8 * ROWS_BACK, 8, stride=ROWS_BACK), :] = jnp.where(
                    left, pltpu.roll(a, 64, 1), b
                )
    for part in range(2):
        tiles = []
        for x in range(part * 8, part * 8 + 8):
            if x < 12:
                at = (x % 2) * 48 + (x // 2) * 8
                tiles.append(cells[at : at + 8, 1536:])
            else:
                tiles.append(jnp.zeros((8, 128), F32))
        for g, tile in enumerate(transpose_blocks(tiles)):
            at = 8 * g * ROWS_BACK + 18 + part
            send_ref[pl.ds(at, 8, stride=ROWS_BACK), :] = tile


def macroscopic(density, momentum, force):
    inverse = 1.0 / density
    vel = [(momentum[k] + 0.5 * force[k]) * inverse for k in range(3)]
    u_square = vel[0] * vel[0] + vel[1] * vel[1] + vel[2] * vel[2]
    u_dot_f = vel[0] * force[0] + vel[1] * force[1] + vel[2] * force[2]
    scaled = OMEGA * density
    base = scaled * (1.0 - 1.5 * u_square) - 0.5 * u_dot_f
    return vel, scaled, base


def along(lattice, vector):
    total = None
    for sign, value in zip(lattice, vector):
        if isinstance(sign, int):
            if sign == 0:
                continue
            term = value if sign == 1 else -value
        else:
            term = sign * value
        total = term if total is None else total + term
    return total


def relax_terms(lattice, vel, force, scaled, base):
    along_u = along(lattice, vel)
    along_f = along(lattice, force)
    even = base + along_u * (4.5 * scaled * along_u + 1.5 * along_f)
    odd = 3.0 * scaled * along_u + 0.5 * along_f
    return even, odd


def shift_z(tile, step, lane):
    if step == 0:
        return tile
    if step == 1:
        return jnp.where(lane % 64 == 0, pltpu.roll(tile, 65, 1), pltpu.roll(tile, 1, 1))
    return jnp.where(lane % 64 == 63, pltpu.roll(tile, 63, 1), pltpu.roll(tile, 127, 1))


def cell_kernel(
    recv_ref,
    table_ref,
    ht_ref,
    ha_ref,
    magnet_ref,
    pop_ref,
    pair_ref,
    next_ref,
    before_ref,
    after_ref,
    out_hbm,
    demag_hbm,
    out_ref,
    demag_ref,
    field_ref,
    total_ref,
    post_ref,
    side_ref,
    enter_ref,
    out_sems,
):
    lane = lanes()
    left = lane < 64
    left4 = lanes((32, 128)) < 64
    parity = lax.rem(lax.axis_index("gx"), 2)
    side_of = ((next_ref, pair_ref), (pair_ref, next_ref))

    def side(which, at, count):
        even, odd = side_of[which]
        return jnp.where(parity == 0, even[at : at + count, :], odd[at : at + count, :])

    def base(c, x):
        return (c * 12 + 2 + x) * PITCH + 2

    def both(tile):
        turned = pltpu.roll(tile, 64, 1)
        first = lanes(tile.shape) < 64
        return jnp.where(first, tile, turned), jnp.where(first, turned, tile)

    own = ((ht_ref, 0), (ht_ref, 256), (ha_ref, 0))
    for c in range(3):
        ref, at = own[c]
        for pair in range(32):
            for odd, tile in enumerate(both(ref[at + pair * 8 : at + pair * 8 + 8, :])):
                total_ref[pl.ds(base(c, 0) + 2 * pair + odd, 8, stride=PITCH), :] = tile
        for edge_ref, y in ((before_ref, -2), (after_ref, 64)):
            for odd, tile in enumerate(both(edge_ref[72 + c * 8 : 80 + c * 8, :])):
                total_ref[pl.ds(base(c, 0) + y + odd, 8, stride=PITCH), :] = tile
        for which, near, far in ((0, -1, -2), (1, 8, 9)):
            for x, k, corner in ((near, 9 + c, 9 + c), (far, 12 + c, 24 + c)):
                for odd, tile in enumerate(both(side(which, k * 32, 32))):
                    total_ref[pl.ds(base(c, x) + odd, 32, stride=2), :] = tile
                after = 12 if x == near else 3
                for y, at in ((-2, CORNER + corner), (64, CORNER + corner + after)):
                    for odd, tile in enumerate(both(side(which, at, 1))):
                        at_row = base(c, x) + y + odd
                        total_ref[at_row : at_row + 1, :] = tile

    for row in range(ROWS_BACK):
        spectrum = recv_ref[pl.ds(row, NZ, stride=ROWS_BACK), :]
        cells = apply_right(spectrum, table_ref[...], 0)
        if row < 18:
            for half in range(2):
                c, x = row // 6, 2 * (row % 6) + half - 2
                at = base(c, x)
                part = cells[half * 64 : half * 64 + 64, :]
                total_ref[at : at + 64, :] += part
                if 0 <= x < 8:
                    at = (c * 8 + x) * OWN_PITCH
                    field_ref[at : at + 64, :] = part
        else:
            for k in range(8):
                x = (row - 18) * 8 + k - 2
                if x < 10:
                    for c in range(3):
                        at, src = base(c, x), k * 16 + c * 4
                        total_ref[at - 2 : at, :] += cells[src : src + 2, :]
                        total_ref[at + 64 : at + 66, :] += cells[src + 2 : src + 4, :]

    def forces(magnet, read, first):
        force = []
        for c in range(3):
            d_x = jnp.where(first, *read(c, 1, 0)) - jnp.where(first, *read(c, -1, 0))
            d_y = jnp.where(first, *read(c, 0, 1)) - jnp.where(first, *read(c, 0, -1))
            a, b = read(c, 0, 0)
            d_z = jnp.where(first, pltpu.roll(a, 127, 1), pltpu.roll(b, 127, 1)) - jnp.where(
                first, pltpu.roll(a, 1, 1), pltpu.roll(b, 1, 1)
            )
            force.append(magnet[0] * d_x + magnet[1] * d_y + magnet[2] * d_z)
        return force

    def column(c, x, y):
        return total_ref[pl.ds(base(c, x) + y, 8, stride=PITCH), :]

    sign = jnp.where(left, -1.0, 1.0)
    values = [
        jnp.where(left, after_ref[k * 8 : k * 8 + 8, :], before_ref[k * 8 : k * 8 + 8, :])
        for k in range(12)
    ]
    force = forces(
        [PULL * value for value in langevin(*values[9:])],
        lambda c, dx, dy: (column(c, dx, 64 + dy), column(c, dx, dy - 1)),
        left,
    )
    vel, scaled, rest = macroscopic(values[5], values[6:9], force)
    for slot, (cx, cz, up, down) in enumerate(Y_FACE):
        even, odd = relax_terms((cx, sign, cz), vel, force, scaled, rest)
        post = (1.0 - OMEGA) * values[slot] + WEIGHTS[up] * (even + odd)
        post_ref[up, 0] = post
        post_ref[down, 33] = post

    row = lax.broadcasted_iota(jnp.int32, (8, 128), 0)
    upper = row == 7

    def edge_rows(k_low, k_high):
        pair = []
        for which, k in ((0, k_low), (1, k_high)):
            value = jnp.where(
                left[:1], side(which, CORNER + 12 + k, 1), side(which, CORNER + k, 1)
            )
            pair.append(jnp.broadcast_to(value, (8, 128)))
        return jnp.where(upper, pair[1], pair[0])

    def corner(c, dx, y):
        return jnp.where(upper, column(c, 1 + dx, y), column(c, dx - 1, y))

    force = forces(
        [PULL * value for value in langevin(*[edge_rows(k, k) for k in (9, 10, 11)])],
        lambda c, dx, dy: (corner(c, dx, 64 + dy), corner(c, dx, dy - 1)),
        left,
    )
    vel, scaled, rest = macroscopic(edge_rows(5, 5), [edge_rows(k, k) for k in (6, 7, 8)], force)
    even, odd = relax_terms((jnp.where(upper, -1.0, 1.0), sign, 0), vel, force, scaled, rest)
    edges = (1.0 - OMEGA) * edge_rows(1, 2) + WEIGHTS[7] * (even + odd)

    for which, x, step in ((0, -1, 1), (1, 8, -1)):

        def read(c, dx, dy):
            at = base(c, x + dx) + dy
            return (
                total_ref[pl.ds(at, 32, stride=2), :],
                total_ref[pl.ds(at + 1, 32, stride=2), :],
            )

        values = [side(which, k * 32, 32) for k in range(12)]
        force = forces([PULL * value for value in langevin(*values[9:])], read, left4)
        vel, scaled, rest = macroscopic(values[5], values[6:9], force)
        at_edge = 7 * which
        lane4 = lanes((32, 128))
        for slot, (cy, cz, up, down) in enumerate(X_FACE):
            even, odd = relax_terms((step, cy, cz), vel, force, scaled, rest)
            post = shift_z((1.0 - OMEGA) * values[slot] + WEIGHTS[up] * (even + odd), cz, lane4)
            if cy != 0:
                side_ref[8:40, :] = post
                if cy == 1:
                    side_ref[7:8, :] = edges[at_edge : at_edge + 1, :]
                    post = jnp.where(left4, post, side_ref[7:39, :])
                else:
                    side_ref[40:41, :] = edges[at_edge : at_edge + 1, :]
                    post = jnp.where(left4, side_ref[9:41, :], post)
                post = pltpu.roll(post, 64, 1)
            enter_ref[which, slot] = post

    def collide(pair, carry):
        ya = 2 * pair
        at = pl.multiple_of(pair * 8, 8)
        for c in range(3):
            src = c * 8 * OWN_PITCH + ya
            demag_ref[pl.ds(c * 256 + at, 8), :] = jnp.where(
                left,
                field_ref[pl.ds(src, 8, stride=OWN_PITCH), :],
                field_ref[pl.ds(src + 1, 8, stride=OWN_PITCH), :],
            )
        force = forces(
            [magnet_ref[pl.ds(c * 256 + at, 8), :] for c in range(3)],
            lambda c, dx, dy: (column(c, dx, ya + dy), column(c, dx, ya + 1 + dy)),
            left,
        )
        rest_popul = pop_ref[0, pl.ds(at, 8), :]
        sums, diffs, density = {}, {}, rest_popul
        for n in range(1, 19, 2):
            up, down = pop_ref[n, pl.ds(at, 8), :], pop_ref[n + 1, pl.ds(at, 8), :]
            sums[n], diffs[n] = up + down, up - down
            density = density + sums[n]
        momentum = []
        for k in range(3):
            signs = [(VELOCITIES[n][k], diffs[n]) for n in range(1, 19, 2)]
            total = None
            for sign_of, value in sorted(signs, key=lambda item: -item[0]):
                if sign_of == 1:
                    total = value if total is None else total + value
                elif sign_of == -1:
                    total = total - value
            momentum.append(total)
        vel, scaled, rest = macroscopic(density, momentum, force)
        post_ref[0, 1 + pair] = (1.0 - OMEGA) * rest_popul + WEIGHTS[0] * rest
        half = 0.5 * (1.0 - OMEGA)
        for first, last in ((1, 7), (7, 19)):
            weight = WEIGHTS[first]
            rest_w = weight * rest
            slope, curve = (3.0 * weight) * scaled, (4.5 * weight) * scaled
            pull = [(0.5 * weight) * value for value in force]
            push = [(1.5 * weight) * value for value in force]
            for n in range(first, last, 2):
                along_u = along(VELOCITIES[n], vel)
                even = rest_w + along_u * (curve * along_u + along(VELOCITIES[n], push))
                odd = slope * along_u + along(VELOCITIES[n], pull)
                even, odd = half * sums[n] + even, half * diffs[n] + odd
                for number, post in ((n, even + odd), (n + 1, even - odd)):
                    cz = 0 if number > 14 else VELOCITIES[number][2]
                    post_ref[number, 1 + pair] = shift_z(post, cz, lane)
        return carry

    lax.fori_loop(0, 32, collide, 0, unroll=8)
    sent = start((demag_ref, demag_hbm, out_sems.at[4]))

    def stream(pair, carry):
        at = pl.multiple_of(pair * 8, 8)
        for n in range(19):
            cx, cy, cz = VELOCITIES[n]
            tile = post_ref[n, 1 + pair]
            if cy == 1:
                tile = jnp.where(left, tile, post_ref[n, pair])
            elif cy == -1:
                tile = jnp.where(left, post_ref[n, 2 + pair], tile)
            if cy != 0 and cz == 0:
                tile = pltpu.roll(tile, 64, 1)
            elif cy != 0:
                edge = lane % 64 == (0 if cz == 1 else 63)
                near, far = (1, 65) if cz == 1 else (127, 63)
                tile = jnp.where(edge, pltpu.roll(tile, near, 1), pltpu.roll(tile, far, 1))
            if cx != 0:
                enters = enter_ref[0 if cx == 1 else 1, X_SLOT[n], pl.ds(pair, 1), :]
                tile = jnp.where(
                    row == (0 if cx == 1 else 7),
                    jnp.broadcast_to(enters, (8, 128)),
                    pltpu.roll(tile, 1 if cx == 1 else 7, 0),
                )
            out_ref[n, pl.ds(at, 8), :] = tile
        return carry

    for part in range(4):
        lax.fori_loop(8 * part, 8 * part + 8, stream, 0, unroll=8)
        rows = pl.ds(64 * part, 64)
        sent += start((out_ref.at[:, rows], out_hbm.at[:, rows], out_sems.at[part]))
    for copy in sent:
        copy.wait()


HBM = pl.BlockSpec(memory_space=pltpu.HBM)
ANY = pl.BlockSpec(memory_space=pl.ANY)
VMEM = pl.BlockSpec(memory_space=pltpu.VMEM)


def call(kernel, ins, outs, scratch, sems, flops, moved, vmem=60):
    return pl.pallas_call(
        kernel,
        out_shape=[jax.ShapeDtypeStruct(shape, F32) for shape, _ in outs],
        in_specs=ins,
        out_specs=[spec for _, spec in outs],
        scratch_shapes=[pltpu.VMEM(shape, F32) for shape in scratch]
        + [pltpu.SemaphoreType.DMA((count,)) for count in sems],
        compiler_params=pltpu.CompilerParams(vmem_limit_bytes=vmem * 1024 * 1024),
        cost_estimate=pl.CostEstimate(flops=flops, bytes_accessed=moved, transcendentals=0),
    )


def ring(values, axis, step):
    size = lax.axis_size(axis)
    return lax.ppermute(values, axis, [(i, (i + step) % size) for i in range(size)])


GROUPS = [[(2 * m + core) * GY + g for g in range(GY) for m in range(8)] for core in range(2)]


def exchange(rows, count):
    blocks = rows.reshape(64, 1, count * 128)
    blocks = lax.all_to_all(
        blocks, ("gx", "gy"), 0, 0, axis_index_groups=GROUPS, tiled=True
    )
    return blocks.reshape(64 * count, 128)


def as_tiles(values):
    return values.reshape(-1, 8, 32, 128).transpose(0, 2, 1, 3)


def from_rows(rows):
    return rows.reshape(-1, 32, 8, 128).transpose(0, 2, 1, 3).reshape(-1, 8, 4096)


def on_device(populations, h_axial, h_transverse):
    t = tables()
    pop_tiles = as_tiles(populations)
    pop_rows = pop_tiles.reshape(19 * 256, 128)
    ht_rows = as_tiles(h_transverse).reshape(512, 128)
    ha_rows = as_tiles(h_axial).reshape(256, 128)
    up, down = call(
        edge_kernel,
        [HBM] * 3,
        [((96, 128), VMEM), ((96, 128), VMEM)],
        [(2, 19, 8, 128)],
        [8],
        100_000,
        300_000,
    )(pop_tiles, ht_rows, ha_rows)
    before = ring(up, "gy", 1)
    after = ring(down, "gy", -1)
    (rows,) = call(
        first_kernel,
        [VMEM] * 3,
        [((64 * ROWS_FWD, 128), VMEM)],
        [(1536, 128)],
        [],
        30_000_000,
        1_800_000,
        8,
    )(ht_rows, ha_rows, t["fwd_z"])
    to_pair, to_next, magnet = call(
        face_kernel,
        [VMEM] * 5,
        [((FACE_ROWS, 128), VMEM), ((FACE_ROWS, 128), VMEM), ((768, 128), VMEM)],
        [],
        [],
        1_000_000,
        4_000_000,
        8,
    )(pop_rows, ht_rows, ha_rows, before, after)
    rows, to_pair, to_next = lax.optimization_barrier((rows, to_pair, to_next))
    own = exchange(rows, ROWS_FWD)
    (own,) = call(
        cells_kernel, [VMEM], [((64, 1536), VMEM)], [], [], 1_000, 40000000, 8
    )(own)
    other = lax.ppermute(own, "gx", [(i, i ^ 1) for i in range(GX)])
    pair = lax.ppermute(to_pair, "gx", [(i, i ^ 1) for i in range(GX)])
    beyond = lax.ppermute(to_next, "gx", [(i, ((i + 1) ^ 1) - 1 & 15) for i in range(GX)])
    (rows,) = call(
        plane_kernel,
        [VMEM] * 11,
        [((64 * ROWS_BACK, 128), VMEM)],
        [],
        [],
        1_000,
        1_000,
        16,
    )(
        own,
        other,
        t["fwd_x"],
        t["back_x"],
        t["even"],
        t["odd"],
        t["back_even"],
        t["back_odd"],
        t["wave_x"],
        t["wave_y"],
        t["wave_z"],
    )
    rows, pair, beyond = lax.optimization_barrier((rows, pair, beyond))
    recv = exchange(rows, ROWS_BACK)
    result, demag = call(
        cell_kernel,
        [VMEM] * 10,
        [((19, 256, 128), HBM), ((3 * 256, 128), HBM)],
        [
            (19, 256, 128),
            (768, 128),
            (24 * OWN_PITCH, 128),
            (36 * PITCH, 128),
            (19, 34, 8, 128),
            (48, 128),
            (2, 5, 32, 128),
        ],
        [5],
        60_000_000,
        8_000_000,
        24,
    )(
        recv,
        t["back_z"],
        ht_rows,
        ha_rows,
        magnet,
        pop_rows.reshape(19, 256, 128),
        pair,
        beyond,
        before,
        after,
    )
    return from_rows(result), from_rows(demag)


def solution(mesh):
    placed = (P(None, "gx", "gy"), P("gx", "gy"), P(None, "gx", "gy"))
    return jax.shard_map(
        on_device,
        mesh=mesh,
        in_specs=placed,
        out_specs=(P(None, "gx", "gy"), P(None, "gx", "gy")),
        check_vma=False,
    )
```
